32 devices in a mesh: dp: 2 (over core), gx: 4 (over y, x), gy: 4 (over z).
Axes of the slice: x: 2, y: 2, z: 4, core: 2. Of those that a mesh axis runs over, the one named last changes fastest.
Arguments:
- hidden_in: bfloat16 [2, 2048, 1088], P(None, ('dp', 'gy'), 'gx'), may hold values from -6 to 6
- segment_ids: int32 [2, 2048], P(None, 'dp'), may hold values from 0 to 31, as said below
- cotangent: bfloat16 [2, 2048, 1088], P(None, ('dp', 'gy'), 'gx'), may hold values from -6 to 6
- norm1_gain: bfloat16 [1088], replicated, may hold values from 0.5 to 1.5
- norm1_shift: bfloat16 [1088], replicated, may hold values from -1.75 to 1.75
- w_qkv: bfloat16 [1088, 3264], P('gx', 'gy'), may hold values from -0.1875 to 0.1875
- q_bias: bfloat16 [1088], replicated, may hold values from -1.75 to 1.75
- v_bias: bfloat16 [1088], replicated, may hold values from -0.1875 to 0.1875
- w_out: bfloat16 [1088, 1088], P('gy', 'gx'), may hold values from -1.5 to 1.5
- out_bias: bfloat16 [1088], replicated, may hold values from -1.75 to 1.75
- norm2_gain: bfloat16 [1088], replicated, may hold values from 0.5 to 1.5
- norm2_shift: bfloat16 [1088], replicated, may hold values from -1.75 to 1.75
- w_up: bfloat16 [1088, 4352], P('gx', 'gy'), may hold values from -0.1875 to 0.1875
- up_bias: bfloat16 [4352], replicated, may hold values from -1.75 to 1.75
- w_down: bfloat16 [4352, 1088], P('gy', 'gx'), may hold values from -0.09375 to 0.09375
- down_bias: bfloat16 [1088], replicated, may hold values from -1.75 to 1.75
Outputs:
- hidden_out: bfloat16 [2, 2048, 1088], P(None, ('dp', 'gy'), 'gx')
- grad_in: bfloat16 [2, 2048, 1088], P(None, ('dp', 'gy'), 'gx')
- grad_norm1_gain: float32 [1088], replicated
- grad_norm1_shift: float32 [1088], replicated
- grad_w_qkv: float32 [1088, 3264], P('gx', 'gy')
- grad_q_bias: float32 [1088], replicated
- grad_v_bias: float32 [1088], replicated
- grad_w_out: float32 [1088, 1088], P('gy', 'gx')
- grad_out_bias: float32 [1088], replicated
- grad_norm2_gain: float32 [1088], replicated
- grad_norm2_shift: float32 [1088], replicated
- grad_w_up: float32 [1088, 4352], P('gx', 'gy')
- grad_up_bias: float32 [4352], replicated
- grad_w_down: float32 [4352, 1088], P('gy', 'gx')
- grad_down_bias: float32 [1088], replicated
The draws below stay inside these ranges and needn't reach their ends.
Inputs may be any that keep to these rules, and one draw needn't show every extreme that they name: `segment_ids`: documents never span two sequences of 1024 tokens; numbers rise along a sequence, its documents but the last are numbered upward from 8 times the sequence's place in the whole array, and its last document is numbered 8 times that place plus 7. Every document but the last of a sequence has 200 to 1000 tokens; the last is cut at the sequence's end, so a sequence holds 2 to 6 documents.
All inputs are finite; a program needn't handle non-finite values.
Results may differ from the reference program's by a relative error of at most 0.014.
Values may be sent and summed in bfloat16 or wider, within the bound.
No kernel may reach another device: no remote copies, remote signals or barrier semaphores. Data moves between devices by JAX's collectives and lax.ppermute only.
A program may use at most 128 MiB of HBM per device.

```python
import jax
import jax.numpy as jnp
from jax import lax

D = 1088
HEADS = 17
HEAD_DIM = 64
FF = 4352
SEQ = 1024
MB = 2
TOKENS = 2048


def draw_segment_ids(key, part):
    key = jax.random.fold_in(key, 3)
    row_count = MB * (TOKENS // SEQ)
    shortest = max(1, SEQ * 200 // 1024)
    longest = max(shortest + 1, SEQ * 1000 // 1024 + 1)
    lengths = jax.random.randint(key, (row_count, 6), shortest, longest).astype(jnp.int32)
    bounds = jnp.cumsum(lengths, axis=1).astype(jnp.int32)
    places = jnp.arange(SEQ, dtype=jnp.int32)
    local_ids = jnp.sum((places[None, :, None] >= bounds[:, None, :]).astype(jnp.int32), axis=2).astype(jnp.int32)
    last_ids = local_ids[:, -1:]
    renamed = jnp.where(local_ids == last_ids, jnp.int32(7), local_ids).astype(jnp.int32)
    numbers = 8 * jnp.arange(row_count, dtype=jnp.int32)[:, None] + renamed
    return numbers.reshape(MB, TOKENS)


def steps_of(key, shape, cuts, low, largest):
    loudness = 1.0
    for position, parts in cuts:
        heights = jax.random.uniform(jax.random.fold_in(jax.random.fold_in(key, 6), position), (parts,), jnp.float32, low / len(cuts), largest / len(cuts))
        loudness = loudness * jnp.repeat(jnp.exp(heights), shape[position] // parts).reshape((-1,) + (1,) * (len(shape) - 1 - position))
    return loudness


def centred(rng, shape, scale, limit, shards=(), kind=jnp.bfloat16):
    loudness = steps_of(rng, shape, shards, -0.22, 0.18) if shards else 1.0
    array = jax.random.normal(rng, shape, jnp.float32) * scale * loudness
    return jnp.minimum(jnp.maximum(array, -limit), limit).astype(kind)


def setup_inputs(seed: int = 0) -> dict:
    key_of = jax.random.split(jax.random.key(seed), 17)
    hidden_in = centred(key_of[0], (MB, TOKENS, D), 1.0, 6.0, ((1, 8), (2, 4)))
    segment_ids = draw_segment_ids(jax.random.fold_in(key_of[16], 71), 0)
    cotangent = centred(key_of[2], (MB, TOKENS, D), 1.0, 6.0, ((1, 8), (2, 4)))
    norm1_gain = jnp.clip(1.0 + 0.1 * jax.random.normal(key_of[3], (D,), jnp.float32), 0.5, 1.5).astype(jnp.bfloat16)
    norm1_shift = centred(key_of[4], (D,), 0.3, 1.75)
    w_qkv = centred(key_of[5], (D, 3 * D), D ** -0.5, 0.1875, ((0, 4), (1, 4)))
    q_bias = centred(key_of[6], (D,), 0.3, 1.75)
    v_bias = centred(key_of[7], (D,), 0.03, 0.1875)
    w_out = centred(key_of[8], (D, D), (max(1, D * 16 // SEQ)) ** -0.5, 1.5, ((0, 4), (1, 4)))
    out_bias = centred(key_of[9], (D,), 0.3, 1.75)
    norm2_gain = jnp.clip(1.0 + 0.1 * jax.random.normal(key_of[10], (D,), jnp.float32), 0.5, 1.5).astype(jnp.bfloat16)
    norm2_shift = centred(key_of[11], (D,), 0.3, 1.75)
    w_up = centred(key_of[12], (D, FF), D ** -0.5, 0.1875, ((0, 4), (1, 4)))
    up_bias = centred(key_of[13], (FF,), 0.3, 1.75)
    w_down = centred(key_of[14], (FF, D), FF ** -0.5, 0.09375, ((0, 4), (1, 4)))
    down_bias = centred(key_of[15], (D,), 0.3, 1.75)
    return {"hidden_in": hidden_in, "segment_ids": segment_ids, "cotangent": cotangent, "norm1_gain": norm1_gain, "norm1_shift": norm1_shift, "w_qkv": w_qkv, "q_bias": q_bias, "v_bias": v_bias, "w_out": w_out, "out_bias": out_bias, "norm2_gain": norm2_gain, "norm2_shift": norm2_shift, "w_up": w_up, "up_bias": up_bias, "w_down": w_down, "down_bias": down_bias}


@jax.custom_vjp
def low(v):
    return lax.optimization_barrier(v.astype(jnp.bfloat16)).astype(jnp.float32)

@jax.custom_vjp
def low_back(v):
    return v

def low_keep(v):
    return (low(v), None)

def low_pass(kept, grad):
    return (grad,)

def back_keep(v):
    return (v, None)

def back_low(kept, grad):
    return (low(grad),)
low.defvjp(low_keep, low_pass)
low_back.defvjp(back_keep, back_low)
epsilon = 1e-05
blocked_score = -1e+30

def matmul_high(left, right):
    return jnp.dot(left, right, precision=lax.Precision.HIGHEST, preferred_element_type=jnp.float32)

def layer_norm(values_in, gain, shift):
    average = lax.optimization_barrier(jnp.mean(values_in, axis=-1, keepdims=True))
    centered = values_in - average
    variance = lax.optimization_barrier(jnp.mean(centered * centered, axis=-1, keepdims=True))
    return centered * lax.rsqrt(variance + epsilon) * gain + shift

def attention(queries, key_rows, value_rows, segments):
    score_scale = HEAD_DIM ** (-0.5)
    block_rows = min(512, SEQ)
    query_heads = queries.reshape(SEQ, HEADS, HEAD_DIM)
    key_heads = key_rows.reshape(SEQ, HEADS, HEAD_DIM)
    value_heads = value_rows.reshape(SEQ, HEADS, HEAD_DIM)
    places = jnp.arange(SEQ, dtype=jnp.int32)

    @jax.checkpoint
    def one_block(block_start):
        query_block = lax.dynamic_slice_in_dim(query_heads, block_start, block_rows, 0)
        segment_block = lax.dynamic_slice_in_dim(segments, block_start, block_rows, 0)
        place_block = block_start + jnp.arange(block_rows, dtype=jnp.int32)
        scores = low_back(jnp.einsum('qhd,khd->hqk', query_block, key_heads, precision=lax.Precision.HIGHEST) * score_scale)
        allowed = (segment_block[:, None] == segments[None, :]) & (places[None, :] <= place_block[:, None])
        masked = jnp.where(allowed[None], scores, blocked_score)
        row_top = lax.optimization_barrier(jnp.max(masked, axis=-1, keepdims=True))
        weights = jnp.exp(masked - row_top)
        probabilities = weights / lax.optimization_barrier(jnp.sum(weights, axis=-1, keepdims=True))
        return jnp.einsum('hqk,khd->qhd', low(probabilities), value_heads, precision=lax.Precision.HIGHEST)
    block_starts = jnp.arange(SEQ // block_rows, dtype=jnp.int32) * block_rows
    return lax.map(one_block, block_starts).reshape(SEQ, HEADS * HEAD_DIM)

def block_forward(hidden, segments, params):
    norm1_gain, norm1_shift, w_qkv, q_bias, v_bias, w_out, out_bias, norm2_gain, norm2_shift, w_up, up_bias, w_down, down_bias = params
    normed = low(layer_norm(hidden, norm1_gain, norm1_shift))
    projected = matmul_high(normed, w_qkv)
    queries = low_back(low(projected[:, :D] + q_bias))
    key_rows = low_back(low(projected[:, D:2 * D]))
    value_rows = low_back(low(projected[:, 2 * D:] + v_bias))
    attended = low_back(low(attention(queries, key_rows, value_rows, segments)))
    branch = low_back(matmul_high(attended, w_out) + out_bias)
    middle = hidden + branch
    normed_two = low(layer_norm(middle, norm2_gain, norm2_shift))
    hidden_pre = low_back(matmul_high(normed_two, w_up) + up_bias)
    activated = low(jax.nn.gelu(hidden_pre, approximate=True))
    feed_out = low_back(matmul_high(activated, w_down) + down_bias)
    return middle + feed_out

def reference(hidden_in, segment_ids, cotangent, norm1_gain, norm1_shift, w_qkv, q_bias, v_bias, w_out, out_bias, norm2_gain, norm2_shift, w_up, up_bias, w_down, down_bias):
    params = tuple((member.astype(jnp.float32) for member in (norm1_gain, norm1_shift, w_qkv, q_bias, v_bias, w_out, out_bias, norm2_gain, norm2_shift, w_up, up_bias, w_down, down_bias)))
    sequence_count = MB * (TOKENS // SEQ)
    inputs = hidden_in.astype(jnp.float32).reshape(sequence_count, SEQ, D)
    segments_all = segment_ids.reshape(sequence_count, SEQ)
    grads_out = cotangent.astype(jnp.float32).reshape(sequence_count, SEQ, D)

    def one_sequence(totals, sequence_item):
        hidden, segments, grad_out = sequence_item
        result, pullback = jax.vjp(lambda block_in, block_weights: block_forward(block_in, segments, block_weights), hidden, params)
        grad_hidden, grad_params = pullback(grad_out)
        return (jax.tree.map(jnp.add, totals, grad_params), (result, grad_hidden))
    zero_totals = jax.tree.map(jnp.zeros_like, params)
    totals, (results, input_grads) = lax.scan(one_sequence, zero_totals, (inputs, segments_all, grads_out))
    block_out = results.reshape(MB, TOKENS, D).astype(jnp.bfloat16)
    grad_input = input_grads.reshape(MB, TOKENS, D).astype(jnp.bfloat16)
    return (block_out, grad_input, totals[0], totals[1], totals[2], totals[3], totals[4], totals[5], totals[6], totals[7], totals[8], totals[9], totals[10], totals[11], totals[12])
```

```python
import math

import jax
import jax.numpy as jnp
from jax import lax
from jax.sharding import Mesh
from jax.sharding import PartitionSpec as P

HEAD_DIM = 64
PAIR = 2 * HEAD_DIM
EPSILON = 1e-05
BLOCKED = -1e30
BF = jnp.bfloat16
F32 = jnp.float32
PLANE = ("c", "gx")
ROOT = math.sqrt(2.0 / math.pi)


def dot(left, right, dims):
    return lax.dot_general(left, right, (dims, ((), ())), preferred_element_type=F32)


def swap_core(value):
    return lax.ppermute(value, "c", [(0, 1), (1, 0)])


def from_peer(value, step):
    return lax.ppermute(value, "gx", [(i, i ^ step) for i in range(4)])


def reordered(blocks, mask):
    return jnp.stack(
        [lax.dynamic_index_in_dim(blocks, i ^ mask, 0, False) for i in range(blocks.shape[0])]
    )


def exchange_gx(blocks, g):
    sent = [lax.dynamic_index_in_dim(blocks, g ^ k, 0, False) for k in range(4)]
    got = jnp.stack([sent[0]] + [from_peer(sent[k], k) for k in range(1, 4)])
    return reordered(got, g)


def gather_plane(own):
    near = jnp.stack([own] + [from_peer(own, k) for k in range(1, 4)])
    return jnp.concatenate([near, swap_core(near)], 0)


def scatter_plane(partial):
    other = swap_core(partial[4:].astype(BF))
    summed = partial[:4].astype(F32) + other.astype(F32)
    total = summed[0]
    for k in range(1, 4):
        total = total + from_peer(summed[k].astype(BF), k).astype(F32)
    return total


def plane_of(core, z, second):
    half = z % 2 if not second else 1 - z % 2
    return (z // 2) * 4 + 2 * half + core


FORWARD = [[(c * 4 + z, plane_of(c, z, second)) for c in range(2) for z in range(4)] for second in (False, True)]
BACKWARD = [[(b, a) for a, b in perm] for perm in FORWARD]


def to_plane(local, z):
    first = lax.ppermute(lax.dynamic_index_in_dim(local, z % 2, 0, False), ("c", "gy"), FORWARD[0])
    second = lax.ppermute(lax.dynamic_index_in_dim(local, 1 - z % 2, 0, False), ("c", "gy"), FORWARD[1])
    low = z // 2 == 0
    return jnp.concatenate([jnp.where(low, first, second), jnp.where(low, second, first)], 0)


def from_plane(half, z):
    rows = half.shape[0] // 2
    parts = half.reshape(2, rows, half.shape[1])
    first = lax.ppermute(lax.dynamic_index_in_dim(parts, z // 2, 0, False), ("c", "gy"), BACKWARD[0])
    second = lax.ppermute(lax.dynamic_index_in_dim(parts, 1 - z // 2, 0, False), ("c", "gy"), BACKWARD[1])
    even = z % 2 == 0
    return jnp.stack([jnp.where(even, first, second), jnp.where(even, second, first)])


def whole_width(half, g):
    near = jnp.stack([half] + [from_peer(half, k) for k in range(1, 4)])
    ordered = reordered(near, g)
    return jnp.concatenate([ordered[i] for i in range(4)], 1)


def norm_parts(rows):
    average = jnp.mean(rows, axis=1, keepdims=True)
    centered = rows - average
    inverse = lax.rsqrt(jnp.mean(centered * centered, axis=1, keepdims=True) + EPSILON)
    return centered * inverse, inverse


def norm_pull(upstream, centered, inverse, gain):
    scaled = upstream * gain
    return inverse * (
        scaled
        - jnp.mean(scaled, axis=1, keepdims=True)
        - centered * jnp.mean(scaled * centered, axis=1, keepdims=True)
    )


def head_forward(query, key, value, allowed):
    scores = dot(query, key, ((1,), (1,))) * HEAD_DIM**-0.5
    masked = jnp.where(allowed, scores, BLOCKED)
    top = jnp.max(masked, axis=1, keepdims=True)
    weights = jnp.exp(masked - top)
    probs = weights / jnp.sum(weights, axis=1, keepdims=True)
    return probs, dot(probs.astype(BF), value, ((1,), (0,))).astype(BF)


def head_backward(query, key, value, probs, grad_out):
    grad_probs = dot(grad_out, value, ((1,), (1,)))
    inner = jnp.sum(probs * grad_probs, axis=1, keepdims=True)
    grad_scores = (probs * (grad_probs - inner)).astype(BF)
    grad_query = dot(grad_scores, key, ((1,), (0,))) * HEAD_DIM**-0.5
    grad_key = dot(grad_scores, query, ((0,), (0,))) * HEAD_DIM**-0.5
    grad_value = dot(probs.astype(BF), grad_out, ((0,), (0,)))
    return grad_query, grad_key, grad_value


def shards(
    hidden_in,
    segment_ids,
    cotangent,
    norm1_gain,
    norm1_shift,
    w_qkv,
    q_bias,
    v_bias,
    w_out,
    out_bias,
    norm2_gain,
    norm2_shift,
    w_up,
    up_bias,
    w_down,
    down_bias,
):
    c = lax.axis_index("c")
    g = lax.axis_index("gx")
    z = lax.axis_index("gy")
    d = c * 4 + g
    width = norm1_gain.shape[0]
    hidden = up_bias.shape[0]
    block = w_qkv.shape[0] // 2
    part = hidden // 32
    qkv_cols = w_qkv.shape[1]
    seq = segment_ids.shape[1]
    rows = seq // 8
    shared_at = 8 * PAIR
    gain1, shift1 = norm1_gain.astype(F32), norm1_shift.astype(F32)
    gain2, shift2 = norm2_gain.astype(F32), norm2_shift.astype(F32)

    x_half = whole_width(to_plane(hidden_in, z), g)
    x_own = lax.dynamic_slice_in_dim(x_half, g * rows, rows, 0).astype(F32)
    normed1_half = (norm_parts(x_half.astype(F32))[0] * gain1 + shift1).astype(BF)
    normed1_other = swap_core(normed1_half)
    low = c == 0
    normed1 = jnp.concatenate(
        [jnp.where(low, normed1_half, normed1_other), jnp.where(low, normed1_other, normed1_half)], 0
    )
    g_half = whole_width(to_plane(cotangent, z), g)
    g_half = reordered(g_half.reshape(4, rows, width), g)
    g_own = g_half[0].astype(F32)
    g_rel = jnp.concatenate([g_half, swap_core(g_half)], 0).reshape(seq, width)

    swapped_ids = swap_core(segment_ids)
    ids = jnp.where(z % 2 == c, segment_ids, swapped_ids)
    segments = lax.dynamic_index_in_dim(ids, z // 2, 0, False)

    qkv_half = lax.dynamic_slice_in_dim(w_qkv, c * block, block, 0)
    qkv_all = lax.all_gather(qkv_half, "gy", axis=1, tiled=True)
    pieces = []
    for t in range(3):
        third = qkv_all[:, t * width : (t + 1) * width]
        pieces.append(third[:, :shared_at].reshape(block, 8, PAIR).transpose(1, 0, 2))
    for t in range(3):
        shared = qkv_all[:, t * width + shared_at : (t + 1) * width]
        pieces.append(jnp.broadcast_to(shared[None], (8, block, HEAD_DIM)))
    qkv_own = lax.all_to_all(jnp.concatenate(pieces, 2), PLANE, split_axis=0, concat_axis=0, tiled=True)
    own_cols = qkv_own.shape[2]
    qkv_own = qkv_own.reshape(2, 4, block, own_cols).transpose(1, 0, 2, 3).reshape(width, own_cols)

    out_half = lax.dynamic_slice_in_dim(w_out, c * block, block, 1)
    out_all = lax.all_gather(out_half, "gy", axis=0, tiled=True)
    out_pieces = jnp.concatenate(
        [
            out_all[:shared_at].reshape(8, PAIR, block),
            jnp.broadcast_to(out_all[None, shared_at:], (8, HEAD_DIM, block)),
        ],
        1,
    )
    out_own = lax.all_to_all(out_pieces, PLANE, split_axis=0, concat_axis=0, tiled=True)
    out_own = out_own.reshape(2, 4, PAIR + HEAD_DIM, block).transpose(2, 1, 0, 3).reshape(-1, width)

    up_half = lax.dynamic_slice_in_dim(w_up, c * 4 * part, 4 * part, 1)
    up_half = up_half.reshape(2 * block, 4, part).transpose(1, 2, 0)
    down_half = lax.dynamic_slice_in_dim(w_down, c * 4 * part, 4 * part, 0).reshape(4, part, 2 * block)
    mlp = exchange_gx(jnp.concatenate([up_half, down_half], 1), g)
    mlp = lax.all_gather(mlp, "gy", axis=0, tiled=False)
    mlp = mlp.reshape(4, 4, 2, part, 2 * block).transpose(2, 0, 3, 1, 4).reshape(2, 4 * part, width)
    up_own, down_own = mlp[0], mlp[1]
    up_bias_own = lax.dynamic_index_in_dim(up_bias.reshape(4, 8, part), d, 1, False).reshape(1, -1).astype(F32)

    bias_pair = jnp.concatenate(
        [
            lax.dynamic_slice_in_dim(q_bias, d * PAIR, PAIR, 0),
            jnp.zeros((PAIR,), BF),
            lax.dynamic_slice_in_dim(v_bias, d * PAIR, PAIR, 0),
            q_bias[shared_at:],
            jnp.zeros((HEAD_DIM,), BF),
            v_bias[shared_at:],
        ]
    ).astype(F32)
    projected = (dot(normed1, qkv_own, ((1,), (0,))) + bias_pair).astype(BF)
    places = jnp.arange(seq, dtype=jnp.int32)
    allowed = (segments[:, None] == segments[None, :]) & (places[None, :] <= places[:, None])
    first_row = d * rows
    allowed_own = lax.dynamic_slice_in_dim(allowed, first_row, rows, 0)
    heads = []
    for h in range(2):
        heads.append([projected[:, t * PAIR + h * HEAD_DIM :][:, :HEAD_DIM] for t in range(3)])
    shared = [projected[:, 3 * PAIR + t * HEAD_DIM :][:, :HEAD_DIM] for t in range(3)]
    shared[0] = lax.dynamic_slice_in_dim(shared[0], first_row, rows, 0)
    kept = [head_forward(*heads[h], allowed) for h in range(2)]
    kept_shared = head_forward(*shared, allowed_own)
    attended = jnp.concatenate([kept[0][1], kept[1][1]], 1)
    attended_rel = reordered(attended.reshape(8, rows, PAIR), d).reshape(seq, PAIR)
    branch = dot(attended_rel, out_own[:PAIR], ((1,), (0,))).reshape(8, rows, width)
    branch_shared = dot(kept_shared[1], out_own[PAIR:], ((1,), (0,)))
    middle = x_own + scatter_plane(branch) + branch_shared + out_bias.astype(F32)

    centered2, inverse2 = norm_parts(middle)
    normed2_own = (centered2 * gain2 + shift2).astype(BF)
    normed2 = gather_plane(normed2_own).reshape(seq, width)
    pre = dot(normed2, up_own, ((1,), (1,))) + up_bias_own
    inner = jnp.tanh(ROOT * (pre + 0.044715 * pre * pre * pre))
    activated = (0.5 * pre * (1.0 + inner)).astype(BF)
    slope = 0.5 * (1.0 + inner) + 0.5 * pre * (1.0 - inner * inner) * ROOT * (1.0 + 3.0 * 0.044715 * pre * pre)
    grad_pre = (dot(g_rel, down_own, ((1,), (1,))) * slope).astype(BF)
    grad_normed2 = scatter_plane(dot(grad_pre, up_own, ((1,), (0,))).reshape(8, rows, width))
    feed = dot(activated, down_own, ((1,), (0,))).reshape(8, rows, width)
    result = middle + scatter_plane(feed) + down_bias.astype(F32)
    grad_down = dot(activated, g_rel, ((0,), (0,)))
    grad_up = dot(grad_pre, normed2, ((0,), (0,)))
    grad_up_bias = jnp.sum(grad_pre.astype(F32), axis=0)

    grad_middle = g_own + norm_pull(grad_normed2, centered2, inverse2, gain2)
    grad_branch_own = grad_middle.astype(BF)
    grad_branch = gather_plane(grad_branch_own).reshape(seq, width)

    grad_attended_rel = dot(grad_branch, out_own[:PAIR], ((1,), (1,))).astype(BF)
    grad_attended = reordered(grad_attended_rel.reshape(8, rows, PAIR), d).reshape(seq, PAIR)
    grad_shared = dot(grad_branch_own, out_own[PAIR:], ((1,), (1,))).astype(BF)
    grad_out = jnp.concatenate(
        [dot(attended_rel, grad_branch, ((0,), (0,))), dot(kept_shared[1], grad_branch_own, ((0,), (0,)))], 0
    )
    backs = [
        head_backward(*heads[h], kept[h][0], grad_attended[:, h * HEAD_DIM : (h + 1) * HEAD_DIM]) for h in range(2)
    ]
    back_shared = head_backward(*shared, kept_shared[0], grad_shared)
    grad_pairs = jnp.concatenate([backs[h][t] for t in range(3) for h in range(2)], 1).astype(BF)
    grad_query_shared = back_shared[0].astype(BF)
    grad_kv_shared = jnp.concatenate([back_shared[1], back_shared[2]], 1).astype(BF)
    grad_pairs_kv = jnp.concatenate([grad_pairs, grad_kv_shared], 1)
    pairs_rel = reordered(grad_pairs_kv.reshape(8, rows, -1), d).reshape(seq, -1)
    cols_kv = jnp.concatenate([qkv_own[:, : 3 * PAIR], qkv_own[:, 3 * PAIR + HEAD_DIM :]], 1)
    grad_first = dot(pairs_rel, cols_kv, ((1,), (1,))).reshape(8, rows, width)
    grad_first_own = dot(grad_query_shared, qkv_own[:, 3 * PAIR :][:, :HEAD_DIM], ((1,), (1,)))
    grad_normed1 = scatter_plane(grad_first) + grad_first_own
    centered1, inverse1 = norm_parts(x_own)
    grad_in = grad_middle + norm_pull(grad_normed1, centered1, inverse1, gain1)
    normed1_own = lax.dynamic_slice_in_dim(normed1, first_row, rows, 0)
    grad_qkv_kv = dot(normed1, grad_pairs_kv, ((0,), (0,)))
    grad_qkv_q = dot(normed1_own, grad_query_shared, ((0,), (0,)))
    grad_qkv = jnp.concatenate([grad_qkv_kv[:, : 3 * PAIR], grad_qkv_q, grad_qkv_kv[:, 3 * PAIR :]], 1)

    outer = lax.axis_size("do") > 1

    def over_outer(value):
        return lax.psum(value, "do") if outer else value

    sent = jnp.concatenate([grad_up.reshape(4, part, width), grad_down.reshape(4, part, width)], 1).astype(BF)
    summed = over_outer(lax.psum_scatter(sent, "gy", scatter_dimension=0, tiled=False))
    lanes = summed.reshape(2 * part, 4, 2 * block).transpose(1, 0, 2)
    mine = exchange_gx(lanes, g)
    theirs = swap_core(mine)
    both = jnp.where(low, jnp.stack([mine, theirs]), jnp.stack([theirs, mine])).reshape(8, 2, part, 2 * block)
    total_up = both[:, 0].reshape(8 * part, 2 * block).T.astype(F32)
    total_down = both[:, 1].reshape(8 * part, 2 * block).astype(F32)

    sent = grad_out.astype(BF).reshape(-1, 4, 2, block).transpose(2, 1, 0, 3).reshape(8, -1, block)
    got = lax.all_to_all(sent, PLANE, split_axis=0, concat_axis=0, tiled=True)
    shared_rows = jnp.sum(got[:, PAIR:].astype(F32), axis=0).astype(BF)
    placed = jnp.concatenate([got[:, :PAIR].reshape(shared_at, block), shared_rows], 0)
    mine = over_outer(lax.psum_scatter(placed, "gy", scatter_dimension=0, tiled=True))
    theirs = swap_core(mine)
    total_out = jnp.concatenate([jnp.where(low, mine, theirs), jnp.where(low, theirs, mine)], 1).astype(F32)

    sent = grad_qkv.astype(BF).reshape(4, 2, block, own_cols).transpose(1, 0, 2, 3).reshape(8, block, own_cols)
    got = lax.all_to_all(sent, PLANE, split_axis=0, concat_axis=0, tiled=True)
    shared_cols = jnp.sum(got[:, :, 3 * PAIR :].astype(F32), axis=0).astype(BF)
    wide = []
    for t in range(3):
        wide.append(got[:, :, t * PAIR : (t + 1) * PAIR].transpose(1, 0, 2).reshape(block, shared_at))
        wide.append(shared_cols[:, t * HEAD_DIM : (t + 1) * HEAD_DIM])
    placed = jnp.concatenate(wide, 1).reshape(block, 4, qkv_cols).transpose(1, 0, 2)
    mine = over_outer(lax.psum_scatter(placed, "gy", scatter_dimension=0, tiled=False))
    theirs = swap_core(mine)
    total_qkv = jnp.concatenate([jnp.where(low, mine, theirs), jnp.where(low, theirs, mine)], 0).astype(F32)

    def spread(pair_sums, shared_sums):
        return lax.dynamic_update_slice_in_dim(
            jnp.concatenate([jnp.zeros((shared_at,), F32), shared_sums]), pair_sums, d * PAIR, 0
        )

    sums = jnp.sum(grad_pairs_kv.astype(F32), axis=0)
    up_sums = lax.dynamic_update_slice_in_dim(
        jnp.zeros((4, 8, part), F32), grad_up_bias.reshape(4, 1, part), d, 1
    ).reshape(hidden)
    smalls = lax.psum(
        (
            jnp.sum(grad_normed1 * centered1, axis=0),
            jnp.sum(grad_normed1, axis=0),
            spread(sums[:PAIR], jnp.sum(grad_query_shared.astype(F32), axis=0)),
            spread(sums[2 * PAIR : 3 * PAIR], sums[3 * PAIR + HEAD_DIM :]),
            jnp.sum(grad_branch_own.astype(F32), axis=0),
            jnp.sum(grad_normed2 * centered2, axis=0),
            jnp.sum(grad_normed2, axis=0),
            up_sums,
            jnp.sum(g_own, axis=0),
        ),
        ("do", "c", "gx", "gy"),
    )

    def to_output(own):
        blocks = own.astype(BF).reshape(rows, 4, 2 * block).transpose(1, 0, 2)
        return from_plane(exchange_gx(blocks, g).reshape(4 * rows, 2 * block), z)

    return (
        to_output(result),
        to_output(grad_in),
        smalls[0],
        smalls[1],
        total_qkv,
        smalls[2],
        smalls[3],
        total_out,
        smalls[4],
        smalls[5],
        smalls[6],
        total_up,
        smalls[7],
        total_down,
        smalls[8],
    )


def solution(mesh):
    devices = mesh.devices
    split = Mesh(
        devices.reshape(devices.shape[0] // 2, 2, devices.shape[1], devices.shape[2]), ("do", "c", "gx", "gy")
    )
    stream = P(None, ("do", "c", "gy"), "gx")
    flat = P()
    tall = P("gx", "gy")
    wide = P("gy", "gx")
    return jax.shard_map(
        shards,
        mesh=split,
        in_specs=(
            stream,
            P(None, ("do", "c")),
            stream,
            flat,
            flat,
            tall,
            flat,
            flat,
            wide,
            flat,
            flat,
            flat,
            tall,
            flat,
            wide,
            flat,
        ),
        out_specs=(
            stream,
            stream,
            flat,
            flat,
            tall,
            flat,
            flat,
            wide,
            flat,
            flat,
            flat,
            tall,
            flat,
            wide,
            flat,
        ),
        check_vma=False,
    )
```

```python
import math

import jax
import jax.numpy as jnp
import numpy as np
from jax import lax
from jax.experimental import pallas as pl
from jax.experimental.pallas import tpu as pltpu
from jax.sharding import Mesh
from jax.sharding import PartitionSpec as P

HEAD_DIM = 64
PAIR = 2 * HEAD_DIM
EPSILON = 1e-05
BLOCKED = -1e30
BF = jnp.bfloat16
F32 = jnp.float32
PLANE = ("c", "gx")
EVERY = ("c", "gx", "gy")
ROOT = math.sqrt(2.0 / math.pi)
WINDOW = 128
TALL = WINDOW + 16
MIB = 1024 * 1024


def dot(left, right, dims):
    return lax.dot_general(left, right, (dims, ((), ())), preferred_element_type=F32)


def kernel(body, outs, scratch, ids, *arrays, us=1.0, limit=40):
    in_specs = [pl.BlockSpec(memory_space=pltpu.SMEM)] + [pl.BlockSpec(memory_space=pltpu.VMEM)] * len(arrays)
    result = pl.pallas_call(
        body,
        out_shape=tuple(jax.ShapeDtypeStruct(shape, kind) for shape, kind in outs),
        in_specs=in_specs,
        out_specs=tuple(pl.BlockSpec(memory_space=pltpu.VMEM) for _ in outs),
        scratch_shapes=[pltpu.VMEM(shape, kind) for shape, kind in scratch],
        compiler_params=pltpu.CompilerParams(vmem_limit_bytes=limit * MIB),
        cost_estimate=pl.CostEstimate(flops=int(us * 6e8), bytes_accessed=int(us * 1e5), transcendentals=0),
    )(ids, *arrays)
    return result if len(outs) > 1 else result[0]


def swap_core(value):
    return lax.ppermute(value, "c", [(0, 1), (1, 0)])


def from_peer(value, step):
    return lax.ppermute(value, "gx", [(i, i ^ step) for i in range(4)])


def from_below(value, step):
    return lax.ppermute(value, "gy", [(i, (i + step) % 4) for i in range(4)])


def gather_plane(own):
    near = [own] + [from_peer(own, k) for k in range(1, 4)]
    return near + [swap_core(piece) for piece in near]


def position(c, g, z):
    return (c * 4 + g) * 4 + z


def token_moves():
    moves = []
    for m in range(4):
        move = []
        for c in range(2):
            for g in range(4):
                for z in range(4):
                    t, mb = (m ^ g) >> 1, (m ^ g) & 1
                    move.append((position(c, g, z), position(z // 2, 2 * (z % 2) + t, 2 * mb + c)))
        moves.append(move)
    return moves


MOVES = token_moves()
BACK = [[(b, a) for a, b in move] for move in MOVES]


def run_table(width, cols):
    table = np.zeros((8, 4, 3), np.int32)
    for d in range(8):
        filled = 0
        for z in range(4):
            for t in range(3):
                low = max(width * t + PAIR * d, cols * z)
                high = min(width * t + PAIR * (d + 1), cols * (z + 1))
                if high > low:
                    table[d, z] = (low - cols * z, high - low, filled)
                    filled += high - low
            if table[d, z, 1] == 0:
                table[d, z, 2] = filled
    return table.reshape(-1)


def aligned(value, step):
    return pl.multiple_of(value, step)


def normed(rows):
    average = jnp.mean(rows, axis=1, keepdims=True)
    centered = rows - average
    inverse = lax.rsqrt(jnp.mean(centered * centered, axis=1, keepdims=True) + EPSILON)
    return centered * inverse, inverse


def norm_pull(upstream, centered, inverse, gain):
    scaled = upstream * gain
    return inverse * (
        scaled
        - jnp.mean(scaled, axis=1, keepdims=True)
        - centered * jnp.mean(scaled * centered, axis=1, keepdims=True)
    )


def column_sum(rows):
    return jnp.sum(rows, axis=0, keepdims=True)


def place(ids):
    return ids[0], ids[1], ids[2], ids[3]


def run_of(ids, d, z):
    at = 4 + d * 12 + z * 3
    return ids[at], ids[at + 1], ids[at + 2]


def send_tokens(ids, src, *outs):
    g = ids[1]
    for m in range(4):
        v = m ^ g
        outs[m][...] = src[v & 1, v >> 1].T


def own_rows(ids, blocks, held):
    e = 2 * (ids[1] & 1) + (ids[2] >> 1)
    for m in range(4):
        held[m ^ e] = blocks[m][...]
    return held[...].astype(F32).reshape(-1, held.shape[2]).T


def take_tokens(ids, b0, b1, b2, b3, out, held):
    out[...] = own_rows(ids, (b0, b1, b2, b3), held).astype(BF)


def take_normed(ids, b0, b1, b2, b3, gain, shift, out, low, held):
    rows = own_rows(ids, (b0, b1, b2, b3), held)
    out[...] = rows.astype(BF)
    low[...] = (normed(rows)[0] * gain[...].astype(F32) + shift[...].astype(F32)).astype(BF)


def split_features(ids, rows, held, outs):
    e = 2 * (ids[1] & 1) + (ids[2] >> 1)
    held[...] = rows.T.reshape(held.shape).astype(BF)
    for m in range(4):
        outs[m][...] = held[m ^ e]


def land_tokens(ids, b0, b1, b2, b3, out):
    g = ids[1]
    for m, block in enumerate((b0, b1, b2, b3)):
        v = m ^ g
        out[v & 1, v >> 1] = block[...].T


def qkv_windows(ids, w, *rest):
    outs, tall = rest[:4], rest[4]
    c, g, z, d = place(ids)
    rows = w.shape[1]
    tall[:rows] = w[...].astype(F32).T
    tall[rows:] = jnp.zeros((tall.shape[0] - rows, tall.shape[1]), F32)
    for k in range(4):
        to = c * 4 + (g ^ k)
        start, _, _ = run_of(ids, to, z)
        outs[k][:WINDOW] = tall[pl.ds(aligned(start, 16), WINDOW)].astype(BF)
        shared = jnp.maximum(272 * z - HEAD_DIM + 8 * to, 0)
        outs[k][WINDOW:] = jnp.concatenate(
            [tall[pl.ds(aligned(shared, 8), 8)], jnp.zeros((8, tall.shape[1]), F32)], 0
        ).astype(BF)


def join_lanes(ids, b0, b1, b2, b3, out, held):
    g = ids[1]
    for k, block in enumerate((b0, b1, b2, b3)):
        held[g ^ k] = block[...]
    part = held.shape[2]
    for i in range(4):
        out[:, i * part : (i + 1) * part] = held[i]


def qkv_assemble(ids, b0, b1, b2, b3, out, shared, held, tall):
    c, g, z, d = place(ids)
    for s, block in enumerate((b0, b1, b2, b3)):
        held[(z + 4 - s) & 3] = block[...]
    for i in range(4):
        _, _, filled = run_of(ids, d, i)
        tall[pl.ds(aligned(filled, 16), WINDOW)] = held[i, :WINDOW]
    out[...] = tall[: out.shape[0]]
    parts = [held[1 + t, WINDOW:].astype(F32)[:8] for t in range(3)]
    shared[...] = jnp.concatenate(parts + [jnp.zeros_like(parts[0])], 0).astype(BF)


def mlp_blocks(ids, up, down, *outs):
    c, g, z, d = place(ids)
    for k in range(4):
        to = c * 4 + (g ^ k)
        outs[k][0] = up[to]
        outs[k][1] = down[to]


def mlp_join(ids, b0, b1, b2, b3, up, down, held):
    g = ids[1]
    for k, block in enumerate((b0, b1, b2, b3)):
        held[g ^ k] = block[...]
    part = held.shape[3]
    for i in range(4):
        up[:, i * part : (i + 1) * part] = held[i, 0]
        down[:, i * part : (i + 1) * part] = held[i, 1]


def out_half(ids, w, out, tall):
    tall[...] = w[...].astype(F32).T
    rows = out.shape[0]
    out[...] = tall[pl.ds(aligned(ids[0] * rows, 8), rows)].astype(BF)


def out_blocks(ids, b0, b1, b2, b3, out, held, wide):
    z = ids[2]
    for s, block in enumerate((b0, b1, b2, b3)):
        held[(z + 4 - s) & 3] = block[...]
    part = held.shape[2]
    for i in range(4):
        wide[:, i * part : (i + 1) * part] = held[i]
    for to in range(8):
        out[to, :, :PAIR] = wide[:, to * PAIR : (to + 1) * PAIR]
        out[to, :, PAIR:] = wide[:, 8 * PAIR :]


def out_weights(w):
    parts = [w[core * 4 + quarter] for quarter in range(4) for core in range(2)]
    return jnp.concatenate([part.astype(F32) for part in parts], 0).astype(BF)


def lane_head(shape):
    return lax.broadcasted_iota(jnp.int32, shape, len(shape) - 1) < HEAD_DIM


def only_head(value, head):
    low = lane_head(value.shape)
    zero = jnp.zeros_like(value)
    return jnp.where(low, value, zero) if head == 0 else jnp.where(low, zero, value)


def softmax_down(scores, allowed):
    masked = jnp.where(allowed, scores, BLOCKED)
    weights = jnp.exp(masked - jnp.max(masked, axis=0, keepdims=True))
    return (weights * (1.0 / jnp.sum(weights, axis=0, keepdims=True))).astype(BF)


def attend(ids, *refs):
    n, refs = refs[:8], refs[8:]
    w, refs = refs[0], refs[1:]
    sh, refs = refs[:8], refs[8:]
    q_bias, v_bias, segments, w_out = refs[:4]
    n_abs, q_out, k_out, v_out, kv_out, qs_out, probs, probs_s, att_rel, att_s, w16, far, near = refs[4:17]
    w16_f, att_abs = refs[17:]
    d = ids[3]
    rows = n_abs.shape[1]
    seq = 8 * rows
    for r in range(8):
        n_abs[r ^ d] = n[r][...]
        for t in range(3):
            w16_f[t, r ^ d] = sh[r][...].astype(F32)[t * 8 : (t + 1) * 8]
    tokens = n_abs[...].reshape(seq, n_abs.shape[2])
    w16_rows = w16_f[...].reshape(3 * HEAD_DIM, n_abs.shape[2]).astype(BF)
    w16[...] = w16_rows
    pair = aligned(d * PAIR, PAIR)
    projected = dot(tokens, w[...], ((1,), (1,)))
    q = (projected[:, :PAIR] + q_bias[:, pl.ds(pair, PAIR)].astype(F32)).astype(BF) * BF(HEAD_DIM**-0.5)
    k = projected[:, PAIR : 2 * PAIR].astype(BF)
    v = (projected[:, 2 * PAIR :] + v_bias[:, pl.ds(pair, PAIR)].astype(F32)).astype(BF)
    q_out[...] = q
    k_out[...] = k
    v_out[...] = v
    nothing = jnp.zeros((1, HEAD_DIM), F32)
    shared_v = jnp.concatenate([nothing, v_bias[:, 8 * PAIR :].astype(F32)], 1)
    shared_q = q_bias[:, 8 * PAIR :].astype(F32)
    kv = (dot(tokens, w16_rows[HEAD_DIM:], ((1,), (1,))) + shared_v).astype(BF)
    qs = (dot(n[0][...], w16_rows[:HEAD_DIM], ((1,), (1,))) + shared_q).astype(BF) * BF(HEAD_DIM**-0.5)
    qs = jnp.concatenate([qs, jnp.zeros_like(qs)], 1)
    kv_out[...] = kv
    qs_out[...] = qs

    seg_row = segments[...]
    seg_col = jnp.broadcast_to(seg_row, (8, seq)).T[:, :1]
    v_t = v.astype(F32).T.astype(BF)
    keys = [only_head(k, h) for h in range(2)]
    step = 2 * rows
    for b in range(4):
        seen = (b + 1) * step
        at = slice(b * step, seen)
        shape = (seen, step)
        causal = lax.broadcasted_iota(jnp.int32, shape, 0) <= lax.broadcasted_iota(jnp.int32, shape, 1) + b * step
        allowed = (seg_col[:seen] == seg_row[:, at]) & causal
        turned = []
        for h in range(2):
            p = softmax_down(dot(keys[h][:seen], q[at], ((1,), (1,))), allowed)
            probs[h, :seen, at] = p
            turned.append(dot(v_t[h * HEAD_DIM : (h + 1) * HEAD_DIM, :seen], p, ((1,), (0,))))
        attended = jnp.concatenate(turned, 0).T.astype(BF)
        att_abs[2 * b] = attended[:rows]
        att_abs[2 * b + 1] = attended[rows:]

    first = aligned(d * rows, rows)
    shape = (seq, rows)
    causal = lax.broadcasted_iota(jnp.int32, shape, 0) <= lax.broadcasted_iota(jnp.int32, shape, 1) + first
    allowed = (seg_col == segments[:, pl.ds(first, rows)]) & causal
    p = softmax_down(dot(only_head(kv, 0), qs, ((1,), (1,))), allowed)
    probs_s[...] = p
    kv_t = kv.astype(F32).T.astype(BF)
    attended_s = dot(kv_t[HEAD_DIM:], p, ((1,), (0,))).T.astype(BF)
    att_s[...] = attended_s

    for r in range(8):
        att_rel[r] = att_abs[r ^ d]
    wo = out_weights(w_out)
    for half, out in ((1, far), (0, near)):
        block = att_rel[4 * half : 4 * half + 4].reshape(4 * rows, PAIR)
        branch = dot(block, wo[:, :PAIR], ((1,), (1,)))
        out[...] = branch.astype(BF).reshape(out.shape)
        if half == 0:
            out[0] = (branch[:rows] + dot(attended_s, wo[:, PAIR:], ((1,), (1,)))).astype(BF)


def attend_back(ids, *refs):
    gb, refs = refs[:8], refs[8:]
    w_out, q_in, k_in, v_in, kv_in, qs_in, probs, probs_s, w, w16 = refs[:10]
    gb_rel, grads, grad_qs, sums, far = refs[10:15]
    g_abs, grads_rel = refs[15:]
    d = ids[3]
    rows = gb_rel.shape[1]
    seq = 8 * rows
    width = gb_rel.shape[2]
    for r in range(8):
        gb_rel[r] = gb[r][...]
    wo = out_weights(w_out)
    back = dot(gb_rel[...].reshape(seq, width), wo[:, :PAIR], ((1,), (0,))).astype(BF)
    for r in range(8):
        g_abs[r ^ d] = back[r * rows : (r + 1) * rows]
    g_all = g_abs[...].reshape(seq, PAIR)
    g_s = dot(gb[0][...], wo[:, PAIR:], ((1,), (0,))).astype(BF)
    q, k, v, kv, qs = q_in[...], k_in[...], v_in[...], kv_in[...], qs_in[...]
    scale = HEAD_DIM**-0.5
    k_t = k.astype(F32).T.astype(BF)
    values = [only_head(v, h) for h in range(2)]
    step = 2 * rows
    grad_q = []
    grad_k = [[jnp.zeros((step, PAIR), F32) for _ in range(4)] for _ in range(2)]
    grad_v = [[jnp.zeros((step, PAIR), F32) for _ in range(4)] for _ in range(2)]
    for b in range(4):
        seen = (b + 1) * step
        at = slice(b * step, seen)
        turned = []
        for h in range(2):
            p_low = probs[h, :seen, at]
            p = p_low.astype(F32)
            gp = dot(values[h][:seen], g_all[at], ((1,), (1,)))
            inner = jnp.sum(p * gp, axis=0, keepdims=True)
            gs = (p * (gp - inner)).astype(BF)
            turned.append(dot(k_t[h * HEAD_DIM : (h + 1) * HEAD_DIM, :seen], gs, ((1,), (0,))) * scale)
            dk = dot(gs, q[at], ((1,), (0,)))
            dv = dot(p_low, g_all[at], ((1,), (0,)))
            for i in range(b + 1):
                grad_k[h][i] = grad_k[h][i] + dk[i * step : (i + 1) * step]
                grad_v[h][i] = grad_v[h][i] + dv[i * step : (i + 1) * step]
        grad_q.append(jnp.concatenate(turned, 0).T)
    low = lane_head((step, PAIR))
    qsum = jnp.zeros((1, PAIR), F32)
    vsum = jnp.zeros((1, PAIR), F32)
    for i in range(4):
        dq = grad_q[i].astype(BF)
        dk = jnp.where(low, grad_k[0][i], grad_k[1][i]).astype(BF)
        dv = jnp.where(low, grad_v[0][i], grad_v[1][i]).astype(BF)
        qsum = qsum + column_sum(dq.astype(F32))
        vsum = vsum + column_sum(dv.astype(F32))
        for j in range(2):
            part = slice(j * rows, (j + 1) * rows)
            grads[2 * i + j, :, :PAIR] = dq[part]
            grads[2 * i + j, :, PAIR : 2 * PAIR] = dk[part]
            grads[2 * i + j, :, 2 * PAIR : 3 * PAIR] = dv[part]

    p_low = probs_s[...]
    p = p_low.astype(F32)
    v_s = jnp.concatenate([kv[:, HEAD_DIM:], jnp.zeros((seq, HEAD_DIM), BF)], 1)
    g_pad = jnp.concatenate([g_s, jnp.zeros((rows, HEAD_DIM), BF)], 1)
    gp = dot(v_s, g_pad, ((1,), (1,)))
    inner = jnp.sum(p * gp, axis=0, keepdims=True)
    gs = (p * (gp - inner)).astype(BF)
    kv_t = kv.astype(F32).T.astype(BF)
    dq = (dot(kv_t[:HEAD_DIM], gs, ((1,), (0,))) * scale).T.astype(BF)
    grad_qs[...] = dq
    dk = dot(gs, qs, ((1,), (0,)))[:, :HEAD_DIM]
    dv = dot(p_low, g_pad, ((1,), (0,)))[:, :HEAD_DIM]
    dkv = jnp.concatenate([dk, dv], 1).astype(BF)
    for r in range(8):
        grads[r, :, 3 * PAIR :] = dkv[r * rows : (r + 1) * rows]
    last = jnp.concatenate([column_sum(dq.astype(F32)), column_sum(dv.astype(BF).astype(F32))], 1)
    sums[...] = jnp.concatenate([qsum, vsum, last, jnp.zeros((5, PAIR), F32)], 0)

    for r in range(4):
        grads_rel[r] = grads[(r + 4) ^ d]
    joined = jnp.concatenate([w[...], w16[HEAD_DIM:]], 0)
    out = dot(grads_rel[...].reshape(4 * rows, 4 * PAIR), joined, ((1,), (0,)))
    far[...] = out.astype(BF).reshape(far.shape)


def qkv_grads(ids, grads, n_abs, grad_qs, n_own, *refs):
    o0, o1, o2, o3, shared_far, shared_near = refs[:6]
    tall, s32 = refs[6:]
    c, g, z, d = place(ids)
    rows, width = n_abs.shape[1], n_abs.shape[2]
    seq = 8 * rows
    tokens = n_abs[...].reshape(seq, width)
    out = dot(grads[...].reshape(seq, 4 * PAIR), tokens, ((0,), (0,)))
    tall[: 3 * PAIR] = out[: 3 * PAIR]
    tall[3 * PAIR :] = jnp.zeros((WINDOW, width), F32)
    line = lax.broadcasted_iota(jnp.int32, (WINDOW, width), 0)
    for s, ref in enumerate((o0, o1, o2, o3)):
        to = (z + s) & 3
        _, length, filled = run_of(ids, d, to)
        window = tall[pl.ds(aligned(filled, 16), WINDOW)]
        ref[...] = jnp.where(line < length, window, 0.0).astype(BF)
    q_part = dot(grad_qs[...], n_own[...], ((0,), (0,)))
    s32[...] = jnp.zeros(s32.shape, F32)
    for a in range(8):
        s32[a, :8] = q_part[a * 8 : (a + 1) * 8]
        s32[a, 8:16] = out[3 * PAIR + a * 8 : 3 * PAIR + (a + 1) * 8]
        s32[a, 16:24] = out[3 * PAIR + HEAD_DIM + a * 8 : 3 * PAIR + HEAD_DIM + (a + 1) * 8]
    for r in range(4):
        shared_near[r] = s32[r ^ d].astype(BF)
        shared_far[r] = s32[(r + 4) ^ d].astype(BF)


def first_near(ids, grads, w, w16, grad_qs, near, grads_rel):
    d = ids[3]
    rows = near.shape[1]
    for r in range(4):
        grads_rel[r] = grads[r ^ d]
    joined = jnp.concatenate([w[...], w16[HEAD_DIM:]], 0)
    out = dot(grads_rel[...].reshape(4 * rows, 4 * PAIR), joined, ((1,), (0,)))
    near[...] = out.astype(BF).reshape(near.shape)
    near[0] = (out[:rows] + dot(grad_qs[...], w16[:HEAD_DIM], ((1,), (0,)))).astype(BF)


def out_grads(ids, gb_rel, att_rel, att_s, out):
    rows, width = gb_rel.shape[1], gb_rel.shape[2]
    tokens = gb_rel[...].reshape(8 * rows, width)
    pair = dot(att_rel[...].reshape(8 * rows, PAIR), tokens, ((0,), (0,))).T
    shared = dot(att_s[...], gb_rel[0], ((0,), (0,))).T
    part = out.shape[1]
    for core in range(2):
        for quarter in range(4):
            at = slice((2 * quarter + core) * part, (2 * quarter + core + 1) * part)
            out[core * 4 + quarter] = jnp.concatenate([pair[at], shared[at]], 1).astype(BF)


def add_far(ids, near, far, s0, s1, s2, s3):
    s0[...] = near[0].astype(F32) + far[0].astype(F32)
    for k, ref in ((1, s1), (2, s2), (3, s3)):
        ref[...] = (near[k].astype(F32) + far[k].astype(F32)).astype(BF)


def add_far_shared(ids, near, far, shared_near, shared_far, s0, s1, s2, s3, t0, t1, t2, t3):
    add_far(ids, near, far, s0, s1, s2, s3)
    add_far(ids, shared_near, shared_far, t0, t1, t2, t3)


def total_of(s0, r1, r2, r3):
    return s0[...] + r1[...].astype(F32) + r2[...].astype(F32) + r3[...].astype(F32)


def middle_norm(ids, s0, r1, r2, r3, x_own, bias, gain, shift, middle, low):
    rows = x_own[...].astype(F32) + (total_of(s0, r1, r2, r3) + bias[...].astype(F32))
    middle[...] = rows
    low[...] = (normed(rows)[0] * gain[...].astype(F32) + shift[...].astype(F32)).astype(BF)


def middle_back(ids, s0, r1, r2, r3, middle, g_own, gain, grad_middle, low, sums):
    upstream = total_of(s0, r1, r2, r3)
    centered, inverse = normed(middle[...])
    g = g_own[...].astype(F32)
    grad = g + norm_pull(upstream, centered, inverse, gain[...].astype(F32))
    grad_middle[...] = grad
    rounded = grad.astype(BF)
    low[...] = rounded
    sums[...] = jnp.concatenate(
        [
            column_sum(rounded.astype(F32)),
            column_sum(upstream * centered),
            column_sum(upstream),
            column_sum(g),
        ],
        0,
    )


def finish_out(ids, s0, r1, r2, r3, middle, bias, o0, o1, o2, o3, held):
    rows = middle[...] + (total_of(s0, r1, r2, r3) + bias[...].astype(F32))
    split_features(ids, rows, held, (o0, o1, o2, o3))


def finish_in(ids, s0, r1, r2, r3, t0, u1, u2, u3, grad_middle, x_own, gain, *refs):
    o0, o1, o2, o3, sums, w0, w1, w2, w3 = refs[:9]
    held, s32 = refs[9:]
    z = ids[2]
    upstream = total_of(s0, r1, r2, r3)
    centered, inverse = normed(x_own[...].astype(F32))
    rows = grad_middle[...] + norm_pull(upstream, centered, inverse, gain[...].astype(F32))
    split_features(ids, rows, held, (o0, o1, o2, o3))
    sums[...] = jnp.concatenate([column_sum(upstream * centered), column_sum(upstream)], 0)
    shared = total_of(t0, u1, u2, u3)
    blank = jnp.zeros((16, shared.shape[1]), F32)
    s32[0] = blank
    for t in range(3):
        s32[1 + t] = jnp.concatenate([shared[t * 8 : (t + 1) * 8], blank[:8]], 0)
    for s, ref in enumerate((w0, w1, w2, w3)):
        ref[...] = s32[(z + s) & 3].astype(BF)


def grad_activated(ids, *refs):
    g, down, g_rel, out = refs[:8], refs[8], refs[9], refs[10]
    rows = g_rel.shape[1]
    for r in range(8):
        g_rel[r] = g[r][...]
    for b in range(4):
        block = g_rel[2 * b : 2 * b + 2].reshape(2 * rows, g_rel.shape[2])
        out[b * 2 * rows : (b + 1) * 2 * rows] = dot(block, down[...], ((1,), (1,)))


def feed_forward(ids, *refs):
    n, refs = refs[:8], refs[8:]
    up, grad_act, bias, n_rel, act, grad_pre, bias_sum, far, near = refs
    rows = n_rel.shape[1]
    for r in range(8):
        n_rel[r] = n[r][...]
    total = jnp.zeros(bias_sum.shape, F32)
    for b in (2, 3, 0, 1):
        at = slice(b * 2 * rows, (b + 1) * 2 * rows)
        block = n_rel[2 * b : 2 * b + 2].reshape(2 * rows, n_rel.shape[2])
        pre = dot(block, up[...], ((1,), (1,))) + bias[...]
        square = pre * pre
        bent = jnp.tanh(ROOT * pre * (1.0 + 0.044715 * square))
        half = 0.5 * (1.0 + bent)
        act[at] = (pre * half).astype(BF)
        slope = half + 0.5 * pre * (1.0 - bent * bent) * (ROOT + ROOT * 3.0 * 0.044715 * square)
        low = (grad_act[at] * slope).astype(BF)
        grad_pre[at] = low
        total = total + column_sum(low.astype(F32))
        out = dot(low, up[...], ((1,), (0,))).astype(BF)
        ref = far if b >= 2 else near
        for j in range(2):
            ref[2 * (b % 2) + j] = out[j * rows : (j + 1) * rows]
    bias_sum[...] = total


def feed_out(ids, act, down, far, near):
    rows = near.shape[1]
    for b in (2, 3, 0, 1):
        out = dot(act[b * 2 * rows : (b + 1) * 2 * rows], down[...], ((1,), (0,))).astype(BF)
        ref = far if b >= 2 else near
        for j in range(2):
            ref[2 * (b % 2) + j] = out[j * rows : (j + 1) * rows]


def mlp_grads(ids, act, grad_pre, n_rel, g_rel, out):
    rows, width = n_rel.shape[1], n_rel.shape[2]
    part = out.shape[2]
    up = dot(grad_pre[...], n_rel[...].reshape(8 * rows, width), ((0,), (0,)))
    for i in range(4):
        out[i, 0] = up[i * part : (i + 1) * part].astype(BF)
    down = dot(act[...], g_rel[...].reshape(8 * rows, width), ((0,), (0,)))
    for i in range(4):
        out[i, 1] = down[i * part : (i + 1) * part].astype(BF)


def mlp_lanes(ids, summed, o0, o1, o2, o3, held):
    g = ids[1]
    part = held.shape[3]
    for i in range(4):
        held[i] = summed[:, :, i * part : (i + 1) * part]
    for k, ref in enumerate((o0, o1, o2, o3)):
        ref[...] = held[g ^ k]


def mlp_land(ids, *refs):
    blocks, up, down, held = refs[:8], refs[8], refs[9], refs[10]
    d = ids[3]
    for r in range(8):
        held[r ^ d] = blocks[r][...].astype(F32)
    up[...] = held[:, 0].reshape(-1, held.shape[3]).T
    down[...] = held[:, 1].reshape(-1, held.shape[3])


def qkv_lanes(ids, b0, b1, b2, b3, w0, w1, w2, w3, o0, o1, o2, o3, held):
    g = ids[1]
    part = held.shape[2]
    window = sum(ref[...].astype(F32) for ref in (b0, b1, b2, b3))
    shared = sum(ref[...].astype(F32) for ref in (w0, w1, w2, w3))
    for i in range(4):
        held[i, :WINDOW] = window[:, i * part : (i + 1) * part].astype(BF)
        held[i, WINDOW:] = shared[:, i * part : (i + 1) * part].astype(BF)
    for k, ref in enumerate((o0, o1, o2, o3)):
        ref[...] = held[g ^ k]


def qkv_land(ids, *refs):
    blocks, out, tall = refs[:8], refs[8], refs[9]
    c, g, z, d = place(ids)
    tall[...] = jnp.zeros(tall.shape, F32)
    keep = jnp.where(z > 0, 1.0, 0.0)
    for r in range(8):
        owner = r ^ d
        start, _, _ = run_of(ids, owner, z)
        start = aligned(start, 16)
        block = blocks[r][...].astype(F32)
        tall[pl.ds(start, WINDOW)] = tall[pl.ds(start, WINDOW)] + block[:WINDOW]
        at = aligned(jnp.maximum(272 * z - HEAD_DIM + 8 * owner, 0), 8)
        tall[pl.ds(at, 8)] = tall[pl.ds(at, 8)] + block[WINDOW : WINDOW + 8] * keep
    out[...] = tall[: out.shape[1]].T


def out_split(ids, got, o0, o1, o2, o3, wide, held):
    z = ids[2]
    part = held.shape[2]
    shared = jnp.zeros((got.shape[1], HEAD_DIM), F32)
    for a in range(8):
        wide[:, a * PAIR : (a + 1) * PAIR] = got[a, :, :PAIR].astype(F32)
        shared = shared + got[a, :, PAIR:].astype(F32)
    wide[:, 8 * PAIR :] = shared
    for i in range(4):
        held[i] = wide[:, i * part : (i + 1) * part].astype(BF)
    for s, ref in enumerate((o0, o1, o2, o3)):
        ref[...] = held[(z + s) & 3]


def sum_four(ids, b0, b1, b2, b3, out):
    out[...] = sum(ref[...].astype(F32) for ref in (b0, b1, b2, b3)).astype(BF)


def out_land(ids, mine, theirs, out, held):
    c = ids[0]
    held[c] = mine[...].astype(F32)
    held[1 - c] = theirs[...].astype(F32)
    out[...] = held[...].reshape(-1, held.shape[2]).T


def shards(
    hidden_in,
    segment_ids,
    cotangent,
    norm1_gain,
    norm1_shift,
    w_qkv,
    q_bias,
    v_bias,
    w_out,
    out_bias,
    norm2_gain,
    norm2_shift,
    w_up,
    up_bias,
    w_down,
    down_bias,
):
    c = lax.axis_index("c")
    g = lax.axis_index("gx")
    z = lax.axis_index("gy")
    d = c * 4 + g
    width = norm1_gain.shape[0]
    hidden = up_bias.shape[0]
    quarter = hidden_in.shape[2]
    half = quarter // 2
    part = hidden // 32
    own_hidden = hidden // 8
    cols = w_qkv.shape[1]
    seq = segment_ids.shape[1]
    rows = seq // 8
    outer = lax.axis_size("do") > 1
    ids = jnp.concatenate(
        [jnp.stack([c, g, z, d]).astype(jnp.int32), jnp.asarray(run_table(width, cols))]
    )

    def row(vector):
        return vector.reshape(1, -1)

    def over_outer(value):
        return lax.psum(value, "do") if outer else value

    block = ((quarter, rows), BF)
    own_bf, own_f32 = ((rows, width), BF), ((rows, width), F32)
    held_tokens = ((4, quarter, rows), BF)

    def move_in(tokens):
        sent = kernel(send_tokens, [block] * 4, [], ids, tokens.reshape(2, 2, rows, quarter), us=1.0)
        return [lax.ppermute(sent[m], EVERY, MOVES[m]) for m in range(4)]

    def move_out(blocks):
        got = [lax.ppermute(blocks[m], EVERY, BACK[m]) for m in range(4)]
        out = kernel(land_tokens, [((2, 2, rows, quarter), BF)], [], ids, *got, us=1.0)
        return out.reshape(2, 2 * rows, quarter)

    x_blocks = move_in(hidden_in)

    window = ((TALL, quarter), BF)
    windows = kernel(qkv_windows, [window] * 4, [((cols + WINDOW, quarter), F32)], ids, w_qkv, us=1.5)
    windows = [windows[0]] + [from_peer(windows[k], k) for k in range(1, 4)]
    joined = kernel(join_lanes, [((TALL, width), BF)], [((4, TALL, quarter), BF)], ids, *windows, us=1.0)
    x_own, n1_own = kernel(
        take_normed, [own_bf, own_bf], [held_tokens], ids, *x_blocks, row(norm1_gain), row(norm1_shift), us=1.5
    )
    n1 = gather_plane(n1_own)
    joined = [joined] + [from_below(joined, s) for s in range(1, 4)]
    w_own, w_shared = kernel(
        qkv_assemble,
        [((3 * PAIR, width), BF), ((32, width), BF)],
        [((4, TALL, width), BF), ((3 * PAIR + WINDOW, width), BF)],
        ids,
        *joined,
        us=1.0,
    )
    w_shared = gather_plane(w_shared)

    out_piece = kernel(out_half, [((half, quarter), BF)], [((quarter, quarter), F32)], ids, w_out, us=0.7)
    out_pieces = [out_piece] + [from_below(out_piece, s) for s in range(1, 4)]
    out_sent = kernel(
        out_blocks,
        [((8, half, PAIR + HEAD_DIM), BF)],
        [((4, half, quarter), BF), ((half, width), BF)],
        ids,
        *out_pieces,
        us=0.7,
    )
    wo = lax.all_to_all(out_sent, PLANE, split_axis=0, concat_axis=0, tiled=True)

    mlp_sent = kernel(
        mlp_blocks,
        [((2, part, quarter), BF)] * 4,
        [],
        ids,
        w_up.T.reshape(8, part, quarter),
        w_down.reshape(8, part, quarter),
        us=1.0,
    )
    mlp_got = [mlp_sent[0]] + [from_peer(mlp_sent[k], k) for k in range(1, 4)]
    up_part, down_part = kernel(
        mlp_join, [((part, width), BF)] * 2, [((4, 2, part, quarter), BF)], ids, *mlp_got, us=1.0
    )
    up_own = lax.all_gather(up_part, "gy", axis=0, tiled=False).reshape(own_hidden, width)
    down_own = lax.all_gather(down_part, "gy", axis=0, tiled=False).reshape(own_hidden, width)
    up_bias_own = lax.dynamic_index_in_dim(up_bias.reshape(4, 8, part), d, 1, False).reshape(1, -1).astype(F32)

    g_own = kernel(take_tokens, [own_bf], [held_tokens], ids, *move_in(cotangent), us=1.0)
    g_all = gather_plane(g_own)

    ids_other = swap_core(segment_ids)
    segments = lax.dynamic_index_in_dim(jnp.where(z % 2 == c, segment_ids, ids_other), z // 2, 0, False)
    segments = row(segments.astype(F32))

    half_rows = ((4, rows, width), BF)
    pair_seq = ((seq, PAIR), BF)
    n_abs, q, k, v, kv, qs, probs, probs_s, att_rel, att_s, w16, far, near = kernel(
        attend,
        [
            ((8, rows, width), BF),
            pair_seq,
            pair_seq,
            pair_seq,
            pair_seq,
            ((rows, PAIR), BF),
            ((2, seq, seq), BF),
            ((seq, rows), BF),
            ((8, rows, PAIR), BF),
            ((rows, HEAD_DIM), BF),
            ((3 * HEAD_DIM, width), BF),
            half_rows,
            half_rows,
        ],
        [((3, 8, 8, width), F32), ((8, rows, PAIR), BF)],
        ids,
        *n1,
        w_own,
        *w_shared,
        row(q_bias),
        row(v_bias),
        segments,
        wo,
        us=12.0,
        limit=56,
    )
    summed = [own_f32, own_bf, own_bf, own_bf]

    def scatter(near, far):
        s = kernel(add_far, summed, [], ids, near, swap_core(far), us=1.2)
        return [s[0]] + [from_peer(s[k], k) for k in range(1, 4)]

    middle, n2_own = kernel(
        middle_norm,
        [own_f32, own_bf],
        [],
        ids,
        *scatter(near, far),
        x_own,
        row(out_bias),
        row(norm2_gain),
        row(norm2_shift),
        us=1.0,
    )
    n2 = gather_plane(n2_own)

    all_bf = ((8, rows, width), BF)
    g_rel, grad_act = kernel(
        grad_activated, [all_bf, ((seq, own_hidden), F32)], [], ids, *g_all, down_own, us=3.0
    )
    n_rel, act, grad_pre, up_sum, far, near = kernel(
        feed_forward,
        [
            all_bf,
            ((seq, own_hidden), BF),
            ((seq, own_hidden), BF),
            ((1, own_hidden), F32),
            half_rows,
            half_rows,
        ],
        [],
        ids,
        *n2,
        up_own,
        grad_act,
        up_bias_own,
        us=7.0,
    )
    parts = scatter(near, far)
    feed_far, feed_near = kernel(feed_out, [half_rows, half_rows], [], ids, act, down_own, us=2.5)
    mlp_partial = kernel(mlp_grads, [((4, 2, part, width), BF)], [], ids, act, grad_pre, n_rel, g_rel, us=5.0)
    mlp_summed = over_outer(lax.psum_scatter(mlp_partial, "gy", scatter_dimension=0, tiled=False))
    grad_middle, gb_own, middle_sums = kernel(
        middle_back,
        [own_f32, own_bf, ((4, width), F32)],
        [],
        ids,
        *parts,
        middle,
        g_own,
        row(norm2_gain),
        us=1.2,
    )
    gb = gather_plane(gb_own)
    result = kernel(
        finish_out,
        [block] * 4,
        [held_tokens],
        ids,
        *scatter(feed_near, feed_far),
        middle,
        row(down_bias),
        us=1.2,
    )
    hidden_out = move_out(result)

    gb_rel, grads, grad_qs, qkv_sums, far = kernel(
        attend_back,
        [all_bf, ((8, rows, 4 * PAIR), BF), ((rows, HEAD_DIM), BF), ((8, PAIR), F32), half_rows],
        [((8, rows, PAIR), BF), ((4, rows, 4 * PAIR), BF)],
        ids,
        *gb,
        wo,
        q,
        k,
        v,
        kv,
        qs,
        probs,
        probs_s,
        w_own,
        w16,
        us=14.0,
        limit=56,
    )
    far = swap_core(far)
    shared_rows = ((4, 32, width), BF)
    window_wide = ((WINDOW, width), BF)
    windows = kernel(
        qkv_grads,
        [window_wide] * 4 + [shared_rows] * 2,
        [((3 * PAIR + WINDOW, width), F32), ((8, 32, width), F32)],
        ids,
        grads,
        n_abs,
        grad_qs,
        n1_own,
        us=4.0,
    )
    shared_far, shared_near = swap_core(windows[4]), windows[5]
    windows = [windows[0]] + [from_below(windows[s], s) for s in range(1, 4)]
    near = kernel(
        first_near, [half_rows], [((4, rows, 4 * PAIR), BF)], ids, grads, w_own, w16, grad_qs, us=1.2
    )
    small_bf, small_f32 = ((32, width), BF), ((32, width), F32)
    s = kernel(
        add_far_shared,
        summed + [small_f32, small_bf, small_bf, small_bf],
        [],
        ids,
        near,
        far,
        shared_near,
        shared_far,
        us=1.4,
    )
    parts = [s[0]] + [from_peer(s[k], k) for k in range(1, 4)]
    shared_parts = [s[4]] + [from_peer(s[4 + k], k) for k in range(1, 4)]
    done = kernel(
        finish_in,
        [block] * 4 + [((2, width), F32)] + [((16, width), BF)] * 4,
        [held_tokens, ((4, 16, width), F32)],
        ids,
        *parts,
        *shared_parts,
        grad_middle,
        x_own,
        row(norm1_gain),
        us=1.5,
    )
    grad_in = move_out(done[:4])
    first_sums = done[4]
    shared_windows = [done[5]] + [from_below(done[5 + s], s) for s in range(1, 4)]

    lanes = kernel(
        mlp_lanes, [((2, part, quarter), BF)] * 4, [((4, 2, part, quarter), BF)], ids, mlp_summed, us=1.0
    )
    near = [lanes[0]] + [from_peer(lanes[k], k) for k in range(1, 4)]
    total_up, total_down = kernel(
        mlp_land,
        [((quarter, hidden // 4), F32), ((hidden // 4, quarter), F32)],
        [((8, 2, part, quarter), F32)],
        ids,
        *near,
        *[swap_core(piece) for piece in near],
        us=2.0,
    )

    out_sent = kernel(out_grads, [((8, half, PAIR + HEAD_DIM), BF)], [], ids, gb_rel, att_rel, att_s, us=2.5)
    out_got = lax.all_to_all(out_sent, PLANE, split_axis=0, concat_axis=0, tiled=True)
    out_split_parts = kernel(
        out_split,
        [((half, quarter), BF)] * 4,
        [((half, width), F32), ((4, half, quarter), BF)],
        ids,
        out_got,
        us=1.0,
    )
    out_split_parts = [out_split_parts[0]] + [from_below(out_split_parts[s], s) for s in range(1, 4)]
    mine = kernel(sum_four, [((half, quarter), BF)], [], ids, *out_split_parts, us=0.6)
    total_out = kernel(
        out_land, [((quarter, quarter), F32)], [((2, half, quarter), F32)], ids, mine, swap_core(mine), us=0.7
    )
    total_out = over_outer(total_out)

    lanes = kernel(
        qkv_lanes, [window] * 4, [((4, TALL, quarter), BF)], ids, *windows, *shared_windows, us=1.0
    )
    near = [lanes[0]] + [from_peer(lanes[k], k) for k in range(1, 4)]
    total_qkv = kernel(
        qkv_land,
        [((quarter, cols), F32)],
        [((cols + WINDOW, quarter), F32)],
        ids,
        *near,
        *[swap_core(piece) for piece in near],
        us=2.0,
    )
    total_qkv = over_outer(total_qkv)

    def spread(pair_sums, shared_sums):
        base = jnp.concatenate([jnp.zeros((8 * PAIR,), F32), shared_sums])
        return row(lax.dynamic_update_slice_in_dim(base, pair_sums, d * PAIR, 0))

    up_rows = lax.dynamic_update_slice_in_dim(
        jnp.zeros((4, 8, part), F32), up_sum.reshape(4, 1, part), d, 1
    ).reshape(4, 8 * part)
    smalls = jnp.concatenate(
        [
            first_sums,
            spread(qkv_sums[0], qkv_sums[2, :HEAD_DIM]),
            spread(qkv_sums[1], qkv_sums[2, HEAD_DIM:]),
            middle_sums,
            up_rows,
        ],
        0,
    )
    smalls = smalls + swap_core(smalls)
    smalls = smalls + from_peer(smalls, 1)
    smalls = smalls + from_peer(smalls, 2)
    smalls = smalls + lax.ppermute(smalls, "gy", [(i, i ^ 1) for i in range(4)])
    smalls = smalls + lax.ppermute(smalls, "gy", [(i, i ^ 2) for i in range(4)])
    smalls = over_outer(smalls)

    return (
        hidden_out,
        grad_in,
        smalls[0],
        smalls[1],
        total_qkv,
        smalls[2],
        smalls[3],
        total_out,
        smalls[4],
        smalls[5],
        smalls[6],
        total_up,
        smalls[8:12].reshape(hidden),
        total_down,
        smalls[7],
    )


def solution(mesh):
    devices = mesh.devices
    split = Mesh(
        devices.reshape(devices.shape[0] // 2, 2, devices.shape[1], devices.shape[2]), ("do", "c", "gx", "gy")
    )
    stream = P(None, ("do", "c", "gy"), "gx")
    flat = P()
    tall = P("gx", "gy")
    wide = P("gy", "gx")
    grads = (flat, flat, tall, flat, flat, wide, flat, flat, flat, tall, flat, wide, flat)
    return jax.shard_map(
        shards,
        mesh=split,
        in_specs=(stream, P(None, ("do", "c")), stream, *grads),
        out_specs=(stream, stream, *grads),
        check_vma=False,
    )
```

```python
import math

import jax
import jax.numpy as jnp
import numpy as np
from jax import lax
from jax.experimental import pallas as pl
from jax.experimental.pallas import tpu as pltpu
from jax.sharding import Mesh
from jax.sharding import PartitionSpec as P

HEAD_DIM = 64
PAIR = 2 * HEAD_DIM
EPSILON = 1e-05
BLOCKED = -1e30
BF = jnp.bfloat16
F32 = jnp.float32
PLANE = ("c", "gx")
EVERY = ("c", "gx", "gy")
ROOT = math.sqrt(2.0 / math.pi)
WINDOW = 128
TALL = WINDOW + 16
MIB = 1024 * 1024


def dot(left, right, dims):
    return lax.dot_general(left, right, (dims, ((), ())), preferred_element_type=F32)


def padded(shape, kind):
    size = jnp.dtype(kind).itemsize
    lines = 1 if len(shape) < 2 else -(-shape[-2] // 16) * 16
    return math.prod(shape[:-2]) * lines * (-(-shape[-1] // 128) * 128) * size


def kernel(body, outs, scratch, ids, *arrays, us=1.0, work=2, after=(), far=False):
    count, late = len(arrays), len(after)

    def run(*refs):
        body(*refs[: 1 + count], *refs[1 + count + late :])

    vmem = pl.BlockSpec(memory_space=pltpu.VMEM)
    total = sum(padded(a.shape, a.dtype) for a in arrays) + sum(padded(*o) for o in [*outs, *scratch])
    result = pl.pallas_call(
        run,
        name=body.__name__,
        out_shape=tuple(jax.ShapeDtypeStruct(shape, kind) for shape, kind in outs),
        in_specs=[pl.BlockSpec(memory_space=pltpu.SMEM)] + [vmem] * count + [pl.BlockSpec(memory_space=pl.ANY)] * late,
        out_specs=tuple(vmem for _ in outs),
        scratch_shapes=[pltpu.VMEM(shape, kind) for shape, kind in scratch],
        compiler_params=pltpu.CompilerParams(vmem_limit_bytes=60 * MIB if far else int(total * 1.02) + work * MIB),
        cost_estimate=pl.CostEstimate(flops=int(us * 5e9), bytes_accessed=int(us * 1e5), transcendentals=0),
    )(ids, *arrays, *after)
    return result if len(outs) > 1 else result[0]


def swap_core(value):
    return lax.ppermute(value, "c", [(0, 1), (1, 0)])


def from_peer(value, step):
    return lax.ppermute(value, "gx", [(i, i ^ step) for i in range(4)])


def from_below(value, step):
    return lax.ppermute(value, "gy", [(i, (i + step) % 4) for i in range(4)])


def gather_plane(own):
    near = [own] + [from_peer(own, k) for k in range(1, 4)]
    return near + [swap_core(piece) for piece in near]


def position(c, g, z):
    return (c * 4 + g) * 4 + z


def token_moves():
    moves = []
    for m in range(4):
        move = []
        for c in range(2):
            for g in range(4):
                for z in range(4):
                    t, mb = (m ^ g) >> 1, (m ^ g) & 1
                    move.append((position(c, g, z), position(z // 2, 2 * (z % 2) + t, 2 * mb + c)))
        moves.append(move)
    return moves


MOVES = token_moves()
BACK = [[(b, a) for a, b in move] for move in MOVES]


def run_table(width, cols):
    table = np.zeros((8, 4, 3), np.int32)
    for d in range(8):
        filled = 0
        for z in range(4):
            for t in range(3):
                low = max(width * t + PAIR * d, cols * z)
                high = min(width * t + PAIR * (d + 1), cols * (z + 1))
                if high > low:
                    table[d, z] = (low - cols * z, high - low, filled)
                    filled += high - low
            if table[d, z, 1] == 0:
                table[d, z, 2] = filled
    return table.reshape(-1)


def aligned(value, step):
    return pl.multiple_of(value, step)


def normed(rows):
    average = jnp.mean(rows, axis=1, keepdims=True)
    centered = rows - average
    inverse = lax.rsqrt(jnp.mean(centered * centered, axis=1, keepdims=True) + EPSILON)
    return centered * inverse, inverse


def norm_pull(upstream, centered, inverse, gain):
    scaled = upstream * gain
    return inverse * (
        scaled
        - jnp.mean(scaled, axis=1, keepdims=True)
        - centered * jnp.mean(scaled * centered, axis=1, keepdims=True)
    )


def column_sum(rows):
    return jnp.sum(rows, axis=0, keepdims=True)


def place(ids):
    return ids[0], ids[1], ids[2], ids[3]


def run_of(ids, d, z):
    at = 4 + d * 12 + z * 3
    return ids[at], ids[at + 1], ids[at + 2]


def lanes_of(half, rows):
    return pl.ds(aligned(half * rows, rows), rows)


def send_tokens(ids, x, g_in, *outs):
    g = ids[1]
    for m in range(4):
        v = m ^ g
        for t, src in enumerate((x, g_in)):
            outs[m][t] = src[v & 1, :, lanes_of(v >> 1, outs[m].shape[2])]


def own_rows(ids, blocks, held, which):
    e = 2 * (ids[1] & 1) + (ids[2] >> 1)
    for m in range(4):
        held[m ^ e] = blocks[m][which]
    return held[...].astype(F32).reshape(-1, held.shape[2]).T


def take_tokens(ids, b0, b1, b2, b3, out, held):
    out[...] = own_rows(ids, (b0, b1, b2, b3), held, 1).astype(BF)


def take_normed(ids, b0, b1, b2, b3, vectors, out, low, held):
    rows = own_rows(ids, (b0, b1, b2, b3), held, 0)
    out[...] = rows.astype(BF)
    low[...] = (normed(rows)[0] * vectors[0:1] + vectors[1:2]).astype(BF)


def land_tokens(ids, b0, b1, b2, b3, first, second):
    g = ids[1]
    for m, block in enumerate((b0, b1, b2, b3)):
        v = m ^ g
        for t, out in enumerate((first, second)):
            out[v & 1, :, lanes_of(v >> 1, block.shape[2])] = block[t]


def qkv_windows(ids, w, o0, o1, o2, o3, tall):
    c, g, z, d = place(ids)
    rows = w.shape[1]
    tall[:rows] = w[...].astype(F32).T
    tall[rows:] = jnp.zeros((tall.shape[0] - rows, tall.shape[1]), F32)
    for k, ref in enumerate((o0, o1, o2, o3)):
        start, _, _ = run_of(ids, c * 4 + (g ^ k), z)
        ref[...] = tall[pl.ds(aligned(start, 16), WINDOW)].astype(BF)


def join_lanes(ids, b0, b1, b2, b3, out, held):
    g = ids[1]
    for k, block in enumerate((b0, b1, b2, b3)):
        held[g ^ k] = block[...]
    part = held.shape[2]
    for i in range(4):
        out[:, i * part : (i + 1) * part] = held[i]


def qkv_assemble(ids, b0, b1, b2, b3, out, held, tall):
    c, g, z, d = place(ids)
    for s, block in enumerate((b0, b1, b2, b3)):
        held[(z + 4 - s) & 3] = block[...]
    for i in range(4):
        _, _, filled = run_of(ids, d, i)
        tall[pl.ds(aligned(filled, 16), WINDOW)] = held[i]
    out[...] = tall[: out.shape[0]]


def mlp_blocks(ids, up, down, bias, o0, o1, o2, o3, own_bias, held):
    c, g, z, d = place(ids)
    for t, w in enumerate((up, down)):
        held[t] = w[...].astype(F32).T.reshape(held.shape[1:])
    for k, ref in enumerate((o0, o1, o2, o3)):
        to = c * 4 + (g ^ k)
        ref[0] = held[0, to].astype(BF)
        ref[1] = held[1, to].astype(BF)
    own_bias[...] = jnp.concatenate([bias[i, pl.ds(d, 1)] for i in range(4)], 1)


def mlp_join(ids, b0, b1, b2, b3, up, down, held):
    g = ids[1]
    for k, block in enumerate((b0, b1, b2, b3)):
        held[g ^ k] = block[...]
    part = held.shape[3]
    for i in range(4):
        up[:, i * part : (i + 1) * part] = held[i, 0]
        down[:, i * part : (i + 1) * part] = held[i, 1]


def out_half(ids, w, wq, out, tall):
    c, _, z, _ = place(ids)
    tall[: w.shape[1]] = w[...].astype(F32).T
    out[:TALL] = tall[pl.ds(aligned(c * WINDOW, 8), TALL)].astype(BF)
    tall[: wq.shape[1]] = wq[...].astype(F32).T
    at = jnp.maximum(272 * z - HEAD_DIM, 0) + c * (HEAD_DIM // 2)
    out[TALL:] = tall[pl.ds(aligned(at, 8), HEAD_DIM // 2)].astype(BF)


def out_join(ids, b0, b1, b2, b3, out, held):
    z = ids[2]
    for s, block in enumerate((b0, b1, b2, b3)):
        held[(z + 4 - s) & 3] = block[...]
    part = held.shape[2]
    for i in range(4):
        out[:TALL, i * part : (i + 1) * part] = held[i, :TALL]
    lines = []
    for t in range(3):
        shared = held[1 + t, TALL:].astype(F32)
        lines.append(jnp.concatenate([shared[8 * i : 8 * i + 8] for i in range(4)], 1))
    lines.append(jnp.zeros_like(lines[0]))
    out[TALL:] = jnp.concatenate(lines, 0).astype(BF)


def out_whole(ids, *refs):
    pieces, out, w16, held = refs[:8], refs[8], refs[9], refs[10]
    d = ids[3]
    part = held.shape[5]
    for r in range(8):
        owner = r ^ d
        core, quarter = owner >> 2, owner & 3
        out[pl.ds(aligned(272 * quarter + WINDOW * core, 16), TALL)] = pieces[r][:TALL]
        shared = pieces[r][TALL:].astype(F32)
        for t in range(3):
            for i in range(4):
                held[quarter, t, core, i] = shared[8 * t : 8 * t + 8, i * part : (i + 1) * part]
    for q in range(4):
        w16[:, q * part : (q + 1) * part] = held[q].reshape(3 * HEAD_DIM, part).astype(BF)


def lane_head(shape):
    return lax.broadcasted_iota(jnp.int32, shape, len(shape) - 1) < HEAD_DIM


def only_head(value, head):
    low = lane_head(value.shape)
    zero = jnp.zeros_like(value)
    return jnp.where(low, value, zero) if head == 0 else jnp.where(low, zero, value)


def softmax_down(scores, allowed):
    masked = jnp.where(allowed, scores, BLOCKED)
    weights = jnp.exp(masked - jnp.max(masked, axis=0, keepdims=True))
    return (weights * (1.0 / jnp.sum(weights, axis=0, keepdims=True))).astype(BF)


def causal_mask(shape, first):
    return lax.broadcasted_iota(jnp.int32, shape, 0) <= lax.broadcasted_iota(jnp.int32, shape, 1) + first


def segments_of(ids, mine, theirs):
    c, _, z, _ = place(ids)
    second = (z >> 1) == 1
    near = jnp.where(second, mine[1:2], mine[0:1])
    far = jnp.where(second, theirs[1:2], theirs[0:1])
    return jnp.where((z & 1) == c, near, far).astype(F32)


def upright(seg_row):
    return jnp.broadcast_to(seg_row, (8, seg_row.shape[1])).T[:, :1]


def attend(ids, *refs):
    n, refs = refs[:8], refs[8:]
    w, vectors, mine, theirs, n_abs, q_out, k_out, v_out, probs, att_abs = refs
    d = ids[3]
    rows = n_abs.shape[1]
    seq = 8 * rows
    for r in range(8):
        n_abs[r ^ d] = n[r][...]
    tokens = n_abs[...].reshape(seq, n_abs.shape[2])
    pair = aligned(d * PAIR, PAIR)
    projected = dot(tokens, w[...], ((1,), (1,)))
    q = (projected[:, :PAIR] + vectors[6:7, pl.ds(pair, PAIR)]).astype(BF) * BF(HEAD_DIM**-0.5)
    k = projected[:, PAIR : 2 * PAIR].astype(BF)
    v = (projected[:, 2 * PAIR :] + vectors[7:8, pl.ds(pair, PAIR)]).astype(BF)
    q_out[...] = q
    k_out[...] = k
    v_out[...] = v
    seg_row = segments_of(ids, mine, theirs)
    seg_col = upright(seg_row)
    v_t = v.astype(F32).T.astype(BF)
    keys = [only_head(k, h) for h in range(2)]
    step = 2 * rows
    for b in range(4):
        seen = (b + 1) * step
        at = slice(b * step, seen)
        allowed = (seg_col[:seen] == seg_row[:, at]) & causal_mask((seen, step), b * step)
        turned = []
        for h in range(2):
            p = softmax_down(dot(keys[h][:seen], q[at], ((1,), (1,))), allowed)
            probs[h, :seen, at] = p
            turned.append(dot(v_t[h * HEAD_DIM : (h + 1) * HEAD_DIM, :seen], p, ((1,), (0,))))
        attended = jnp.concatenate(turned, 0).T.astype(BF)
        att_abs[2 * b] = attended[:rows]
        att_abs[2 * b + 1] = attended[rows:]


def attend_shared(ids, n_abs, n_own, w16, vectors, mine, theirs, kv_out, qs_out, probs_s, att_s, seg_row):
    d = ids[3]
    rows, width = n_abs.shape[1], n_abs.shape[2]
    seq = 8 * rows
    w16_rows = w16[...]
    nothing = jnp.zeros((1, HEAD_DIM), F32)
    shared_v = jnp.concatenate([nothing, vectors[7:8, 8 * PAIR :]], 1)
    shared_q = vectors[6:7, 8 * PAIR :]
    kv = (dot(n_abs[...].reshape(seq, width), w16_rows[HEAD_DIM:], ((1,), (1,))) + shared_v).astype(BF)
    qs = (dot(n_own[...], w16_rows[:HEAD_DIM], ((1,), (1,))) + shared_q).astype(BF) * BF(HEAD_DIM**-0.5)
    qs = jnp.concatenate([qs, jnp.zeros_like(qs)], 1)
    kv_out[...] = kv
    qs_out[...] = qs
    first = aligned(d * rows, rows)
    seg_row[...] = segments_of(ids, mine, theirs)
    allowed = (upright(seg_row[...]) == seg_row[:, pl.ds(first, rows)]) & causal_mask((seq, rows), first)
    p = softmax_down(dot(only_head(kv, 0), qs, ((1,), (1,))), allowed)
    probs_s[...] = p
    kv_t = kv.astype(F32).T.astype(BF)
    att_s[...] = dot(kv_t[HEAD_DIM:], p, ((1,), (0,))).T.astype(BF)


def out_norm(ids, got, att_s, wo, x_own, vectors, middle, low):
    attended = jnp.concatenate([got[a] for a in range(8)] + [att_s[...]], 1)
    rows = x_own[...].astype(F32) + (dot(attended, wo[...], ((1,), (1,))) + vectors[4:5])
    middle[...] = rows
    low[...] = (normed(rows)[0] * vectors[2:3] + vectors[3:4]).astype(BF)


def attend_back(ids, g_in, gs_in, q_in, k_in, v_in, kv_in, qs_in, probs, probs_s, w, w16, *refs):
    grads, grad_qs, sums, far, grads_rel = *refs[:3], refs[3:7], refs[7]
    d = ids[3]
    rows = g_in.shape[1]
    seq = 8 * rows
    g_all = g_in[...].reshape(seq, PAIR)
    g_s = gs_in[...]
    q, k, v, kv, qs = q_in[...], k_in[...], v_in[...], kv_in[...], qs_in[...]
    scale = HEAD_DIM**-0.5
    k_t = k.astype(F32).T.astype(BF)
    values = [only_head(v, h) for h in range(2)]
    step = 2 * rows
    grad_q = []
    grad_k = [[jnp.zeros((step, PAIR), F32) for _ in range(4)] for _ in range(2)]
    grad_v = [[jnp.zeros((step, PAIR), F32) for _ in range(4)] for _ in range(2)]
    for b in range(4):
        seen = (b + 1) * step
        at = slice(b * step, seen)
        turned = []
        for h in range(2):
            p_low = probs[h, :seen, at]
            p = p_low.astype(F32)
            gp = dot(values[h][:seen], g_all[at], ((1,), (1,)))
            inner = jnp.sum(p * gp, axis=0, keepdims=True)
            gs = (p * (gp - inner)).astype(BF)
            turned.append(dot(k_t[h * HEAD_DIM : (h + 1) * HEAD_DIM, :seen], gs, ((1,), (0,))) * scale)
            dk = dot(gs, q[at], ((1,), (0,)))
            dv = dot(p_low, g_all[at], ((1,), (0,)))
            for i in range(b + 1):
                grad_k[h][i] = grad_k[h][i] + dk[i * step : (i + 1) * step]
                grad_v[h][i] = grad_v[h][i] + dv[i * step : (i + 1) * step]
        grad_q.append(jnp.concatenate(turned, 0).T)
    low = lane_head((step, PAIR))
    qsum = jnp.zeros((1, PAIR), F32)
    vsum = jnp.zeros((1, PAIR), F32)
    for i in range(4):
        dq = grad_q[i].astype(BF)
        dk = jnp.where(low, grad_k[0][i], grad_k[1][i]).astype(BF)
        dv = jnp.where(low, grad_v[0][i], grad_v[1][i]).astype(BF)
        qsum = qsum + column_sum(dq.astype(F32))
        vsum = vsum + column_sum(dv.astype(F32))
        for j in range(2):
            part = slice(j * rows, (j + 1) * rows)
            grads[2 * i + j, :, :PAIR] = dq[part]
            grads[2 * i + j, :, PAIR : 2 * PAIR] = dk[part]
            grads[2 * i + j, :, 2 * PAIR : 3 * PAIR] = dv[part]

    p_low = probs_s[...]
    p = p_low.astype(F32)
    v_s = jnp.concatenate([kv[:, HEAD_DIM:], jnp.zeros((seq, HEAD_DIM), BF)], 1)
    g_pad = jnp.concatenate([g_s, jnp.zeros((rows, HEAD_DIM), BF)], 1)
    gp = dot(v_s, g_pad, ((1,), (1,)))
    inner = jnp.sum(p * gp, axis=0, keepdims=True)
    gs = (p * (gp - inner)).astype(BF)
    kv_t = kv.astype(F32).T.astype(BF)
    dq = (dot(kv_t[:HEAD_DIM], gs, ((1,), (0,))) * scale).T.astype(BF)
    grad_qs[...] = dq
    dk = dot(gs, qs, ((1,), (0,)))[:, :HEAD_DIM]
    dv = dot(p_low, g_pad, ((1,), (0,)))[:, :HEAD_DIM]
    dkv = jnp.concatenate([dk, dv], 1).astype(BF)
    for r in range(8):
        grads[r, :, 3 * PAIR :] = dkv[r * rows : (r + 1) * rows]
    last = jnp.concatenate([column_sum(dq.astype(F32)), column_sum(dv.astype(BF).astype(F32))], 1)
    sums[...] = jnp.concatenate([qsum, vsum, last, jnp.zeros((5, PAIR), F32)], 0)

    for r in range(4):
        grads_rel[r] = grads[(r + 4) ^ d]
    joined = jnp.concatenate([w[...], w16[HEAD_DIM:]], 0)
    out = dot(grads_rel[...].reshape(4 * rows, 4 * PAIR), joined, ((1,), (0,)))
    for k, ref in enumerate(far):
        ref[...] = out[k * rows : (k + 1) * rows].astype(BF)


def qkv_grads(ids, grads, n_abs, o0, o1, o2, o3, tall):
    c, g, z, d = place(ids)
    rows, width = n_abs.shape[1], n_abs.shape[2]
    seq = 8 * rows
    tokens = n_abs[...].reshape(seq, width)
    tall[: 3 * PAIR] = dot(grads[:, :, : 3 * PAIR].reshape(seq, 3 * PAIR), tokens, ((0,), (0,)))
    tall[3 * PAIR :] = jnp.zeros((WINDOW, width), F32)
    line = lax.broadcasted_iota(jnp.int32, (WINDOW, width), 0)
    for s, ref in enumerate((o0, o1, o2, o3)):
        _, length, filled = run_of(ids, d, (z + s) & 3)
        window = tall[pl.ds(aligned(filled, 16), WINDOW)]
        ref[...] = jnp.where(line < length, window, 0.0).astype(BF)


def first_near(ids, grads, w, w16, grad_qs, near, grads_rel):
    d = ids[3]
    rows = grad_qs.shape[0]
    for r in range(4):
        grads_rel[r] = grads[r ^ d]
    joined = jnp.concatenate([w[...], w16[HEAD_DIM:]], 0)
    out = dot(grads_rel[...].reshape(4 * rows, 4 * PAIR), joined, ((1,), (0,)))
    near[...] = out.astype(BF)
    near[:rows] = (out[:rows] + dot(grad_qs[...], w16[:HEAD_DIM], ((1,), (0,)))).astype(BF)


def out_grads(ids, *refs):
    gb, att_abs, att_s, grads, grad_qs, n_abs, n_own, out, gb_abs = refs[:8], *refs[8:]
    d = ids[3]
    rows, width = gb_abs.shape[1], gb_abs.shape[2]
    seq = 8 * rows
    for r in range(8):
        gb_abs[r ^ d] = gb[r][...]
    pair = dot(att_abs[...].reshape(seq, PAIR), gb_abs[...].reshape(seq, width), ((0,), (0,)))
    shared = dot(att_s[...], gb[0][...], ((0,), (0,)))
    q_part = dot(grad_qs[...], n_own[...], ((0,), (0,)))
    kv_part = dot(grads[:, :, 3 * PAIR :].reshape(seq, PAIR), n_abs[...].reshape(seq, width), ((0,), (0,)))
    tall = jnp.concatenate([pair, shared, q_part, kv_part], 0).T
    part = out.shape[1]
    for core in range(2):
        for quarter in range(4):
            at = slice((2 * quarter + core) * part, (2 * quarter + core + 1) * part)
            out[core * 4 + quarter] = tall[at].astype(BF)


def add_far(ids, near, f0, f1, f2, f3, s0, s1, s2, s3):
    rows = s0.shape[0]
    for k, (far, ref) in enumerate(((f0, s0), (f1, s1), (f2, s2), (f3, s3))):
        ref[...] = (near[k * rows : (k + 1) * rows].astype(F32) + far[...].astype(F32)).astype(ref.dtype)


def total_of(s0, r1, r2, r3):
    return s0[...] + r1[...].astype(F32) + r2[...].astype(F32) + r3[...].astype(F32)


def middle_back(ids, s0, r1, r2, r3, middle, g_own, wo, vectors, grad_middle, low, sums, back, back_s):
    upstream = total_of(s0, r1, r2, r3)
    centered, inverse = normed(middle[...])
    g = g_own[...].astype(F32)
    grad = g + norm_pull(upstream, centered, inverse, vectors[2:3])
    grad_middle[...] = grad
    rounded = grad.astype(BF)
    low[...] = rounded
    attended = dot(rounded, wo[...], ((1,), (0,))).astype(BF)
    for a in range(8):
        back[a] = attended[:, a * PAIR : (a + 1) * PAIR]
    back_s[...] = attended[:, 8 * PAIR :]
    sums[...] = jnp.concatenate(
        [
            column_sum(rounded.astype(F32)),
            column_sum(upstream * centered),
            column_sum(upstream),
            column_sum(g),
        ],
        0,
    )


def split_features(ids, rows, held, outs, which):
    e = 2 * (ids[1] & 1) + (ids[2] >> 1)
    held[...] = rows.T.reshape(held.shape).astype(BF)
    for m in range(4):
        outs[m][which] = held[m ^ e]


def finish(ids, s0, r1, r2, r3, t0, u1, u2, u3, middle, grad_middle, x_own, vectors, *refs):
    outs, sums, held = refs[:4], refs[4], refs[5]
    rows = middle[...] + (total_of(t0, u1, u2, u3) + vectors[5:6])
    split_features(ids, rows, held, outs, 0)
    upstream = total_of(s0, r1, r2, r3)
    centered, inverse = normed(x_own[...].astype(F32))
    rows = grad_middle[...] + norm_pull(upstream, centered, inverse, vectors[0:1])
    split_features(ids, rows, held, outs, 1)
    sums[...] = jnp.concatenate([column_sum(upstream * centered), column_sum(upstream)], 0)


def grad_activated(ids, *refs):
    g, down, g_rel, out = refs[:8], refs[8], refs[9], refs[10]
    rows = g_rel.shape[1]
    for r in range(8):
        g_rel[r] = g[r][...]
    for b in range(4):
        block = g_rel[2 * b : 2 * b + 2].reshape(2 * rows, g_rel.shape[2])
        out[b * 2 * rows : (b + 1) * 2 * rows] = dot(block, down[...], ((1,), (1,)))


def feed_forward(ids, *refs):
    n, refs = refs[:8], refs[8:]
    up, grad_act, bias, n_rel, act, grad_pre, bias_sum = refs[:7]
    far, near = refs[7:11], refs[11]
    rows = n_rel.shape[1]
    for r in range(8):
        n_rel[r] = n[r][...]
    total = jnp.zeros(bias_sum.shape, F32)
    for b in (2, 3, 0, 1):
        at = slice(b * 2 * rows, (b + 1) * 2 * rows)
        block = n_rel[2 * b : 2 * b + 2].reshape(2 * rows, n_rel.shape[2])
        pre = dot(block, up[...], ((1,), (1,))) + bias[...]
        square = pre * pre
        bent = jnp.tanh(ROOT * pre * (1.0 + 0.044715 * square))
        half = 0.5 * (1.0 + bent)
        act[at] = (pre * half).astype(BF)
        slope = half + 0.5 * pre * (1.0 - bent * bent) * (ROOT + ROOT * 3.0 * 0.044715 * square)
        low = (grad_act[at] * slope).astype(BF)
        grad_pre[at] = low
        total = total + column_sum(low.astype(F32))
        out = dot(low, up[...], ((1,), (0,))).astype(BF)
        if b >= 2:
            far[2 * b - 4][...] = out[:rows]
            far[2 * b - 3][...] = out[rows:]
        else:
            near[2 * rows * b : 2 * rows * (b + 1)] = out
    bias_sum[...] = total


def feed_out(ids, act, down, *refs):
    far, near = refs[:4], refs[4]
    half = near.shape[0]
    out = dot(act[half:], down[...], ((1,), (0,))).astype(BF)
    rows = half // 4
    for k, ref in enumerate(far):
        ref[...] = out[k * rows : (k + 1) * rows]
    near[...] = dot(act[:half], down[...], ((1,), (0,))).astype(BF)


def mlp_grads(ids, act, grad_pre, n_rel, g_rel, out):
    rows, width = n_rel.shape[1], n_rel.shape[2]
    part = out.shape[2]
    up = dot(grad_pre[...], n_rel[...].reshape(8 * rows, width), ((0,), (0,)))
    for i in range(4):
        out[i, 0] = up[i * part : (i + 1) * part].astype(BF)
    down = dot(act[...], g_rel[...].reshape(8 * rows, width), ((0,), (0,)))
    for i in range(4):
        out[i, 1] = down[i * part : (i + 1) * part].astype(BF)


def mlp_lanes(ids, summed, o0, o1, o2, o3, held):
    g = ids[1]
    part = held.shape[3]
    for i in range(4):
        held[i] = summed[:, :, i * part : (i + 1) * part]
    for k, ref in enumerate((o0, o1, o2, o3)):
        ref[...] = held[g ^ k]


def mlp_land(ids, *refs):
    blocks, up, down, held = refs[:8], refs[8], refs[9], refs[10]
    d = ids[3]
    for r in range(8):
        held[r ^ d] = blocks[r][...].astype(F32)
    up[...] = held[:, 0].reshape(-1, held.shape[3]).T
    down[...] = held[:, 1].reshape(-1, held.shape[3]).T


def qkv_lanes(ids, b0, b1, b2, b3, o0, o1, o2, o3, held):
    g = ids[1]
    part = held.shape[2]
    window = sum(ref[...].astype(F32) for ref in (b0, b1, b2, b3))
    for i in range(4):
        held[i] = window[:, i * part : (i + 1) * part].astype(BF)
    for k, ref in enumerate((o0, o1, o2, o3)):
        ref[...] = held[g ^ k]


def qkv_land(ids, *refs):
    blocks, mine, theirs, out, tall, held = refs[:8], *refs[8:]
    c, g, z, d = place(ids)
    tall[...] = jnp.zeros(tall.shape, F32)
    for r in range(8):
        start, _, _ = run_of(ids, r ^ d, z)
        at = pl.ds(aligned(start, 16), WINDOW)
        tall[at] = tall[at] + blocks[r][...].astype(F32)
    held[c] = mine[:, 272:].astype(F32)
    held[1 - c] = theirs[:, 272:].astype(F32)
    shared = held[...].reshape(-1, HEAD_DIM).T
    keep = jnp.where(z > 0, 1.0, 0.0)
    at = pl.ds(aligned(jnp.maximum(272 * z - HEAD_DIM, 0), 8), HEAD_DIM)
    tall[at] = tall[at] + shared * keep
    out[...] = tall[: out.shape[1]].T


def out_split(ids, got, o0, o1, o2, o3, wide, held):
    z = ids[2]
    part = wide.shape[1] // 4
    shared = jnp.zeros((got.shape[1], 4 * HEAD_DIM), F32)
    for a in range(8):
        wide[:, a * PAIR : (a + 1) * PAIR] = got[a, :, :PAIR].astype(F32)
        shared = shared + got[a, :, PAIR:].astype(F32)
    wide[:, 8 * PAIR :] = shared[:, :HEAD_DIM]
    for i in range(4):
        at = max(i, 1) * HEAD_DIM
        held[i] = jnp.concatenate(
            [wide[:, i * part : (i + 1) * part], shared[:, at : at + HEAD_DIM]], 1
        ).astype(BF)
    for s, ref in enumerate((o0, o1, o2, o3)):
        ref[...] = held[(z + s) & 3]


def sum_four(ids, b0, b1, b2, b3, out):
    out[...] = sum(ref[...].astype(F32) for ref in (b0, b1, b2, b3)).astype(BF)


def out_land(ids, mine, theirs, out, held):
    c = ids[0]
    held[c] = mine[:, :272].astype(F32)
    held[1 - c] = theirs[:, :272].astype(F32)
    out[...] = held[...].reshape(-1, held.shape[2]).T


def join_sums(ids, first, qkv, middle, up, out):
    d = ids[3]
    out[:2] = first[...]
    out[2:4] = jnp.zeros((2, out.shape[1]), F32)
    at = pl.ds(aligned(d * PAIR, PAIR), PAIR)
    out[2:3, at] = qkv[0:1]
    out[3:4, at] = qkv[1:2]
    out[2:3, 8 * PAIR :] = qkv[2:3, :HEAD_DIM]
    out[3:4, 8 * PAIR :] = qkv[2:3, HEAD_DIM:]
    out[4:8] = middle[...]
    part = up.shape[1] // 4
    for i in range(4):
        piece = up[:, i * part : (i + 1) * part]
        out[8 + i : 9 + i] = jnp.concatenate([jnp.where(d == a, piece, 0.0) for a in range(8)], 1)


def shards(
    hidden_in,
    segment_ids,
    cotangent,
    norm1_gain,
    norm1_shift,
    w_qkv,
    q_bias,
    v_bias,
    w_out,
    out_bias,
    norm2_gain,
    norm2_shift,
    w_up,
    up_bias,
    w_down,
    down_bias,
):
    c = lax.axis_index("c")
    g = lax.axis_index("gx")
    z = lax.axis_index("gy")
    d = c * 4 + g
    width = norm1_gain.shape[0]
    hidden = up_bias.shape[0]
    quarter = hidden_in.shape[2]
    half = quarter // 2
    part = hidden // 32
    own_hidden = hidden // 8
    cols = w_qkv.shape[1]
    seq = segment_ids.shape[1]
    rows = seq // 8
    outer = lax.axis_size("do") > 1
    ids = jnp.concatenate(
        [jnp.stack([c, g, z, d]).astype(jnp.int32), jnp.asarray(run_table(width, cols))]
    )
    vectors = jnp.stack(
        [norm1_gain, norm1_shift, norm2_gain, norm2_shift, out_bias, down_bias, q_bias, v_bias]
    ).astype(F32)

    def row(vector):
        return vector.reshape(1, -1)

    def over_outer(value):
        return lax.psum(value, "do") if outer else value

    block = ((2, quarter, rows), BF)
    own_bf, own_f32 = ((rows, width), BF), ((rows, width), F32)
    held_tokens = ((4, quarter, rows), BF)

    def peers(blocks):
        return [blocks[0]] + [from_peer(blocks[k], k) for k in range(1, 4)]

    def shifted(blocks):
        return [blocks[0]] + [from_below(blocks[s], s) for s in range(1, 4)]

    sent = kernel(
        send_tokens, [block] * 4, [], ids, hidden_in.transpose(0, 2, 1), cotangent.transpose(0, 2, 1), us=1.0
    )
    blocks = [lax.ppermute(sent[m], EVERY, MOVES[m]) for m in range(4)]
    window = ((WINDOW, quarter), BF)
    window_wide = ((WINDOW, width), BF)
    windows = kernel(
        qkv_windows, [window] * 4, [((cols + WINDOW, quarter), F32)], ids, w_qkv, us=1.5, after=(blocks[0],)
    )
    windows = peers(windows)
    x_own, n1_own = kernel(
        take_normed, [own_bf, own_bf], [held_tokens], ids, *blocks, vectors, us=1.5
    )
    joined = kernel(
        join_lanes, [window_wide], [((4, WINDOW, quarter), BF)], ids, *windows, us=1.0, after=(n1_own,)
    )
    n1 = gather_plane(n1_own)
    joined = shifted([joined] * 4)
    wide_piece = TALL + HEAD_DIM // 2
    out_piece = kernel(
        out_half,
        [((wide_piece, quarter), BF)],
        [((cols, quarter), F32)],
        ids,
        w_out,
        w_qkv,
        us=1.0,
        after=(joined[0],),
    )
    out_pieces = shifted([out_piece] * 4)
    *mlp_sent, up_bias_own = kernel(
        mlp_blocks,
        [((2, part, quarter), BF)] * 4 + [((1, own_hidden), F32)],
        [((2, 8, part, quarter), F32)],
        ids,
        w_up,
        w_down.T,
        up_bias.astype(F32).reshape(4, 8, part),
        us=2.0,
        after=(n1_own,),
    )
    mlp_got = peers(mlp_sent)
    out_row = kernel(
        out_join,
        [((wide_piece, width), BF)],
        [((4, wide_piece, quarter), BF)],
        ids,
        *out_pieces,
        us=0.7,
        after=(n1[1], n1[2], n1[3]),
    )
    up_part, down_part = kernel(
        mlp_join,
        [((part, width), BF)] * 2,
        [((4, 2, part, quarter), BF)],
        ids,
        *mlp_got,
        us=1.0,
        after=(joined[1],),
    )
    g_own = kernel(
        take_tokens, [own_bf], [held_tokens], ids, *blocks, us=1.0, after=(up_part, n1[1], n1[2], n1[3])
    )
    out_rows = gather_plane(out_row)
    g_all = gather_plane(g_own)
    w_own = kernel(
        qkv_assemble,
        [((3 * PAIR, width), BF)],
        [((4, WINDOW, width), BF), ((3 * PAIR + WINDOW, width), BF)],
        ids,
        *joined,
        us=1.0,
    )
    up_own = lax.all_gather(up_part, "gy", axis=0, tiled=False).reshape(own_hidden, width)
    down_own = lax.all_gather(down_part, "gy", axis=0, tiled=False).reshape(own_hidden, width)
    swapped_ids = swap_core(segment_ids)

    half_rows = ((4 * rows, width), BF)
    all_bf = ((8, rows, width), BF)
    heads_bf = ((8, rows, PAIR), BF)
    pair_seq = ((seq, PAIR), BF)
    n_abs, q, k, v, probs, att = kernel(
        attend,
        [all_bf, pair_seq, pair_seq, pair_seq, ((2, seq, seq), BF), heads_bf],
        [],
        ids,
        *n1,
        w_own,
        vectors,
        segment_ids,
        swapped_ids,
        us=11.0,
        work=16,
    )
    att_got = lax.all_to_all(att, PLANE, split_axis=0, concat_axis=0, tiled=True)
    wo, w16 = kernel(
        out_whole,
        [((width, width), BF), ((3 * HEAD_DIM, width), BF)],
        [((4, 3, 2, 4, 8, quarter), F32)],
        ids,
        *out_rows,
        us=1.0,
        after=(att,),
    )
    kv, qs, probs_s, att_s = kernel(
        attend_shared,
        [pair_seq, ((rows, PAIR), BF), ((seq, rows), BF), ((rows, HEAD_DIM), BF)],
        [((1, seq), F32)],
        ids,
        n_abs,
        n1_own,
        w16,
        vectors,
        segment_ids,
        swapped_ids,
        us=2.0,
        work=6,
    )
    middle, n2_own = kernel(
        out_norm, [own_f32, own_bf], [], ids, att_got, att_s, wo, x_own, vectors, us=2.0, work=6
    )
    summed = [own_f32, own_bf, own_bf, own_bf]

    def scatter(near, far, after=()):
        return peers(
            kernel(add_far, summed, [], ids, near, *[swap_core(f) for f in far], us=1.2, after=after)
        )

    n2 = gather_plane(n2_own)

    g_rel, grad_act = kernel(
        grad_activated, [all_bf, ((seq, own_hidden), F32)], [], ids, *g_all, down_own, us=3.0, after=(n2_own, up_own)
    )
    n_rel, act, grad_pre, up_sum, *far, near = kernel(
        feed_forward,
        [
            all_bf,
            ((seq, own_hidden), BF),
            ((seq, own_hidden), BF),
            ((1, own_hidden), F32),
            *[own_bf] * 4,
            half_rows,
        ],
        [],
        ids,
        *n2,
        up_own,
        grad_act,
        up_bias_own,
        us=7.0,
        work=8,
    )
    parts = scatter(near, far)
    *feed_far, feed_near = kernel(
        feed_out, [own_bf] * 4 + [half_rows], [], ids, act, down_own, us=2.5, work=4, after=(parts[0],)
    )
    mlp_partial = kernel(
        mlp_grads,
        [((4, 2, part, width), BF)],
        [],
        ids,
        act,
        grad_pre,
        n_rel,
        g_rel,
        us=5.0,
        work=8,
        after=(parts[0],),
    )
    mlp_summed = over_outer(lax.psum_scatter(mlp_partial, "gy", scatter_dimension=0, tiled=False))
    grad_middle, gb_own, middle_sums, back, back_s = kernel(
        middle_back,
        [own_f32, own_bf, ((4, width), F32), heads_bf, ((rows, HEAD_DIM), BF)],
        [],
        ids,
        *parts,
        middle,
        g_own,
        wo,
        vectors,
        us=2.5,
        work=6,
    )
    back = lax.all_to_all(back, PLANE, split_axis=0, concat_axis=0, tiled=True)
    gb = gather_plane(gb_own)

    grads, grad_qs, qkv_sums, *far = kernel(
        attend_back,
        [((8, rows, 4 * PAIR), BF), ((rows, HEAD_DIM), BF), ((8, PAIR), F32)] + [own_bf] * 4,
        [((4, rows, 4 * PAIR), BF)],
        ids,
        back,
        back_s,
        q,
        k,
        v,
        kv,
        qs,
        probs,
        probs_s,
        w_own,
        w16,
        us=10.0,
        work=16,
    )
    windows = kernel(
        qkv_grads,
        [window_wide] * 4,
        [((3 * PAIR + WINDOW, width), F32)],
        ids,
        grads,
        n_abs,
        us=3.0,
        work=6,
    )
    near = kernel(
        first_near,
        [half_rows],
        [((4, rows, 4 * PAIR), BF)],
        ids,
        grads,
        w_own,
        w16,
        grad_qs,
        us=1.2,
        work=4,
        after=(windows[0],),
    )
    windows = shifted(windows)
    parts = scatter(near, far)
    out_sent = kernel(
        out_grads,
        [((8, half, PAIR + 4 * HEAD_DIM), BF)],
        [all_bf],
        ids,
        *gb,
        att,
        att_s,
        grads,
        grad_qs,
        n_abs,
        n1_own,
        us=3.5,
        work=10,
        after=(parts[0],),
    )
    out_got = lax.all_to_all(out_sent, PLANE, split_axis=0, concat_axis=0, tiled=True)
    feed_parts = scatter(feed_near, feed_far, (out_sent,))
    *done, first_sums = kernel(
        finish,
        [block] * 4 + [((2, width), F32)],
        [held_tokens],
        ids,
        *parts,
        *feed_parts,
        middle,
        grad_middle,
        x_own,
        vectors,
        us=2.5,
    )
    landed = [lax.ppermute(done[m], EVERY, BACK[m]) for m in range(4)]
    hidden_out, grad_in = kernel(land_tokens, [((2, quarter, 2 * rows), BF)] * 2, [], ids, *landed, us=1.0)

    lanes = kernel(
        mlp_lanes,
        [((2, part, quarter), BF)] * 4,
        [((4, 2, part, quarter), BF)],
        ids,
        mlp_summed,
        us=1.0,
        after=(out_sent,),
    )
    near = peers(lanes)
    total_up, total_down = kernel(
        mlp_land,
        [((quarter, hidden // 4), F32)] * 2,
        [((8, 2, part, quarter), F32)],
        ids,
        *near,
        *[swap_core(piece) for piece in near],
        us=2.0,
    )
    split_piece = ((half, quarter + HEAD_DIM), BF)
    out_split_parts = shifted(
        kernel(
            out_split,
            [split_piece] * 4,
            [((half, width), F32), ((4, half, quarter + HEAD_DIM), BF)],
            ids,
            out_got,
            us=1.0,
        )
    )
    mine = kernel(sum_four, [split_piece], [], ids, *out_split_parts, us=0.6)
    theirs = swap_core(mine)
    total_out = kernel(
        out_land, [((quarter, quarter), F32)], [((2, half, quarter), F32)], ids, mine, theirs, us=0.7
    )
    total_out = over_outer(total_out)

    lanes = kernel(
        qkv_lanes, [window] * 4, [((4, WINDOW, quarter), BF)], ids, *windows, us=1.0
    )
    near = peers(lanes)
    total_qkv = kernel(
        qkv_land,
        [((quarter, cols), F32)],
        [((cols + WINDOW, quarter), F32), ((2, half, HEAD_DIM), F32)],
        ids,
        *near,
        *[swap_core(piece) for piece in near],
        mine,
        theirs,
        us=2.0,
    )
    total_qkv = over_outer(total_qkv)

    smalls = kernel(
        join_sums, [((12, width), F32)], [], ids, first_sums, qkv_sums, middle_sums, up_sum, us=0.7
    )
    smalls = smalls + swap_core(smalls)
    smalls = smalls + from_peer(smalls, 1)
    smalls = smalls + from_peer(smalls, 2)
    smalls = smalls + lax.ppermute(smalls, "gy", [(i, i ^ 1) for i in range(4)])
    smalls = smalls + lax.ppermute(smalls, "gy", [(i, i ^ 2) for i in range(4)])
    smalls = over_outer(smalls)

    return (
        hidden_out.transpose(0, 2, 1),
        grad_in.transpose(0, 2, 1),
        smalls[0],
        smalls[1],
        total_qkv,
        smalls[2],
        smalls[3],
        total_out,
        smalls[4],
        smalls[5],
        smalls[6],
        total_up,
        smalls[8:12].reshape(hidden),
        total_down.T,
        smalls[7],
    )


def solution(mesh):
    devices = mesh.devices
    split = Mesh(
        devices.reshape(devices.shape[0] // 2, 2, devices.shape[1], devices.shape[2]), ("do", "c", "gx", "gy")
    )
    stream = P(None, ("do", "c", "gy"), "gx")
    flat = P()
    tall = P("gx", "gy")
    wide = P("gy", "gx")
    grads = (flat, flat, tall, flat, flat, wide, flat, flat, flat, tall, flat, wide, flat)
    return jax.shard_map(
        shards,
        mesh=split,
        in_specs=(stream, P(None, ("do", "c")), stream, *grads),
        out_specs=(stream, stream, *grads),
        check_vma=False,
    )
```

```python
import math

import jax
import jax.numpy as jnp
import numpy as np
from jax import lax
from jax.experimental import pallas as pl
from jax.experimental.pallas import tpu as pltpu
from jax.sharding import Mesh
from jax.sharding import PartitionSpec as P

HEAD_DIM = 64
PAIR = 2 * HEAD_DIM
EPSILON = 1e-05
BLOCKED = -1e30
BF = jnp.bfloat16
F32 = jnp.float32
PLANE = ("c", "gx")
EVERY = ("c", "gx", "gy")
ROOT = math.sqrt(2.0 / math.pi)
WINDOW = 128
TALL = WINDOW + 16
MIB = 1024 * 1024


def dot(left, right, dims):
    return lax.dot_general(left, right, (dims, ((), ())), preferred_element_type=F32)


def padded(shape, kind):
    size = jnp.dtype(kind).itemsize
    lines = 1 if len(shape) < 2 else -(-shape[-2] // 16) * 16
    return math.prod(shape[:-2]) * lines * (-(-shape[-1] // 128) * 128) * size


def kernel(body, outs, scratch, ids, *arrays, us=1.0, work=2, after=(), far=False):
    count, late = len(arrays), len(after)

    def run(*refs):
        body(*refs[: 1 + count], *refs[1 + count + late :])

    vmem = pl.BlockSpec(memory_space=pltpu.VMEM)
    total = sum(padded(a.shape, a.dtype) for a in arrays) + sum(padded(*o) for o in [*outs, *scratch])
    result = pl.pallas_call(
        run,
        name=body.__name__,
        out_shape=tuple(jax.ShapeDtypeStruct(shape, kind) for shape, kind in outs),
        in_specs=[pl.BlockSpec(memory_space=pltpu.SMEM)] + [vmem] * count + [pl.BlockSpec(memory_space=pl.ANY)] * late,
        out_specs=tuple(vmem for _ in outs),
        scratch_shapes=[pltpu.VMEM(shape, kind) for shape, kind in scratch],
        compiler_params=pltpu.CompilerParams(vmem_limit_bytes=60 * MIB if far else int(total * 1.02) + work * MIB),
        cost_estimate=pl.CostEstimate(flops=int(us * 5e9), bytes_accessed=int(us * 1e5), transcendentals=0),
    )(ids, *arrays, *after)
    return result if len(outs) > 1 else result[0]


def swap_core(value):
    return lax.ppermute(value, "c", [(0, 1), (1, 0)])


def from_peer(value, step):
    return lax.ppermute(value, "gx", [(i, i ^ step) for i in range(4)])


def from_below(value, step):
    return lax.ppermute(value, "gy", [(i, (i + step) % 4) for i in range(4)])


def gather_plane(own):
    near = [own] + [from_peer(own, k) for k in range(1, 4)]
    return near + [swap_core(piece) for piece in near]


def position(c, g, z):
    return (c * 4 + g) * 4 + z


def token_moves():
    moves = []
    for m in range(4):
        move = []
        for c in range(2):
            for g in range(4):
                for z in range(4):
                    t, mb = (m ^ g) >> 1, (m ^ g) & 1
                    move.append((position(c, g, z), position(z // 2, 2 * (z % 2) + t, 2 * mb + c)))
        moves.append(move)
    return moves


MOVES = token_moves()
BACK = [[(b, a) for a, b in move] for move in MOVES]


def run_table(width, cols):
    table = np.zeros((8, 4, 3), np.int32)
    for d in range(8):
        filled = 0
        for z in range(4):
            for t in range(3):
                low = max(width * t + PAIR * d, cols * z)
                high = min(width * t + PAIR * (d + 1), cols * (z + 1))
                if high > low:
                    table[d, z] = (low - cols * z, high - low, filled)
                    filled += high - low
            if table[d, z, 1] == 0:
                table[d, z, 2] = filled
    return table.reshape(-1)


def aligned(value, step):
    return pl.multiple_of(value, step)


def normed(rows):
    average = jnp.mean(rows, axis=1, keepdims=True)
    centered = rows - average
    inverse = lax.rsqrt(jnp.mean(centered * centered, axis=1, keepdims=True) + EPSILON)
    return centered * inverse, inverse


def norm_pull(upstream, centered, inverse, gain):
    scaled = upstream * gain
    return inverse * (
        scaled
        - jnp.mean(scaled, axis=1, keepdims=True)
        - centered * jnp.mean(scaled * centered, axis=1, keepdims=True)
    )


def column_sum(rows):
    return jnp.sum(rows, axis=0, keepdims=True)


def place(ids):
    return ids[0], ids[1], ids[2], ids[3]


def run_of(ids, d, z):
    at = 4 + d * 12 + z * 3
    return ids[at], ids[at + 1], ids[at + 2]


def lanes_of(half, rows):
    return pl.ds(aligned(half * rows, rows), rows)


def send_tokens(ids, x, g_in, *outs):
    g = ids[1]
    for m in range(4):
        v = m ^ g
        for t, src in enumerate((x, g_in)):
            outs[m][t] = src[v & 1, :, lanes_of(v >> 1, outs[m].shape[2])]


def own_rows(ids, blocks, held, which):
    e = 2 * (ids[1] & 1) + (ids[2] >> 1)
    for m in range(4):
        held[m ^ e] = blocks[m][which]
    return held[...].astype(F32).reshape(-1, held.shape[2]).T


def take_tokens(ids, b0, b1, b2, b3, out, held):
    out[...] = own_rows(ids, (b0, b1, b2, b3), held, 1).astype(BF)


def take_normed(ids, b0, b1, b2, b3, vectors, out, low, held):
    rows = own_rows(ids, (b0, b1, b2, b3), held, 0)
    out[...] = rows.astype(BF)
    low[...] = (normed(rows)[0] * vectors[0:1] + vectors[1:2]).astype(BF)


def land_tokens(ids, b0, b1, b2, b3, first, second):
    g = ids[1]
    for m, block in enumerate((b0, b1, b2, b3)):
        v = m ^ g
        for t, out in enumerate((first, second)):
            out[v & 1, :, lanes_of(v >> 1, block.shape[2])] = block[t]


def qkv_windows(ids, w, o0, o1, o2, o3, tall):
    c, g, z, d = place(ids)
    rows = w.shape[1]
    tall[:rows] = w[...].astype(F32).T
    tall[rows:] = jnp.zeros((tall.shape[0] - rows, tall.shape[1]), F32)
    for k, ref in enumerate((o0, o1, o2, o3)):
        start, _, _ = run_of(ids, c * 4 + (g ^ k), z)
        ref[...] = tall[pl.ds(aligned(start, 16), WINDOW)].astype(BF)


def join_lanes(ids, b0, b1, b2, b3, piece, out, held):
    g = ids[1]
    for k, block in enumerate((b0, b1, b2, b3)):
        held[g ^ k] = block[...]
    part = held.shape[2]
    lines = piece.shape[0] // 4
    for i in range(4):
        at = slice(i * part, (i + 1) * part)
        out[:WINDOW, at] = held[i]
        out[WINDOW:, at] = piece[i * lines : (i + 1) * lines]


def qkv_assemble(ids, b0, b1, b2, b3, out, row, held, tall):
    c, g, z, d = place(ids)
    for s, block in enumerate((b0, b1, b2, b3)):
        held[(z + 4 - s) & 3] = block[...]
    for i in range(4):
        _, _, filled = run_of(ids, d, i)
        tall[pl.ds(aligned(filled, 16), WINDOW)] = held[i, :WINDOW]
    out[...] = tall[: out.shape[0]]
    part = out.shape[1] // 4
    lines = held.shape[1] - WINDOW
    shared = []
    for i in range(4):
        for j in range(3):
            piece = held[i, WINDOW:, j * part : (j + 1) * part]
            row[j * lines : (j + 1) * lines, i * part : (i + 1) * part] = piece
        if i:
            piece = held[i, WINDOW:, 3 * part :].astype(F32)
            shared.append(jnp.concatenate([piece[8 * k : 8 * k + 8] for k in range(4)], 1))
    shared.append(jnp.zeros_like(shared[0]))
    row[TALL:] = jnp.concatenate(shared, 0).astype(BF)


def mlp_blocks(ids, up, down, bias, o0, o1, o2, o3, own_bias, held):
    c, g, z, d = place(ids)
    for t, w in enumerate((up, down)):
        held[t] = w[...].astype(F32).T.reshape(held.shape[1:])
    for k, ref in enumerate((o0, o1, o2, o3)):
        to = c * 4 + (g ^ k)
        ref[0] = held[0, to].astype(BF)
        ref[1] = held[1, to].astype(BF)
    own_bias[...] = jnp.concatenate([bias[i, pl.ds(d, 1)] for i in range(4)], 1)


def mlp_join(ids, b0, b1, b2, b3, up, down, held):
    g = ids[1]
    for k, block in enumerate((b0, b1, b2, b3)):
        held[g ^ k] = block[...]
    part = held.shape[3]
    for i in range(4):
        up[:, i * part : (i + 1) * part] = held[i, 0]
        down[:, i * part : (i + 1) * part] = held[i, 1]


def out_half(ids, w, wq, out, tall):
    c, _, z, _ = place(ids)
    tall[: w.shape[1]] = w[...].astype(F32).T
    out[:TALL] = tall[pl.ds(aligned(c * WINDOW, 8), TALL)].astype(BF)
    tall[: wq.shape[1]] = wq[...].astype(F32).T
    at = jnp.maximum(272 * z - HEAD_DIM, 0) + c * (HEAD_DIM // 2)
    shared = tall[pl.ds(aligned(at, 8), HEAD_DIM // 2)]
    out[TALL:] = jnp.concatenate([shared, jnp.zeros((16, shared.shape[1]), F32)], 0).astype(BF)


def out_whole(ids, *refs):
    pieces, out, w16, held = refs[:8], refs[8], refs[9], refs[10]
    d = ids[3]
    part = held.shape[5]
    for r in range(8):
        owner = r ^ d
        core, quarter = owner >> 2, owner & 3
        out[pl.ds(aligned(272 * quarter + WINDOW * core, 16), TALL)] = pieces[r][:TALL]
        shared = pieces[r][TALL:].astype(F32)
        for t in range(3):
            for i in range(4):
                held[quarter, t, core, i] = shared[8 * t : 8 * t + 8, i * part : (i + 1) * part]
    for q in range(4):
        w16[:, q * part : (q + 1) * part] = held[q].reshape(3 * HEAD_DIM, part).astype(BF)


def lane_head(shape):
    return lax.broadcasted_iota(jnp.int32, shape, len(shape) - 1) < HEAD_DIM


def only_head(value, head):
    low = lane_head(value.shape)
    zero = jnp.zeros_like(value)
    return jnp.where(low, value, zero) if head == 0 else jnp.where(low, zero, value)


def softmax_down(scores, allowed):
    masked = jnp.where(allowed, scores, BLOCKED)
    weights = jnp.exp(masked - jnp.max(masked, axis=0, keepdims=True))
    return (weights * (1.0 / jnp.sum(weights, axis=0, keepdims=True))).astype(BF)


def causal_mask(shape, first):
    return lax.broadcasted_iota(jnp.int32, shape, 0) <= lax.broadcasted_iota(jnp.int32, shape, 1) + first


def segments_of(ids, mine, theirs):
    c, _, z, _ = place(ids)
    second = (z >> 1) == 1
    near = jnp.where(second, mine[1:2], mine[0:1])
    far = jnp.where(second, theirs[1:2], theirs[0:1])
    return jnp.where((z & 1) == c, near, far).astype(F32)


def upright(seg_row):
    return jnp.broadcast_to(seg_row, (8, seg_row.shape[1])).T[:, :1]


def attend(ids, *refs):
    n, refs = refs[:8], refs[8:]
    w, vectors, mine, theirs, n_abs, q_out, k_out, v_out, probs, att_abs = refs
    d = ids[3]
    rows = n_abs.shape[1]
    seq = 8 * rows
    for r in range(8):
        n_abs[r ^ d] = n[r][...]
    tokens = n_abs[...].reshape(seq, n_abs.shape[2])
    pair = aligned(d * PAIR, PAIR)
    projected = dot(tokens, w[...], ((1,), (1,)))
    q = (projected[:, :PAIR] + vectors[6:7, pl.ds(pair, PAIR)]).astype(BF) * BF(HEAD_DIM**-0.5)
    k = projected[:, PAIR : 2 * PAIR].astype(BF)
    v = (projected[:, 2 * PAIR :] + vectors[7:8, pl.ds(pair, PAIR)]).astype(BF)
    q_out[...] = q
    k_out[...] = k
    v_out[...] = v
    seg_row = segments_of(ids, mine, theirs)
    seg_col = upright(seg_row)
    v_t = v.astype(F32).T.astype(BF)
    keys = [only_head(k, h) for h in range(2)]
    step = 2 * rows
    for b in range(4):
        seen = (b + 1) * step
        at = slice(b * step, seen)
        allowed = (seg_col[:seen] == seg_row[:, at]) & causal_mask((seen, step), b * step)
        turned = []
        for h in range(2):
            p = softmax_down(dot(keys[h][:seen], q[at], ((1,), (1,))), allowed)
            probs[h, :seen, at] = p
            turned.append(dot(v_t[h * HEAD_DIM : (h + 1) * HEAD_DIM, :seen], p, ((1,), (0,))))
        attended = jnp.concatenate(turned, 0).T.astype(BF)
        att_abs[2 * b] = attended[:rows]
        att_abs[2 * b + 1] = attended[rows:]


def attend_shared(ids, n_abs, n_own, w16, vectors, mine, theirs, kv_out, qs_out, probs_s, att_s, seg_row):
    d = ids[3]
    rows, width = n_abs.shape[1], n_abs.shape[2]
    seq = 8 * rows
    w16_rows = w16[...]
    nothing = jnp.zeros((1, HEAD_DIM), F32)
    shared_v = jnp.concatenate([nothing, vectors[7:8, 8 * PAIR :]], 1)
    shared_q = vectors[6:7, 8 * PAIR :]
    kv = (dot(n_abs[...].reshape(seq, width), w16_rows[HEAD_DIM:], ((1,), (1,))) + shared_v).astype(BF)
    qs = (dot(n_own[...], w16_rows[:HEAD_DIM], ((1,), (1,))) + shared_q).astype(BF) * BF(HEAD_DIM**-0.5)
    qs = jnp.concatenate([qs, jnp.zeros_like(qs)], 1)
    kv_out[...] = kv
    qs_out[...] = qs
    first = aligned(d * rows, rows)
    seg_row[...] = segments_of(ids, mine, theirs)
    allowed = (upright(seg_row[...]) == seg_row[:, pl.ds(first, rows)]) & causal_mask((seq, rows), first)
    p = softmax_down(dot(only_head(kv, 0), qs, ((1,), (1,))), allowed)
    probs_s[...] = p
    kv_t = kv.astype(F32).T.astype(BF)
    att_s[...] = dot(kv_t[HEAD_DIM:], p, ((1,), (0,))).T.astype(BF)


def out_norm(ids, got, att_s, wo, x_own, vectors, middle, low):
    attended = jnp.concatenate([got[a] for a in range(8)] + [att_s[...]], 1)
    rows = x_own[...].astype(F32) + (dot(attended, wo[...], ((1,), (1,))) + vectors[4:5])
    middle[...] = rows
    low[...] = (normed(rows)[0] * vectors[2:3] + vectors[3:4]).astype(BF)


def weighted(sums, w):
    high = sums.astype(BF)
    low = (sums - high.astype(F32)).astype(BF)
    return dot(high, w, ((1,), (0,))) + dot(low, w, ((1,), (0,)))


def attend_back(ids, g_in, gs_in, q_in, k_in, v_in, kv_in, qs_in, probs, probs_s, w, w16, n_abs, *refs):
    grad_kv, grad_qs, sums, moments, near = refs[:5]
    far, windows, grads, grads_rel, tall = refs[5:9], refs[9:13], *refs[13:]
    d = ids[3]
    rows = g_in.shape[1]
    seq = 8 * rows
    g_all = g_in[...].reshape(seq, PAIR)
    g_s = gs_in[...]
    q, k, v, kv, qs = q_in[...], k_in[...], v_in[...], kv_in[...], qs_in[...]
    scale = HEAD_DIM**-0.5
    k_t = k.astype(F32).T.astype(BF)
    values = [only_head(v, h) for h in range(2)]
    step = 2 * rows
    grad_q = []
    grad_k = [[jnp.zeros((step, PAIR), F32) for _ in range(4)] for _ in range(2)]
    grad_v = [[jnp.zeros((step, PAIR), F32) for _ in range(4)] for _ in range(2)]
    for b in range(4):
        seen = (b + 1) * step
        at = slice(b * step, seen)
        turned = []
        for h in range(2):
            p_low = probs[h, :seen, at]
            p = p_low.astype(F32)
            gp = dot(values[h][:seen], g_all[at], ((1,), (1,)))
            inner = jnp.sum(p * gp, axis=0, keepdims=True)
            gs = (p * (gp - inner)).astype(BF)
            turned.append(dot(k_t[h * HEAD_DIM : (h + 1) * HEAD_DIM, :seen], gs, ((1,), (0,))) * scale)
            dk = dot(gs, q[at], ((1,), (0,)))
            dv = dot(p_low, g_all[at], ((1,), (0,)))
            for i in range(b + 1):
                grad_k[h][i] = grad_k[h][i] + dk[i * step : (i + 1) * step]
                grad_v[h][i] = grad_v[h][i] + dv[i * step : (i + 1) * step]
        grad_q.append(jnp.concatenate(turned, 0).T)
    low = lane_head((step, PAIR))
    qsum = jnp.zeros((1, PAIR), F32)
    ksum = jnp.zeros((1, PAIR), F32)
    vsum = jnp.zeros((1, PAIR), F32)
    for i in range(4):
        dq = grad_q[i].astype(BF)
        dk = jnp.where(low, grad_k[0][i], grad_k[1][i]).astype(BF)
        dv = jnp.where(low, grad_v[0][i], grad_v[1][i]).astype(BF)
        qsum = qsum + column_sum(dq.astype(F32))
        ksum = ksum + column_sum(dk.astype(F32))
        vsum = vsum + column_sum(dv.astype(F32))
        for j in range(2):
            part = slice(j * rows, (j + 1) * rows)
            grads[2 * i + j, :, :PAIR] = dq[part]
            grads[2 * i + j, :, PAIR : 2 * PAIR] = dk[part]
            grads[2 * i + j, :, 2 * PAIR : 3 * PAIR] = dv[part]

    p_low = probs_s[...]
    p = p_low.astype(F32)
    v_s = jnp.concatenate([kv[:, HEAD_DIM:], jnp.zeros((seq, HEAD_DIM), BF)], 1)
    g_pad = jnp.concatenate([g_s, jnp.zeros((rows, HEAD_DIM), BF)], 1)
    gp = dot(v_s, g_pad, ((1,), (1,)))
    inner = jnp.sum(p * gp, axis=0, keepdims=True)
    gs = (p * (gp - inner)).astype(BF)
    kv_t = kv.astype(F32).T.astype(BF)
    dq = (dot(kv_t[:HEAD_DIM], gs, ((1,), (0,))) * scale).T.astype(BF)
    grad_qs[...] = dq
    dk = dot(gs, qs, ((1,), (0,)))[:, :HEAD_DIM]
    dv = dot(p_low, g_pad, ((1,), (0,)))[:, :HEAD_DIM]
    dkv = jnp.concatenate([dk, dv], 1).astype(BF)
    for r in range(8):
        grads[r, :, 3 * PAIR :] = dkv[r * rows : (r + 1) * rows]
    last = jnp.concatenate([column_sum(dq.astype(F32)), column_sum(dv.astype(BF).astype(F32))], 1)
    sums[...] = jnp.concatenate([qsum, vsum, last, jnp.zeros((5, PAIR), F32)], 0)

    grad_kv[...] = dkv
    joined = jnp.concatenate([w[...], w16[HEAD_DIM:]], 0)
    for r in range(8):
        grads_rel[r] = grads[r ^ d]
    out = dot(grads_rel[4:].reshape(4 * rows, 4 * PAIR), joined, ((1,), (0,)))
    for k, ref in enumerate(far):
        ref[...] = out[k * rows : (k + 1) * rows].astype(BF)

    width = n_abs.shape[2]
    tokens = n_abs[...].reshape(seq, width)
    pairs = dot(grads[:, :, : 3 * PAIR].reshape(seq, 3 * PAIR), tokens, ((0,), (0,)))
    tall[: 3 * PAIR] = pairs
    tall[3 * PAIR :] = jnp.zeros((WINDOW, width), F32)
    z = ids[2]
    line = lax.broadcasted_iota(jnp.int32, (WINDOW, width), 0)
    for s, ref in enumerate(windows):
        _, length, filled = run_of(ids, d, (z + s) & 3)
        window = tall[pl.ds(aligned(filled, 16), WINDOW)]
        ref[...] = jnp.where(line < length, window, 0.0).astype(BF)
    pair_sums = jnp.concatenate([qsum, ksum, vsum], 1)
    moments[...] = jnp.concatenate(
        [column_sum(pairs * w[...].astype(F32)), weighted(jnp.broadcast_to(pair_sums, (8, 3 * PAIR)), w[...])[:1]], 0
    )

    out = dot(grads_rel[:4].reshape(4 * rows, 4 * PAIR), joined, ((1,), (0,)))
    near[...] = out.astype(BF)
    near[:rows] = (out[:rows] + dot(dq, w16[:HEAD_DIM], ((1,), (0,)))).astype(BF)


def out_grads(ids, *refs):
    gb, att_abs, att_s, grad_kv, grad_qs, n_abs, n_own, w16, out, moments, gb_abs = refs[:8], *refs[8:]
    d = ids[3]
    rows, width = gb_abs.shape[1], gb_abs.shape[2]
    seq = 8 * rows
    for r in range(8):
        gb_abs[r ^ d] = gb[r][...]
    pair = dot(att_abs[...].reshape(seq, PAIR), gb_abs[...].reshape(seq, width), ((0,), (0,)))
    shared = dot(att_s[...], gb[0][...], ((0,), (0,)))
    q_part = dot(grad_qs[...], n_own[...], ((0,), (0,)))
    kv_part = dot(grad_kv[...], n_abs[...].reshape(seq, width), ((0,), (0,)))
    projections = jnp.concatenate([q_part, kv_part], 0)
    sums = jnp.concatenate([column_sum(grad_qs[...].astype(F32)), column_sum(grad_kv[...].astype(F32))], 1)
    moments[...] = jnp.concatenate(
        [
            column_sum(projections * w16[...].astype(F32)),
            weighted(jnp.broadcast_to(sums, (8, 3 * HEAD_DIM)), w16[...])[:1],
        ],
        0,
    )
    tall = jnp.concatenate([pair, shared, projections], 0).T
    part = out.shape[1]
    for core in range(2):
        for quarter in range(4):
            at = slice((2 * quarter + core) * part, (2 * quarter + core + 1) * part)
            out[core * 4 + quarter] = tall[at].astype(BF)


def add_far(ids, near, f0, f1, f2, f3, s0, s1, s2, s3):
    rows = s0.shape[0]
    for k, (far, ref) in enumerate(((f0, s0), (f1, s1), (f2, s2), (f3, s3))):
        ref[...] = (near[k * rows : (k + 1) * rows].astype(F32) + far[...].astype(F32)).astype(ref.dtype)


def total_of(s0, r1, r2, r3):
    return s0[...] + r1[...].astype(F32) + r2[...].astype(F32) + r3[...].astype(F32)


def middle_back(ids, s0, r1, r2, r3, middle, g_own, wo, vectors, grad_middle, low, sums, back, back_s):
    upstream = total_of(s0, r1, r2, r3)
    centered, inverse = normed(middle[...])
    g = g_own[...].astype(F32)
    grad = g + norm_pull(upstream, centered, inverse, vectors[2:3])
    grad_middle[...] = grad
    rounded = grad.astype(BF)
    low[...] = rounded
    attended = dot(rounded, wo[...], ((1,), (0,))).astype(BF)
    for a in range(8):
        back[a] = attended[:, a * PAIR : (a + 1) * PAIR]
    back_s[...] = attended[:, 8 * PAIR :]
    sums[...] = jnp.concatenate(
        [
            column_sum(rounded.astype(F32)),
            column_sum(upstream * centered),
            column_sum(upstream),
            column_sum(g),
        ],
        0,
    )


def split_features(ids, rows, held, outs, which):
    e = 2 * (ids[1] & 1) + (ids[2] >> 1)
    held[...] = rows.T.reshape(held.shape).astype(BF)
    for m in range(4):
        outs[m][which] = held[m ^ e]


def finish(ids, s0, r1, r2, r3, t0, u1, u2, u3, middle, grad_middle, x_own, vectors, *refs):
    outs, held = refs[:4], refs[4]
    rows = middle[...] + (total_of(t0, u1, u2, u3) + vectors[5:6])
    split_features(ids, rows, held, outs, 0)
    upstream = total_of(s0, r1, r2, r3)
    centered, inverse = normed(x_own[...].astype(F32))
    rows = grad_middle[...] + norm_pull(upstream, centered, inverse, vectors[0:1])
    split_features(ids, rows, held, outs, 1)


def grad_activated(ids, *refs):
    g, down, g_rel, out = refs[:8], refs[8], refs[9], refs[10]
    rows = g_rel.shape[1]
    for r in range(8):
        g_rel[r] = g[r][...]
    for b in range(4):
        block = g_rel[2 * b : 2 * b + 2].reshape(2 * rows, g_rel.shape[2])
        out[b * 2 * rows : (b + 1) * 2 * rows] = dot(block, down[...], ((1,), (1,)))


def feed_forward(ids, *refs):
    n, refs = refs[:8], refs[8:]
    up, grad_act, bias, n_rel, act, grad_pre, bias_sum = refs[:7]
    far, near = refs[7:11], refs[11]
    rows = n_rel.shape[1]
    for r in range(8):
        n_rel[r] = n[r][...]
    total = jnp.zeros(bias_sum.shape, F32)
    for b in (2, 3, 0, 1):
        at = slice(b * 2 * rows, (b + 1) * 2 * rows)
        block = n_rel[2 * b : 2 * b + 2].reshape(2 * rows, n_rel.shape[2])
        pre = dot(block, up[...], ((1,), (1,))) + bias[...]
        square = pre * pre
        bent = jnp.tanh(ROOT * pre * (1.0 + 0.044715 * square))
        half = 0.5 * (1.0 + bent)
        act[at] = (pre * half).astype(BF)
        slope = half + 0.5 * pre * (1.0 - bent * bent) * (ROOT + ROOT * 3.0 * 0.044715 * square)
        low = (grad_act[at] * slope).astype(BF)
        grad_pre[at] = low
        total = total + column_sum(low.astype(F32))
        out = dot(low, up[...], ((1,), (0,))).astype(BF)
        if b >= 2:
            far[2 * b - 4][...] = out[:rows]
            far[2 * b - 3][...] = out[rows:]
        else:
            near[2 * rows * b : 2 * rows * (b + 1)] = out
    bias_sum[...] = total


def feed_out(ids, act, down, *refs):
    far, near = refs[:4], refs[4]
    half = near.shape[0]
    out = dot(act[half:], down[...], ((1,), (0,))).astype(BF)
    rows = half // 4
    for k, ref in enumerate(far):
        ref[...] = out[k * rows : (k + 1) * rows]
    near[...] = dot(act[:half], down[...], ((1,), (0,))).astype(BF)


def mlp_grads(ids, act, grad_pre, n_rel, g_rel, out):
    rows, width = n_rel.shape[1], n_rel.shape[2]
    part = out.shape[2]
    up = dot(grad_pre[...], n_rel[...].reshape(8 * rows, width), ((0,), (0,)))
    for i in range(4):
        out[i, 0] = up[i * part : (i + 1) * part].astype(BF)
    down = dot(act[...], g_rel[...].reshape(8 * rows, width), ((0,), (0,)))
    for i in range(4):
        out[i, 1] = down[i * part : (i + 1) * part].astype(BF)


def mlp_lanes(ids, summed, o0, o1, o2, o3, held):
    g = ids[1]
    part = held.shape[3]
    for i in range(4):
        held[i] = summed[:, :, i * part : (i + 1) * part]
    for k, ref in enumerate((o0, o1, o2, o3)):
        ref[...] = held[g ^ k]


def mlp_land(ids, *refs):
    blocks, up, down, held = refs[:8], refs[8], refs[9], refs[10]
    d = ids[3]
    for r in range(8):
        held[r ^ d] = blocks[r][...].astype(F32)
    up[...] = held[:, 0].reshape(-1, held.shape[3]).T
    down[...] = held[:, 1].reshape(-1, held.shape[3]).T


def qkv_lanes(ids, b0, b1, b2, b3, o0, o1, o2, o3, held):
    g = ids[1]
    part = held.shape[2]
    window = sum(ref[...].astype(F32) for ref in (b0, b1, b2, b3))
    for i in range(4):
        held[i] = window[:, i * part : (i + 1) * part].astype(BF)
    for k, ref in enumerate((o0, o1, o2, o3)):
        ref[...] = held[g ^ k]


def qkv_land(ids, *refs):
    blocks, mine, theirs, out, tall, held = refs[:8], *refs[8:]
    c, g, z, d = place(ids)
    tall[...] = jnp.zeros(tall.shape, F32)
    for r in range(8):
        start, _, _ = run_of(ids, r ^ d, z)
        at = pl.ds(aligned(start, 16), WINDOW)
        tall[at] = tall[at] + blocks[r][...].astype(F32)
    held[c] = mine[:, 272:].astype(F32)
    held[1 - c] = theirs[:, 272:].astype(F32)
    shared = held[...].reshape(-1, HEAD_DIM).T
    keep = jnp.where(z > 0, 1.0, 0.0)
    at = pl.ds(aligned(jnp.maximum(272 * z - HEAD_DIM, 0), 8), HEAD_DIM)
    tall[at] = tall[at] + shared * keep
    out[...] = tall[: out.shape[1]].T


def out_split(ids, got, o0, o1, o2, o3, wide, held):
    z = ids[2]
    part = wide.shape[1] // 4
    shared = jnp.zeros((got.shape[1], 4 * HEAD_DIM), F32)
    for a in range(8):
        wide[:, a * PAIR : (a + 1) * PAIR] = got[a, :, :PAIR].astype(F32)
        shared = shared + got[a, :, PAIR:].astype(F32)
    wide[:, 8 * PAIR :] = shared[:, :HEAD_DIM]
    for i in range(4):
        at = max(i, 1) * HEAD_DIM
        held[i] = jnp.concatenate(
            [wide[:, i * part : (i + 1) * part], shared[:, at : at + HEAD_DIM]], 1
        ).astype(BF)
    for s, ref in enumerate((o0, o1, o2, o3)):
        ref[...] = held[(z + s) & 3]


def sum_four(ids, b0, b1, b2, b3, out):
    out[...] = sum(ref[...].astype(F32) for ref in (b0, b1, b2, b3)).astype(BF)


def out_land(ids, mine, theirs, out, held):
    c = ids[0]
    held[c] = mine[:, :272].astype(F32)
    held[1 - c] = theirs[:, :272].astype(F32)
    out[...] = held[...].reshape(-1, held.shape[2]).T


def join_sums(ids, first, second, qkv, middle, up, out):
    d = ids[3]
    out[:2] = first[...] + second[...]
    out[2:4] = jnp.zeros((2, out.shape[1]), F32)
    at = pl.ds(aligned(d * PAIR, PAIR), PAIR)
    out[2:3, at] = qkv[0:1]
    out[3:4, at] = qkv[1:2]
    out[2:3, 8 * PAIR :] = qkv[2:3, :HEAD_DIM]
    out[3:4, 8 * PAIR :] = qkv[2:3, HEAD_DIM:]
    out[4:8] = middle[...]
    part = up.shape[1] // 4
    for i in range(4):
        piece = up[:, i * part : (i + 1) * part]
        out[8 + i : 9 + i] = jnp.concatenate([jnp.where(d == a, piece, 0.0) for a in range(8)], 1)


def keep(ids, *refs):
    count = len(refs) // 2
    for source, target in zip(refs[:count], refs[count:], strict=True):
        target[...] = source[...]


def add_two(ids, a, b, out):
    out[...] = a[...] + b[...]


def split_sums(ids, a, b, vectors, out):
    total = a[...] + b[...]
    out[...] = total
    out[0:1] = (total[0:1] - vectors[1:2] * total[1:2]) / vectors[0:1]


def shards(
    hidden_in,
    segment_ids,
    cotangent,
    norm1_gain,
    norm1_shift,
    w_qkv,
    q_bias,
    v_bias,
    w_out,
    out_bias,
    norm2_gain,
    norm2_shift,
    w_up,
    up_bias,
    w_down,
    down_bias,
):
    c = lax.axis_index("c")
    g = lax.axis_index("gx")
    z = lax.axis_index("gy")
    d = c * 4 + g
    width = norm1_gain.shape[0]
    hidden = up_bias.shape[0]
    quarter = hidden_in.shape[2]
    half = quarter // 2
    part = hidden // 32
    own_hidden = hidden // 8
    cols = w_qkv.shape[1]
    seq = segment_ids.shape[1]
    rows = seq // 8
    outer = lax.axis_size("do") > 1
    ids = jnp.concatenate(
        [jnp.stack([c, g, z, d]).astype(jnp.int32), jnp.asarray(run_table(width, cols))]
    )
    vectors = jnp.stack(
        [norm1_gain, norm1_shift, norm2_gain, norm2_shift, out_bias, down_bias, q_bias, v_bias]
    ).astype(F32)

    def row(vector):
        return vector.reshape(1, -1)

    def over_outer(value):
        return lax.psum(value, "do") if outer else value

    block = ((2, quarter, rows), BF)
    own_bf, own_f32 = ((rows, width), BF), ((rows, width), F32)
    held_tokens = ((4, quarter, rows), BF)

    def peers(blocks):
        return [blocks[0]] + [from_peer(blocks[k], k) for k in range(1, 4)]

    def gather_near(own):
        return [own] + [from_peer(own, k) for k in range(1, 4)]

    def gather_later(near, after):
        held = kernel(keep, [(a.shape, a.dtype) for a in near], [], ids, *near, us=0.8, after=after)
        return near + [swap_core(piece) for piece in held]

    def shifted(blocks):
        return [blocks[0]] + [from_below(blocks[s], s) for s in range(1, 4)]

    sent = kernel(
        send_tokens, [block] * 4, [], ids, hidden_in.transpose(0, 2, 1), cotangent.transpose(0, 2, 1), us=1.0
    )
    blocks = [lax.ppermute(sent[m], EVERY, MOVES[m]) for m in range(4)]
    window = ((WINDOW, quarter), BF)
    window_wide = ((WINDOW, width), BF)
    windows = peers(
        kernel(
            qkv_windows, [window] * 4, [((cols + WINDOW, quarter), F32)], ids, w_qkv, us=1.5, after=(sent[0],)
        )
    )
    lines = TALL + 3 * 16
    out_piece = kernel(
        out_half, [((lines, quarter), BF)], [((cols, quarter), F32)], ids, w_out, w_qkv, us=1.0, after=(sent[0],)
    )
    x_own, n1_own = kernel(take_normed, [own_bf, own_bf], [held_tokens], ids, *blocks, vectors, us=1.5)
    n1 = gather_plane(n1_own)
    piece = ((WINDOW + lines // 4, width), BF)
    joined = kernel(join_lanes, [piece], [((4, WINDOW, quarter), BF)], ids, *windows, out_piece, us=1.0)
    joined = shifted([joined] * 4)
    *mlp_sent, up_bias_own = kernel(
        mlp_blocks,
        [((2, part, quarter), BF)] * 4 + [((1, own_hidden), F32)],
        [((2, 8, part, quarter), F32)],
        ids,
        w_up,
        w_down.T,
        up_bias.astype(F32).reshape(4, 8, part),
        us=2.0,
        after=(joined[0], n1[1], n1[2], n1[3]),
    )
    mlp_got = peers(mlp_sent)
    g_own = kernel(
        take_tokens, [own_bf], [held_tokens], ids, *blocks, us=1.0, after=(n1[1], n1[2], n1[3])
    )
    g_near = gather_near(g_own)
    w_own, out_row = kernel(
        qkv_assemble,
        [((3 * PAIR, width), BF), ((TALL + 32, width), BF)],
        [((4, *piece[0]), BF), ((3 * PAIR + WINDOW, width), BF)],
        ids,
        *joined,
        us=1.0,
        after=(*g_near[1:], *mlp_got[1:]),
    )
    up_part, down_part = kernel(
        mlp_join,
        [((part, width), BF)] * 2,
        [((4, 2, part, quarter), BF)],
        ids,
        *mlp_got,
        us=1.0,
        after=(w_own,),
    )
    up_own = lax.all_gather(up_part, "gy", axis=0, tiled=False).reshape(own_hidden, width)
    down_own = lax.all_gather(down_part, "gy", axis=0, tiled=False).reshape(own_hidden, width)
    swapped_ids = swap_core(segment_ids)

    half_rows = ((4 * rows, width), BF)
    all_bf = ((8, rows, width), BF)
    heads_bf = ((8, rows, PAIR), BF)
    pair_seq = ((seq, PAIR), BF)
    n_abs, q, k, v, probs, att = kernel(
        attend,
        [all_bf, pair_seq, pair_seq, pair_seq, ((2, seq, seq), BF), heads_bf],
        [],
        ids,
        *n1,
        w_own,
        vectors,
        segment_ids,
        swapped_ids,
        us=11.0,
        far=True,
    )
    out_rows = gather_later(gather_near(out_row), (att,))
    att_got = lax.all_to_all(att, PLANE, split_axis=0, concat_axis=0, tiled=True)
    wo, w16 = kernel(
        out_whole,
        [((width, width), BF), ((3 * HEAD_DIM, width), BF)],
        [((4, 3, 2, 4, 8, quarter), F32)],
        ids,
        *out_rows,
        us=1.0,
        after=(att_got,),
    )
    kv, qs, probs_s, att_s = kernel(
        attend_shared,
        [pair_seq, ((rows, PAIR), BF), ((seq, rows), BF), ((rows, HEAD_DIM), BF)],
        [((1, seq), F32)],
        ids,
        n_abs,
        n1_own,
        w16,
        vectors,
        segment_ids,
        swapped_ids,
        us=2.0,
        work=6,
    )
    middle, n2_own = kernel(
        out_norm, [own_f32, own_bf], [], ids, att_got, att_s, wo, x_own, vectors, us=2.0, work=6
    )
    g_all = gather_later(g_near, (n2_own,))
    summed = [own_f32, own_bf, own_bf, own_bf]

    def scatter(near, far, after=()):
        return peers(
            kernel(add_far, summed, [], ids, near, *[swap_core(f) for f in far], us=1.2, after=after)
        )

    n2 = gather_plane(n2_own)

    g_rel, grad_act = kernel(
        grad_activated, [all_bf, ((seq, own_hidden), F32)], [], ids, *g_all, down_own, us=3.0, after=(n2_own, up_own)
    )
    n_rel, act, grad_pre, up_sum, *far, near = kernel(
        feed_forward,
        [
            all_bf,
            ((seq, own_hidden), BF),
            ((seq, own_hidden), BF),
            ((1, own_hidden), F32),
            *[own_bf] * 4,
            half_rows,
        ],
        [],
        ids,
        *n2,
        up_own,
        grad_act,
        up_bias_own,
        us=7.0,
        work=8,
    )
    parts = scatter(near, far)
    mlp_partial = kernel(
        mlp_grads,
        [((4, 2, part, width), BF)],
        [],
        ids,
        act,
        grad_pre,
        n_rel,
        g_rel,
        us=5.0,
        work=8,
        after=(parts[0],),
    )
    *feed_far, feed_near = kernel(
        feed_out, [own_bf] * 4 + [half_rows], [], ids, act, down_own, us=2.5, work=4, after=(mlp_partial,)
    )
    mlp_summed = over_outer(lax.psum_scatter(mlp_partial, "gy", scatter_dimension=0, tiled=False))
    grad_middle, gb_own, middle_sums, back, back_s = kernel(
        middle_back,
        [own_f32, own_bf, ((4, width), F32), heads_bf, ((rows, HEAD_DIM), BF)],
        [],
        ids,
        *parts,
        middle,
        g_own,
        wo,
        vectors,
        us=2.5,
        work=6,
        after=(mlp_partial,),
    )
    back = lax.all_to_all(back, PLANE, split_axis=0, concat_axis=0, tiled=True)
    gb = gather_plane(gb_own)

    feed_parts = scatter(feed_near, feed_far, (back,))

    grad_kv, grad_qs, qkv_sums, moments, near, *rest = kernel(
        attend_back,
        [pair_seq, ((rows, HEAD_DIM), BF), ((8, PAIR), F32), ((2, width), F32), half_rows]
        + [own_bf] * 4
        + [window_wide] * 4,
        [
            ((8, rows, 4 * PAIR), BF),
            ((8, rows, 4 * PAIR), BF),
            ((3 * PAIR + WINDOW, width), F32),
        ],
        ids,
        back,
        back_s,
        q,
        k,
        v,
        kv,
        qs,
        probs,
        probs_s,
        w_own,
        w16,
        n_abs,
        us=13.0,
        far=True,
        after=(feed_parts[0],),
    )
    far = rest[:4]
    windows = shifted(rest[4:])
    parts = scatter(near, far)
    out_sent, moments_s = kernel(
        out_grads,
        [((8, half, PAIR + 4 * HEAD_DIM), BF), ((2, width), F32)],
        [all_bf],
        ids,
        *gb,
        att,
        att_s,
        grad_kv,
        grad_qs,
        n_abs,
        n1_own,
        w16,
        us=3.5,
        work=10,
        after=tuple(parts[1:]),
    )
    out_got = lax.all_to_all(out_sent, PLANE, split_axis=0, concat_axis=0, tiled=True)
    mlp_parts = kernel(
        mlp_lanes,
        [((2, part, quarter), BF)] * 4,
        [((4, 2, part, quarter), BF)],
        ids,
        mlp_summed,
        us=1.0,
    )
    split_piece = ((half, quarter + HEAD_DIM), BF)
    out_split_parts = shifted(
        kernel(
            out_split,
            [split_piece] * 4,
            [((half, width), F32), ((4, half, quarter + HEAD_DIM), BF)],
            ids,
            out_got,
            us=1.0,
        )
    )
    done = kernel(
        finish,
        [block] * 4,
        [held_tokens],
        ids,
        *parts,
        *feed_parts,
        middle,
        grad_middle,
        x_own,
        vectors,
        us=2.5,
    )
    landed = [lax.ppermute(done[m], EVERY, BACK[m]) for m in range(4)]
    hidden_out, grad_in = kernel(land_tokens, [((2, quarter, 2 * rows), BF)] * 2, [], ids, *landed, us=1.0)

    smalls = kernel(
        join_sums, [((12, width), F32)], [], ids, moments, moments_s, qkv_sums, middle_sums, up_sum, us=0.7
    )
    smalls = smalls + swap_core(smalls)
    smalls = smalls + from_peer(smalls, 1)
    others = from_peer(smalls, 2)
    blocks = peers(mlp_parts)
    lanes = kernel(
        qkv_lanes, [window] * 4, [((4, WINDOW, quarter), BF)], ids, *windows, us=1.0, after=(*landed, *blocks[1:], out_split_parts[0], others)
    )
    near = peers(lanes)
    near = [*near, *[swap_core(piece) for piece in near]]
    total_up, total_down = kernel(
        mlp_land,
        [((quarter, hidden // 4), F32)] * 2,
        [((8, 2, part, quarter), F32)],
        ids,
        *blocks,
        *[swap_core(piece) for piece in blocks],
        us=2.0,
        after=(lanes[0],),
    )
    mine = kernel(sum_four, [split_piece], [], ids, *out_split_parts, us=0.6, after=(lanes[0],))
    theirs = swap_core(mine)
    total_out = kernel(
        out_land, [((quarter, quarter), F32)], [((2, half, quarter), F32)], ids, mine, theirs, us=0.7
    )
    total_out = over_outer(total_out)

    total_qkv = kernel(
        qkv_land,
        [((quarter, cols), F32)],
        [((cols + WINDOW, quarter), F32), ((2, half, HEAD_DIM), F32)],
        ids,
        *near,
        mine,
        theirs,
        us=2.0,
    )
    total_qkv = over_outer(total_qkv)
    smalls = kernel(add_two, [((12, width), F32)], [], ids, smalls, others, us=0.7, after=(lanes[0],))
    smalls = smalls + lax.ppermute(smalls, "gy", [(i, i ^ 1) for i in range(4)])
    others = lax.ppermute(smalls, "gy", [(i, i ^ 2) for i in range(4)])
    smalls, others = over_outer(smalls), over_outer(others)
    smalls = kernel(split_sums, [((12, width), F32)], [], ids, smalls, others, vectors, us=0.7)


    return (
        hidden_out.transpose(0, 2, 1),
        grad_in.transpose(0, 2, 1),
        smalls[0],
        smalls[1],
        total_qkv,
        smalls[2],
        smalls[3],
        total_out,
        smalls[4],
        smalls[5],
        smalls[6],
        total_up,
        smalls[8:12].reshape(hidden),
        total_down.T,
        smalls[7],
    )


def solution(mesh):
    devices = mesh.devices
    split = Mesh(
        devices.reshape(devices.shape[0] // 2, 2, devices.shape[1], devices.shape[2]), ("do", "c", "gx", "gy")
    )
    stream = P(None, ("do", "c", "gy"), "gx")
    flat = P()
    tall = P("gx", "gy")
    wide = P("gy", "gx")
    grads = (flat, flat, tall, flat, flat, wide, flat, flat, flat, tall, flat, wide, flat)
    return jax.shard_map(
        shards,
        mesh=split,
        in_specs=(stream, P(None, ("do", "c")), stream, *grads),
        out_specs=(stream, stream, *grads),
        check_vma=False,
    )
```

```python
import math

import jax
import jax.numpy as jnp
import numpy as np
from jax import lax
from jax.experimental import pallas as pl
from jax.experimental.pallas import tpu as pltpu
from jax.sharding import Mesh
from jax.sharding import PartitionSpec as P

HEAD_DIM = 64
PAIR = 2 * HEAD_DIM
EPSILON = 1e-05
BLOCKED = -1e30
BF = jnp.bfloat16
F32 = jnp.float32
PLANE = ("c", "gx")
EVERY = ("c", "gx", "gy")
ROOT = math.sqrt(2.0 / math.pi)
WINDOW = 128
TALL = WINDOW + 16
MIB = 1024 * 1024


def dot(left, right, dims):
    return lax.dot_general(left, right, (dims, ((), ())), preferred_element_type=F32)


def padded(shape, kind):
    size = jnp.dtype(kind).itemsize
    lines = 1 if len(shape) < 2 else -(-shape[-2] // 16) * 16
    return math.prod(shape[:-2]) * lines * (-(-shape[-1] // 128) * 128) * size


def kernel(body, outs, scratch, ids, *arrays, us=1.0, work=2, after=(), far=False):
    count, late = len(arrays), len(after)

    def run(*refs):
        body(*refs[: 1 + count], *refs[1 + count + late :])

    vmem = pl.BlockSpec(memory_space=pltpu.VMEM)
    total = sum(padded(a.shape, a.dtype) for a in arrays) + sum(padded(*o) for o in [*outs, *scratch])
    result = pl.pallas_call(
        run,
        name=body.__name__,
        out_shape=tuple(jax.ShapeDtypeStruct(shape, kind) for shape, kind in outs),
        in_specs=[pl.BlockSpec(memory_space=pltpu.SMEM)] + [vmem] * count + [pl.BlockSpec(memory_space=pl.ANY)] * late,
        out_specs=tuple(vmem for _ in outs),
        scratch_shapes=[pltpu.VMEM(shape, kind) for shape, kind in scratch],
        compiler_params=pltpu.CompilerParams(vmem_limit_bytes=60 * MIB if far else int(total * 1.02) + work * MIB),
        cost_estimate=pl.CostEstimate(flops=int(us * 5e9), bytes_accessed=int(us * 1e5), transcendentals=0),
    )(ids, *arrays, *after)
    return result if len(outs) > 1 else result[0]


def swap_core(value):
    return lax.ppermute(value, "c", [(0, 1), (1, 0)])


def from_peer(value, step):
    return lax.ppermute(value, "gx", [(i, i ^ step) for i in range(4)])


def from_below(value, step):
    return lax.ppermute(value, "gy", [(i, (i + step) % 4) for i in range(4)])


def gather_plane(own):
    near = [own] + [from_peer(own, k) for k in range(1, 4)]
    return near + [swap_core(piece) for piece in near]


def position(c, g, z):
    return (c * 4 + g) * 4 + z


def token_moves():
    moves = []
    for m in range(4):
        move = []
        for c in range(2):
            for g in range(4):
                for z in range(4):
                    t, mb = (m ^ g) >> 1, (m ^ g) & 1
                    move.append((position(c, g, z), position(z // 2, 2 * (z % 2) + t, 2 * mb + c)))
        moves.append(move)
    return moves


MOVES = token_moves()
BACK = [[(b, a) for a, b in move] for move in MOVES]


def run_table(width, cols):
    table = np.zeros((8, 4, 3), np.int32)
    for d in range(8):
        filled = 0
        for z in range(4):
            for t in range(3):
                low = max(width * t + PAIR * d, cols * z)
                high = min(width * t + PAIR * (d + 1), cols * (z + 1))
                if high > low:
                    table[d, z] = (low - cols * z, high - low, filled)
                    filled += high - low
            if table[d, z, 1] == 0:
                table[d, z, 2] = filled
    return table.reshape(-1)


def aligned(value, step):
    return pl.multiple_of(value, step)


def normed(rows):
    average = jnp.mean(rows, axis=1, keepdims=True)
    centered = rows - average
    inverse = lax.rsqrt(jnp.mean(centered * centered, axis=1, keepdims=True) + EPSILON)
    return centered * inverse, inverse


def norm_pull(upstream, centered, inverse, gain):
    scaled = upstream * gain
    return inverse * (
        scaled
        - jnp.mean(scaled, axis=1, keepdims=True)
        - centered * jnp.mean(scaled * centered, axis=1, keepdims=True)
    )


def column_sum(rows):
    return jnp.sum(rows, axis=0, keepdims=True)


def place(ids):
    return ids[0], ids[1], ids[2], ids[3]


def run_of(ids, d, z):
    at = 4 + d * 12 + z * 3
    return ids[at], ids[at + 1], ids[at + 2]


def lanes_of(half, rows):
    return pl.ds(aligned(half * rows, rows), rows)


def send_tokens(ids, x, g_in, *outs):
    g = ids[1]
    for m in range(4):
        v = m ^ g
        for t, src in enumerate((x, g_in)):
            outs[m][t] = src[v & 1, :, lanes_of(v >> 1, outs[m].shape[2])]


def own_rows(ids, blocks, held, which):
    e = 2 * (ids[1] & 1) + (ids[2] >> 1)
    for m in range(4):
        held[m ^ e] = blocks[m][which]
    return held[...].astype(F32).reshape(-1, held.shape[2]).T


def take_tokens(ids, b0, b1, b2, b3, out, held):
    out[...] = own_rows(ids, (b0, b1, b2, b3), held, 1).astype(BF)


def take_normed(ids, b0, b1, b2, b3, vectors, out, low, held):
    rows = own_rows(ids, (b0, b1, b2, b3), held, 0)
    out[...] = rows.astype(BF)
    low[...] = (normed(rows)[0] * vectors[0:1] + vectors[1:2]).astype(BF)


def land_tokens(ids, b0, b1, b2, b3, first, second):
    g = ids[1]
    for m, block in enumerate((b0, b1, b2, b3)):
        v = m ^ g
        for t, out in enumerate((first, second)):
            out[v & 1, :, lanes_of(v >> 1, block.shape[2])] = block[t]


def qkv_windows(ids, w, o0, o1, o2, o3, tall):
    c, g, z, d = place(ids)
    rows = w.shape[1]
    tall[:rows] = w[...].astype(F32).T
    tall[rows:] = jnp.zeros((tall.shape[0] - rows, tall.shape[1]), F32)
    for k, ref in enumerate((o0, o1, o2, o3)):
        start, _, _ = run_of(ids, c * 4 + (g ^ k), z)
        ref[...] = tall[pl.ds(aligned(start, 16), WINDOW)].astype(BF)


def join_lanes(ids, b0, b1, b2, b3, piece, out, held):
    g = ids[1]
    for k, block in enumerate((b0, b1, b2, b3)):
        held[g ^ k] = block[...]
    part = held.shape[2]
    lines = piece.shape[0] // 4
    for i in range(4):
        at = slice(i * part, (i + 1) * part)
        out[:WINDOW, at] = held[i]
        out[WINDOW:, at] = piece[i * lines : (i + 1) * lines]


def qkv_assemble(ids, b0, b1, b2, b3, out, row, held, tall):
    c, g, z, d = place(ids)
    for s, block in enumerate((b0, b1, b2, b3)):
        held[(z + 4 - s) & 3] = block[...]
    for i in range(4):
        _, _, filled = run_of(ids, d, i)
        tall[pl.ds(aligned(filled, 16), WINDOW)] = held[i, :WINDOW]
    out[...] = tall[: out.shape[0]]
    part = out.shape[1] // 4
    lines = held.shape[1] - WINDOW
    shared = []
    for i in range(4):
        for j in range(3):
            piece = held[i, WINDOW:, j * part : (j + 1) * part]
            row[j * lines : (j + 1) * lines, i * part : (i + 1) * part] = piece
        if i:
            piece = held[i, WINDOW:, 3 * part :].astype(F32)
            shared.append(jnp.concatenate([piece[8 * k : 8 * k + 8] for k in range(4)], 1))
    shared.append(jnp.zeros_like(shared[0]))
    row[TALL:] = jnp.concatenate(shared, 0).astype(BF)


def mlp_blocks(ids, up, down, bias, o0, o1, o2, o3, own_bias, held):
    c, g, z, d = place(ids)
    for t, w in enumerate((up, down)):
        held[t] = w[...].astype(F32).T.reshape(held.shape[1:])
    for k, ref in enumerate((o0, o1, o2, o3)):
        to = c * 4 + (g ^ k)
        ref[0] = held[0, to].astype(BF)
        ref[1] = held[1, to].astype(BF)
    own_bias[...] = jnp.concatenate([bias[i, pl.ds(d, 1)] for i in range(4)], 1)


def mlp_join(ids, b0, b1, b2, b3, out, held):
    g = ids[1]
    for k, block in enumerate((b0, b1, b2, b3)):
        held[g ^ k] = block[...]
    part = held.shape[3]
    for i in range(4):
        out[:, :, i * part : (i + 1) * part] = held[i]


def rows_of(both, which):
    return both[:, which].astype(F32).reshape(-1, both.shape[3]).astype(BF)


def out_half(ids, w, wq, out, tall):
    c, _, z, _ = place(ids)
    tall[: w.shape[1]] = w[...].astype(F32).T
    out[:TALL] = tall[pl.ds(aligned(c * WINDOW, 8), TALL)].astype(BF)
    tall[: wq.shape[1]] = wq[...].astype(F32).T
    at = jnp.maximum(272 * z - HEAD_DIM, 0) + c * (HEAD_DIM // 2)
    shared = tall[pl.ds(aligned(at, 8), HEAD_DIM // 2)]
    out[TALL:] = jnp.concatenate([shared, jnp.zeros((16, shared.shape[1]), F32)], 0).astype(BF)


def out_whole(ids, *refs):
    pieces, out, w16, held = refs[:8], refs[8], refs[9], refs[10]
    d = ids[3]
    part = held.shape[5]
    for r in range(8):
        owner = r ^ d
        core, quarter = owner >> 2, owner & 3
        out[pl.ds(aligned(272 * quarter + WINDOW * core, 16), TALL)] = pieces[r][:TALL]
        shared = pieces[r][TALL:].astype(F32)
        for t in range(3):
            for i in range(4):
                held[quarter, t, core, i] = shared[8 * t : 8 * t + 8, i * part : (i + 1) * part]
    for q in range(4):
        w16[:, q * part : (q + 1) * part] = held[q].reshape(3 * HEAD_DIM, part).astype(BF)


def lane_head(shape):
    return lax.broadcasted_iota(jnp.int32, shape, len(shape) - 1) < HEAD_DIM


def only_head(value, head):
    low = lane_head(value.shape)
    zero = jnp.zeros_like(value)
    return jnp.where(low, value, zero) if head == 0 else jnp.where(low, zero, value)


def softmax_down(scores, allowed):
    masked = jnp.where(allowed, scores, BLOCKED)
    weights = jnp.exp(masked - jnp.max(masked, axis=0, keepdims=True))
    return (weights * (1.0 / jnp.sum(weights, axis=0, keepdims=True))).astype(BF)


def causal_mask(shape, first):
    return lax.broadcasted_iota(jnp.int32, shape, 0) <= lax.broadcasted_iota(jnp.int32, shape, 1) + first


def segments_of(ids, mine, theirs):
    c, _, z, _ = place(ids)
    second = (z >> 1) == 1
    near = jnp.where(second, mine[1:2], mine[0:1])
    far = jnp.where(second, theirs[1:2], theirs[0:1])
    return jnp.where((z & 1) == c, near, far).astype(F32)


def upright(seg_row):
    return jnp.broadcast_to(seg_row, (8, seg_row.shape[1])).T[:, :1]


def attend(ids, *refs):
    n, refs = refs[:8], refs[8:]
    w, vectors, mine, theirs, n_abs, q_out, k_out, v_out, probs, att_abs = refs
    d = ids[3]
    rows = n_abs.shape[1]
    seq = 8 * rows
    for r in range(8):
        n_abs[r ^ d] = n[r][...]
    tokens = n_abs[...].reshape(seq, n_abs.shape[2])
    pair = aligned(d * PAIR, PAIR)
    projected = dot(tokens, w[...], ((1,), (1,)))
    q = (projected[:, :PAIR] + vectors[6:7, pl.ds(pair, PAIR)]).astype(BF) * BF(HEAD_DIM**-0.5)
    k = projected[:, PAIR : 2 * PAIR].astype(BF)
    v = (projected[:, 2 * PAIR :] + vectors[7:8, pl.ds(pair, PAIR)]).astype(BF)
    q_out[...] = q
    k_out[...] = k
    v_out[...] = v
    seg_row = segments_of(ids, mine, theirs)
    seg_col = upright(seg_row)
    v_t = v.astype(F32).T.astype(BF)
    keys = [only_head(k, h) for h in range(2)]
    step = 2 * rows
    for b in range(4):
        seen = (b + 1) * step
        at = slice(b * step, seen)
        allowed = (seg_col[:seen] == seg_row[:, at]) & causal_mask((seen, step), b * step)
        turned = []
        for h in range(2):
            p = softmax_down(dot(keys[h][:seen], q[at], ((1,), (1,))), allowed)
            probs[h, :seen, at] = p
            turned.append(dot(v_t[h * HEAD_DIM : (h + 1) * HEAD_DIM, :seen], p, ((1,), (0,))))
        attended = jnp.concatenate(turned, 0).T.astype(BF)
        att_abs[2 * b] = attended[:rows]
        att_abs[2 * b + 1] = attended[rows:]


def attend_shared(ids, n_abs, n_own, w16, vectors, mine, theirs, kv_out, qs_out, probs_s, att_s, seg_row):
    d = ids[3]
    rows, width = n_abs.shape[1], n_abs.shape[2]
    seq = 8 * rows
    w16_rows = w16[...]
    nothing = jnp.zeros((1, HEAD_DIM), F32)
    shared_v = jnp.concatenate([nothing, vectors[7:8, 8 * PAIR :]], 1)
    shared_q = vectors[6:7, 8 * PAIR :]
    kv = (dot(n_abs[...].reshape(seq, width), w16_rows[HEAD_DIM:], ((1,), (1,))) + shared_v).astype(BF)
    qs = (dot(n_own[...], w16_rows[:HEAD_DIM], ((1,), (1,))) + shared_q).astype(BF) * BF(HEAD_DIM**-0.5)
    qs = jnp.concatenate([qs, jnp.zeros_like(qs)], 1)
    kv_out[...] = kv
    qs_out[...] = qs
    first = aligned(d * rows, rows)
    seg_row[...] = segments_of(ids, mine, theirs)
    allowed = (upright(seg_row[...]) == seg_row[:, pl.ds(first, rows)]) & causal_mask((seq, rows), first)
    p = softmax_down(dot(only_head(kv, 0), qs, ((1,), (1,))), allowed)
    probs_s[...] = p
    kv_t = kv.astype(F32).T.astype(BF)
    att_s[...] = dot(kv_t[HEAD_DIM:], p, ((1,), (0,))).T.astype(BF)


def out_norm(ids, got, att_s, wo, x_own, vectors, middle, low):
    attended = jnp.concatenate([got[a] for a in range(8)] + [att_s[...]], 1)
    rows = x_own[...].astype(F32) + (dot(attended, wo[...], ((1,), (1,))) + vectors[4:5])
    middle[...] = rows
    low[...] = (normed(rows)[0] * vectors[2:3] + vectors[3:4]).astype(BF)


def weighted(sums, w):
    high = sums.astype(BF)
    low = (sums - high.astype(F32)).astype(BF)
    return dot(high, w, ((1,), (0,))) + dot(low, w, ((1,), (0,)))


def attend_back(ids, g_in, gs_in, q_in, k_in, v_in, kv_in, qs_in, probs, probs_s, w, w16, n_abs, *refs):
    grad_kv, grad_qs, sums, moments, near = refs[:5]
    far, windows, grads, grads_rel, tall = refs[5:9], *refs[9:]
    d = ids[3]
    rows = g_in.shape[1]
    seq = 8 * rows
    g_all = g_in[...].reshape(seq, PAIR)
    g_s = gs_in[...]
    q, k, v, kv, qs = q_in[...], k_in[...], v_in[...], kv_in[...], qs_in[...]
    scale = HEAD_DIM**-0.5
    k_t = k.astype(F32).T.astype(BF)
    values = [only_head(v, h) for h in range(2)]
    step = 2 * rows
    grad_q = []
    grad_k = [[jnp.zeros((step, PAIR), F32) for _ in range(4)] for _ in range(2)]
    grad_v = [[jnp.zeros((step, PAIR), F32) for _ in range(4)] for _ in range(2)]
    for b in range(4):
        seen = (b + 1) * step
        at = slice(b * step, seen)
        turned = []
        for h in range(2):
            p_low = probs[h, :seen, at]
            p = p_low.astype(F32)
            gp = dot(values[h][:seen], g_all[at], ((1,), (1,)))
            inner = jnp.sum(p * gp, axis=0, keepdims=True)
            gs = (p * (gp - inner)).astype(BF)
            turned.append(dot(k_t[h * HEAD_DIM : (h + 1) * HEAD_DIM, :seen], gs, ((1,), (0,))) * scale)
            dk = dot(gs, q[at], ((1,), (0,)))
            dv = dot(p_low, g_all[at], ((1,), (0,)))
            for i in range(b + 1):
                grad_k[h][i] = grad_k[h][i] + dk[i * step : (i + 1) * step]
                grad_v[h][i] = grad_v[h][i] + dv[i * step : (i + 1) * step]
        grad_q.append(jnp.concatenate(turned, 0).T)
    low = lane_head((step, PAIR))
    qsum = jnp.zeros((1, PAIR), F32)
    ksum = jnp.zeros((1, PAIR), F32)
    vsum = jnp.zeros((1, PAIR), F32)
    for i in range(4):
        dq = grad_q[i].astype(BF)
        dk = jnp.where(low, grad_k[0][i], grad_k[1][i]).astype(BF)
        dv = jnp.where(low, grad_v[0][i], grad_v[1][i]).astype(BF)
        qsum = qsum + column_sum(dq.astype(F32))
        ksum = ksum + column_sum(dk.astype(F32))
        vsum = vsum + column_sum(dv.astype(F32))
        for j in range(2):
            part = slice(j * rows, (j + 1) * rows)
            grads[2 * i + j, :, :PAIR] = dq[part]
            grads[2 * i + j, :, PAIR : 2 * PAIR] = dk[part]
            grads[2 * i + j, :, 2 * PAIR : 3 * PAIR] = dv[part]

    p_low = probs_s[...]
    p = p_low.astype(F32)
    v_s = jnp.concatenate([kv[:, HEAD_DIM:], jnp.zeros((seq, HEAD_DIM), BF)], 1)
    g_pad = jnp.concatenate([g_s, jnp.zeros((rows, HEAD_DIM), BF)], 1)
    gp = dot(v_s, g_pad, ((1,), (1,)))
    inner = jnp.sum(p * gp, axis=0, keepdims=True)
    gs = (p * (gp - inner)).astype(BF)
    kv_t = kv.astype(F32).T.astype(BF)
    dq = (dot(kv_t[:HEAD_DIM], gs, ((1,), (0,))) * scale).T.astype(BF)
    grad_qs[...] = dq
    dk = dot(gs, qs, ((1,), (0,)))[:, :HEAD_DIM]
    dv = dot(p_low, g_pad, ((1,), (0,)))[:, :HEAD_DIM]
    dkv = jnp.concatenate([dk, dv], 1).astype(BF)
    for r in range(8):
        grads[r, :, 3 * PAIR :] = dkv[r * rows : (r + 1) * rows]
    last = jnp.concatenate([column_sum(dq.astype(F32)), column_sum(dv.astype(BF).astype(F32))], 1)
    sums[...] = jnp.concatenate([qsum, vsum, last, jnp.zeros((5, PAIR), F32)], 0)

    grad_kv[...] = dkv
    joined = jnp.concatenate([w[...], w16[HEAD_DIM:]], 0)
    for r in range(8):
        grads_rel[r] = grads[r ^ d]
    out = dot(grads_rel[4:].reshape(4 * rows, 4 * PAIR), joined, ((1,), (0,)))
    for k, ref in enumerate(far):
        ref[...] = out[k * rows : (k + 1) * rows].astype(BF)

    width = n_abs.shape[2]
    tokens = n_abs[...].reshape(seq, width)
    pairs = dot(grads[:, :, : 3 * PAIR].reshape(seq, 3 * PAIR), tokens, ((0,), (0,)))
    tall[: 3 * PAIR] = pairs
    tall[3 * PAIR :] = jnp.zeros((WINDOW, width), F32)
    line = lax.broadcasted_iota(jnp.int32, (WINDOW, width), 0)
    for i in range(4):
        _, length, filled = run_of(ids, d, i)
        window = tall[pl.ds(aligned(filled, 16), WINDOW)]
        windows[i] = jnp.where(line < length, window, 0.0).astype(BF)
    pair_sums = jnp.concatenate([qsum, ksum, vsum], 1)
    moments[...] = jnp.concatenate(
        [column_sum(pairs * w[...].astype(F32)), weighted(jnp.broadcast_to(pair_sums, (8, 3 * PAIR)), w[...])[:1]], 0
    )

    out = dot(grads_rel[:4].reshape(4 * rows, 4 * PAIR), joined, ((1,), (0,)))
    near[...] = out.astype(BF)
    near[:rows] = (out[:rows] + dot(dq, w16[:HEAD_DIM], ((1,), (0,)))).astype(BF)


def out_grads(ids, *refs):
    gb, att_abs, att_s, grad_kv, grad_qs, n_abs, n_own, w16, out, moments, gb_abs = refs[:8], *refs[8:]
    d = ids[3]
    rows, width = gb_abs.shape[1], gb_abs.shape[2]
    seq = 8 * rows
    for r in range(8):
        gb_abs[r ^ d] = gb[r][...]
    pair = dot(att_abs[...].reshape(seq, PAIR), gb_abs[...].reshape(seq, width), ((0,), (0,)))
    shared = dot(att_s[...], gb[0][...], ((0,), (0,)))
    q_part = dot(grad_qs[...], n_own[...], ((0,), (0,)))
    kv_part = dot(grad_kv[...], n_abs[...].reshape(seq, width), ((0,), (0,)))
    projections = jnp.concatenate([q_part, kv_part], 0)
    sums = jnp.concatenate([column_sum(grad_qs[...].astype(F32)), column_sum(grad_kv[...].astype(F32))], 1)
    moments[...] = jnp.concatenate(
        [
            column_sum(projections * w16[...].astype(F32)),
            weighted(jnp.broadcast_to(sums, (8, 3 * HEAD_DIM)), w16[...])[:1],
        ],
        0,
    )
    tall = jnp.concatenate([pair, shared, projections], 0).T
    part = out.shape[1]
    for core in range(2):
        for quarter in range(4):
            at = slice((2 * quarter + core) * part, (2 * quarter + core + 1) * part)
            out[core * 4 + quarter] = tall[at].astype(BF)


def add_far(ids, near, f0, f1, f2, f3, s0, s1, s2, s3):
    rows = s0.shape[0]
    for k, (far, ref) in enumerate(((f0, s0), (f1, s1), (f2, s2), (f3, s3))):
        ref[...] = (near[k * rows : (k + 1) * rows].astype(F32) + far[...].astype(F32)).astype(ref.dtype)


def total_of(s0, r1, r2, r3):
    return s0[...] + r1[...].astype(F32) + r2[...].astype(F32) + r3[...].astype(F32)


def middle_back(ids, s0, r1, r2, r3, middle, g_own, wo, vectors, grad_middle, low, sums, back, back_s):
    upstream = total_of(s0, r1, r2, r3)
    centered, inverse = normed(middle[...])
    g = g_own[...].astype(F32)
    grad = g + norm_pull(upstream, centered, inverse, vectors[2:3])
    grad_middle[...] = grad
    rounded = grad.astype(BF)
    low[...] = rounded
    attended = dot(rounded, wo[...], ((1,), (0,))).astype(BF)
    for a in range(8):
        back[a] = attended[:, a * PAIR : (a + 1) * PAIR]
    back_s[...] = attended[:, 8 * PAIR :]
    sums[...] = jnp.concatenate(
        [
            column_sum(rounded.astype(F32)),
            column_sum(upstream * centered),
            column_sum(upstream),
            column_sum(g),
        ],
        0,
    )


def split_features(ids, rows, held, outs, which):
    e = 2 * (ids[1] & 1) + (ids[2] >> 1)
    held[...] = rows.T.reshape(held.shape).astype(BF)
    for m in range(4):
        outs[m][which] = held[m ^ e]


def finish(ids, s0, r1, r2, r3, t0, u1, u2, u3, middle, grad_middle, x_own, vectors, *refs):
    outs, held = refs[:4], refs[4]
    rows = middle[...] + (total_of(t0, u1, u2, u3) + vectors[5:6])
    split_features(ids, rows, held, outs, 0)
    upstream = total_of(s0, r1, r2, r3)
    centered, inverse = normed(x_own[...].astype(F32))
    rows = grad_middle[...] + norm_pull(upstream, centered, inverse, vectors[0:1])
    split_features(ids, rows, held, outs, 1)


def grad_activated(ids, *refs):
    g, both, out, held = refs[:8], *refs[8:]
    rows = held.shape[1]
    down = rows_of(both, 1)
    for r in range(8):
        held[r] = g[r][...]
    for b in range(4):
        block = held[2 * b : 2 * b + 2].reshape(2 * rows, held.shape[2])
        out[b * 2 * rows : (b + 1) * 2 * rows] = dot(block, down, ((1,), (1,)))


def feed_forward(ids, *refs):
    n, refs = refs[:8], refs[8:]
    both, grad_act, bias, n_rel, act, grad_pre, bias_sum = refs[:7]
    up = rows_of(both, 0)
    far, near = refs[7:11], refs[11]
    rows = n_rel.shape[1]
    for r in range(8):
        n_rel[r] = n[r][...]
    total = jnp.zeros(bias_sum.shape, F32)
    for b in (2, 3, 0, 1):
        at = slice(b * 2 * rows, (b + 1) * 2 * rows)
        block = n_rel[2 * b : 2 * b + 2].reshape(2 * rows, n_rel.shape[2])
        pre = dot(block, up, ((1,), (1,))) + bias[...]
        square = pre * pre
        bent = jnp.tanh(ROOT * pre * (1.0 + 0.044715 * square))
        half = 0.5 * (1.0 + bent)
        act[at] = (pre * half).astype(BF)
        slope = half + 0.5 * pre * (1.0 - bent * bent) * (ROOT + ROOT * 3.0 * 0.044715 * square)
        low = (grad_act[at] * slope).astype(BF)
        grad_pre[at] = low
        total = total + column_sum(low.astype(F32))
        out = dot(low, up, ((1,), (0,))).astype(BF)
        if b >= 2:
            far[2 * b - 4][...] = out[:rows]
            far[2 * b - 3][...] = out[rows:]
        else:
            near[2 * rows * b : 2 * rows * (b + 1)] = out
    bias_sum[...] = total


def feed_out(ids, act, both, *refs):
    far, near = refs[:4], refs[4]
    down = rows_of(both, 1)
    half = near.shape[0]
    out = dot(act[half:], down, ((1,), (0,))).astype(BF)
    rows = half // 4
    for k, ref in enumerate(far):
        ref[...] = out[k * rows : (k + 1) * rows]
    near[...] = dot(act[:half], down, ((1,), (0,))).astype(BF)


def mlp_grads(ids, act, grad_pre, n_rel, *refs):
    g, out, held = refs[:8], refs[8], refs[9]
    rows, width = n_rel.shape[1], n_rel.shape[2]
    part = out.shape[2]
    for r in range(8):
        held[r] = g[r][...]
    up = dot(grad_pre[...], n_rel[...].reshape(8 * rows, width), ((0,), (0,)))
    for i in range(4):
        out[i, 0] = up[i * part : (i + 1) * part].astype(BF)
    down = dot(act[...], held[...].reshape(8 * rows, width), ((0,), (0,)))
    for i in range(4):
        out[i, 1] = down[i * part : (i + 1) * part].astype(BF)


def mlp_lanes(ids, summed, o0, o1, o2, o3, held):
    g = ids[1]
    part = held.shape[3]
    for i in range(4):
        held[i] = summed[:, :, i * part : (i + 1) * part]
    for k, ref in enumerate((o0, o1, o2, o3)):
        ref[...] = held[g ^ k]


def mlp_land(ids, *refs):
    blocks, up, down, held = refs[:8], refs[8], refs[9], refs[10]
    d = ids[3]
    for r in range(8):
        held[r ^ d] = blocks[r][...].astype(F32)
    up[...] = held[:, 0].reshape(-1, held.shape[3]).T
    down[...] = held[:, 1].reshape(-1, held.shape[3]).T


def qkv_lanes(ids, window, o0, o1, o2, o3, held):
    g = ids[1]
    part = held.shape[2]
    for i in range(4):
        held[i] = window[:, i * part : (i + 1) * part]
    for k, ref in enumerate((o0, o1, o2, o3)):
        ref[...] = held[g ^ k]


def qkv_land(ids, *refs):
    blocks, mine, theirs, out, tall, held = refs[:8], *refs[8:]
    c, g, z, d = place(ids)
    tall[...] = jnp.zeros(tall.shape, F32)
    for r in range(8):
        start, _, _ = run_of(ids, r ^ d, z)
        at = pl.ds(aligned(start, 16), WINDOW)
        tall[at] = tall[at] + blocks[r][...].astype(F32)
    held[c] = mine[:, 272:].astype(F32)
    held[1 - c] = theirs[:, 272:].astype(F32)
    shared = held[...].reshape(-1, HEAD_DIM).T
    keep = jnp.where(z > 0, 1.0, 0.0)
    at = pl.ds(aligned(jnp.maximum(272 * z - HEAD_DIM, 0), 8), HEAD_DIM)
    tall[at] = tall[at] + shared * keep
    out[...] = tall[: out.shape[1]].T


def out_split(ids, got, o0, o1, o2, o3, wide, held):
    z = ids[2]
    part = wide.shape[1] // 4
    shared = jnp.zeros((got.shape[1], 4 * HEAD_DIM), F32)
    for a in range(8):
        wide[:, a * PAIR : (a + 1) * PAIR] = got[a, :, :PAIR].astype(F32)
        shared = shared + got[a, :, PAIR:].astype(F32)
    wide[:, 8 * PAIR :] = shared[:, :HEAD_DIM]
    for i in range(4):
        at = max(i, 1) * HEAD_DIM
        held[i] = jnp.concatenate(
            [wide[:, i * part : (i + 1) * part], shared[:, at : at + HEAD_DIM]], 1
        ).astype(BF)
    for s, ref in enumerate((o0, o1, o2, o3)):
        ref[...] = held[(z + s) & 3]


def sum_four(ids, b0, b1, b2, b3, out):
    out[...] = sum(ref[...].astype(F32) for ref in (b0, b1, b2, b3)).astype(BF)


def out_land(ids, mine, theirs, out, held):
    c = ids[0]
    held[c] = mine[:, :272].astype(F32)
    held[1 - c] = theirs[:, :272].astype(F32)
    out[...] = held[...].reshape(-1, held.shape[2]).T


def join_sums(ids, first, second, qkv, middle, up, out):
    d = ids[3]
    out[:2] = first[...] + second[...]
    out[2:4] = jnp.zeros((2, out.shape[1]), F32)
    at = pl.ds(aligned(d * PAIR, PAIR), PAIR)
    out[2:3, at] = qkv[0:1]
    out[3:4, at] = qkv[1:2]
    out[2:3, 8 * PAIR :] = qkv[2:3, :HEAD_DIM]
    out[3:4, 8 * PAIR :] = qkv[2:3, HEAD_DIM:]
    out[4:8] = middle[...]
    part = up.shape[1] // 4
    for i in range(4):
        piece = up[:, i * part : (i + 1) * part]
        out[8 + i : 9 + i] = jnp.concatenate([jnp.where(d == a, piece, 0.0) for a in range(8)], 1)


def keep(ids, *refs):
    count = len(refs) // 2
    for source, target in zip(refs[:count], refs[count:], strict=True):
        target[...] = source[...]


def add_two(ids, a, b, out):
    out[...] = a[...] + b[...]


def split_sums(ids, a, b, vectors, out):
    total = a[...] + b[...]
    out[...] = total
    out[0:1] = (total[0:1] - vectors[1:2] * total[1:2]) / vectors[0:1]


def shards(
    hidden_in,
    segment_ids,
    cotangent,
    norm1_gain,
    norm1_shift,
    w_qkv,
    q_bias,
    v_bias,
    w_out,
    out_bias,
    norm2_gain,
    norm2_shift,
    w_up,
    up_bias,
    w_down,
    down_bias,
):
    c = lax.axis_index("c")
    g = lax.axis_index("gx")
    z = lax.axis_index("gy")
    d = c * 4 + g
    width = norm1_gain.shape[0]
    hidden = up_bias.shape[0]
    quarter = hidden_in.shape[2]
    half = quarter // 2
    part = hidden // 32
    own_hidden = hidden // 8
    cols = w_qkv.shape[1]
    seq = segment_ids.shape[1]
    rows = seq // 8
    outer = lax.axis_size("do") > 1
    ids = jnp.concatenate(
        [jnp.stack([c, g, z, d]).astype(jnp.int32), jnp.asarray(run_table(width, cols))]
    )
    vectors = jnp.stack(
        [norm1_gain, norm1_shift, norm2_gain, norm2_shift, out_bias, down_bias, q_bias, v_bias]
    ).astype(F32)

    def row(vector):
        return vector.reshape(1, -1)

    def over_outer(value):
        return lax.psum(value, "do") if outer else value

    block = ((2, quarter, rows), BF)
    own_bf, own_f32 = ((rows, width), BF), ((rows, width), F32)
    held_tokens = ((4, quarter, rows), BF)

    def peers(blocks):
        return [blocks[0]] + [from_peer(blocks[k], k) for k in range(1, 4)]

    def gather_near(own):
        return [own] + [from_peer(own, k) for k in range(1, 4)]

    def gather_later(near, after):
        held = kernel(keep, [(a.shape, a.dtype) for a in near], [], ids, *near, us=0.8, after=after)
        return near + [swap_core(piece) for piece in held]

    def shifted(blocks):
        return [blocks[0]] + [from_below(blocks[s], s) for s in range(1, 4)]

    window = ((WINDOW, quarter), BF)
    window_wide = ((WINDOW, width), BF)
    windows = kernel(qkv_windows, [window] * 4, [((cols + WINDOW, quarter), F32)], ids, w_qkv, us=1.5)
    first = windows[0]
    windows = peers(windows)
    sent = kernel(
        send_tokens, [block] * 4, [], ids, hidden_in.transpose(0, 2, 1), cotangent.transpose(0, 2, 1), us=1.0, after=(first,)
    )
    blocks = [lax.ppermute(sent[m], EVERY, MOVES[m]) for m in range(4)]
    lines = TALL + 3 * 16
    out_piece = kernel(
        out_half, [((lines, quarter), BF)], [((cols, quarter), F32)], ids, w_out, w_qkv, us=1.0, after=(sent[0],)
    )
    piece = ((WINDOW + lines // 4, width), BF)
    joined = kernel(join_lanes, [piece], [((4, WINDOW, quarter), BF)], ids, *windows, out_piece, us=1.0)
    joined = shifted([joined] * 4)
    *mlp_sent, up_bias_own = kernel(
        mlp_blocks,
        [((2, part, quarter), BF)] * 4 + [((1, own_hidden), F32)],
        [((2, 8, part, quarter), F32)],
        ids,
        w_up,
        w_down.T,
        up_bias.astype(F32).reshape(4, 8, part),
        us=2.0,
        after=(joined[0],),
    )
    mlp_got = peers(mlp_sent)
    x_own, n1_own = kernel(
        take_normed, [own_bf, own_bf], [held_tokens], ids, *blocks, vectors, us=1.5, after=(joined[1], joined[3], *mlp_got[1:])
    )
    n1 = gather_plane(n1_own)
    g_own = kernel(
        take_tokens, [own_bf], [held_tokens], ids, *blocks, us=1.0, after=(n1_own,)
    )
    g_near = gather_near(g_own)
    w_own, out_row = kernel(
        qkv_assemble,
        [((3 * PAIR, width), BF), ((TALL + 32, width), BF)],
        [((4, *piece[0]), BF), ((3 * PAIR + WINDOW, width), BF)],
        ids,
        *joined,
        us=1.0,
        after=(g_own,),
    )
    mlp_part = kernel(
        mlp_join,
        [((2, part, width), BF)],
        [((4, 2, part, quarter), BF)],
        ids,
        *mlp_got,
        us=1.0,
        after=(w_own,),
    )
    mlp_own = lax.all_gather(mlp_part, "gy", axis=0, tiled=False)
    swapped_ids = swap_core(segment_ids)

    half_rows = ((4 * rows, width), BF)
    all_bf = ((8, rows, width), BF)
    heads_bf = ((8, rows, PAIR), BF)
    pair_seq = ((seq, PAIR), BF)
    n_abs, q, k, v, probs, att = kernel(
        attend,
        [all_bf, pair_seq, pair_seq, pair_seq, ((2, seq, seq), BF), heads_bf],
        [],
        ids,
        *n1,
        w_own,
        vectors,
        segment_ids,
        swapped_ids,
        us=3.0,
        far=True,
        after=(mlp_part,),
    )
    att_got = lax.all_to_all(att, PLANE, split_axis=0, concat_axis=0, tiled=True)
    out_rows = gather_later(gather_near(out_row), (att_got,))
    wo, w16 = kernel(
        out_whole,
        [((width, width), BF), ((3 * HEAD_DIM, width), BF)],
        [((4, 3, 2, 4, 8, quarter), F32)],
        ids,
        *out_rows,
        us=1.0,
    )
    kv, qs, probs_s, att_s = kernel(
        attend_shared,
        [pair_seq, ((rows, PAIR), BF), ((seq, rows), BF), ((rows, HEAD_DIM), BF)],
        [((1, seq), F32)],
        ids,
        n_abs,
        n1_own,
        w16,
        vectors,
        segment_ids,
        swapped_ids,
        us=0.5,
        work=6,
    )
    middle, n2_own = kernel(
        out_norm, [own_f32, own_bf], [], ids, att_got, att_s, wo, x_own, vectors, us=0.5, work=6
    )
    g_all = gather_later(g_near, (n2_own,))
    summed = [own_f32, own_bf, own_bf, own_bf]

    def scatter(near, far, after=()):
        return peers(
            kernel(add_far, summed, [], ids, near, *[swap_core(f) for f in far], us=1.2, after=after)
        )

    n2 = gather_plane(n2_own)

    grad_act = kernel(
        grad_activated,
        [((seq, own_hidden), F32)],
        [all_bf],
        ids,
        *g_all,
        mlp_own,
        us=3.0,
        far=True,
        after=(n2_own,),
    )
    n_rel, act, grad_pre, up_sum, *far, near = kernel(
        feed_forward,
        [
            all_bf,
            ((seq, own_hidden), BF),
            ((seq, own_hidden), BF),
            ((1, own_hidden), F32),
            *[own_bf] * 4,
            half_rows,
        ],
        [],
        ids,
        *n2,
        mlp_own,
        grad_act,
        up_bias_own,
        us=7.0,
        work=14,
    )
    parts = scatter(near, far)
    mlp_partial = kernel(
        mlp_grads,
        [((4, 2, part, width), BF)],
        [all_bf],
        ids,
        act,
        grad_pre,
        n_rel,
        *g_all,
        us=5.0,
        far=True,
        after=(parts[0],),
    )
    *feed_far, feed_near = kernel(
        feed_out, [own_bf] * 4 + [half_rows], [], ids, act, mlp_own, us=2.5, work=8, after=(mlp_partial,)
    )
    mlp_summed = over_outer(lax.psum_scatter(mlp_partial, "gy", scatter_dimension=0, tiled=False))
    grad_middle, gb_own, middle_sums, back, back_s = kernel(
        middle_back,
        [own_f32, own_bf, ((4, width), F32), heads_bf, ((rows, HEAD_DIM), BF)],
        [],
        ids,
        *parts,
        middle,
        g_own,
        wo,
        vectors,
        us=2.5,
        work=6,
        after=(mlp_partial,),
    )
    back = lax.all_to_all(back, PLANE, split_axis=0, concat_axis=0, tiled=True)
    gb = gather_plane(gb_own)

    feed_parts = scatter(feed_near, feed_far, (back,))

    grad_kv, grad_qs, qkv_sums, moments, near, *rest = kernel(
        attend_back,
        [pair_seq, ((rows, HEAD_DIM), BF), ((8, PAIR), F32), ((2, width), F32), half_rows]
        + [own_bf] * 4
        + [((4, WINDOW, width), BF)],
        [
            ((8, rows, 4 * PAIR), BF),
            ((8, rows, 4 * PAIR), BF),
            ((3 * PAIR + WINDOW, width), F32),
        ],
        ids,
        back,
        back_s,
        q,
        k,
        v,
        kv,
        qs,
        probs,
        probs_s,
        w_own,
        w16,
        n_abs,
        us=3.0,
        far=True,
        after=(feed_parts[0],),
    )
    far = rest[:4]
    window_sum = lax.psum_scatter(rest[4], "gy", scatter_dimension=0, tiled=False)
    parts = scatter(near, far)
    out_sent, moments_s = kernel(
        out_grads,
        [((8, half, PAIR + 4 * HEAD_DIM), BF), ((2, width), F32)],
        [all_bf],
        ids,
        *gb,
        att,
        att_s,
        grad_kv,
        grad_qs,
        n_abs,
        n1_own,
        w16,
        us=3.5,
        work=10,
        after=tuple(parts[1:]),
    )
    out_got = lax.all_to_all(out_sent, PLANE, split_axis=0, concat_axis=0, tiled=True)
    mlp_parts = kernel(
        mlp_lanes,
        [((2, part, quarter), BF)] * 4,
        [((4, 2, part, quarter), BF)],
        ids,
        mlp_summed,
        us=1.0,
    )
    split_piece = ((half, quarter + HEAD_DIM), BF)
    out_split_parts = shifted(
        kernel(
            out_split,
            [split_piece] * 4,
            [((half, width), F32), ((4, half, quarter + HEAD_DIM), BF)],
            ids,
            out_got,
            us=1.0,
        )
    )
    done = kernel(
        finish,
        [block] * 4,
        [held_tokens],
        ids,
        *parts,
        *feed_parts,
        middle,
        grad_middle,
        x_own,
        vectors,
        us=2.5,
    )
    landed = [lax.ppermute(done[m], EVERY, BACK[m]) for m in range(4)]
    hidden_out, grad_in = kernel(land_tokens, [((2, quarter, 2 * rows), BF)] * 2, [], ids, *landed, us=1.0)

    smalls = kernel(
        join_sums, [((12, width), F32)], [], ids, moments, moments_s, qkv_sums, middle_sums, up_sum, us=0.7
    )
    smalls = smalls + swap_core(smalls)
    smalls = smalls + from_peer(smalls, 1)
    others = from_peer(smalls, 2)
    blocks = peers(mlp_parts)
    lanes = kernel(
        qkv_lanes, [window] * 4, [((4, WINDOW, quarter), BF)], ids, window_sum, us=1.0, after=(*landed, *blocks[1:], out_split_parts[0], others)
    )
    near = peers(lanes)
    near = [*near, *[swap_core(piece) for piece in near]]
    total_up, total_down = kernel(
        mlp_land,
        [((quarter, hidden // 4), F32)] * 2,
        [((8, 2, part, quarter), F32)],
        ids,
        *blocks,
        *[swap_core(piece) for piece in blocks],
        us=2.0,
        after=(lanes[0],),
    )
    mine = kernel(sum_four, [split_piece], [], ids, *out_split_parts, us=0.6, after=(lanes[0],))
    theirs = swap_core(mine)
    total_out = kernel(
        out_land, [((quarter, quarter), F32)], [((2, half, quarter), F32)], ids, mine, theirs, us=0.7
    )
    total_out = over_outer(total_out)

    total_qkv = kernel(
        qkv_land,
        [((quarter, cols), F32)],
        [((cols + WINDOW, quarter), F32), ((2, half, HEAD_DIM), F32)],
        ids,
        *near,
        mine,
        theirs,
        us=2.0,
    )
    total_qkv = over_outer(total_qkv)
    smalls = kernel(add_two, [((12, width), F32)], [], ids, smalls, others, us=0.7, after=(lanes[0],))
    smalls = smalls + lax.ppermute(smalls, "gy", [(i, i ^ 1) for i in range(4)])
    others = lax.ppermute(smalls, "gy", [(i, i ^ 2) for i in range(4)])
    smalls, others = over_outer(smalls), over_outer(others)
    smalls = kernel(split_sums, [((12, width), F32)], [], ids, smalls, others, vectors, us=0.7)


    return (
        hidden_out.transpose(0, 2, 1),
        grad_in.transpose(0, 2, 1),
        smalls[0],
        smalls[1],
        total_qkv,
        smalls[2],
        smalls[3],
        total_out,
        smalls[4],
        smalls[5],
        smalls[6],
        total_up,
        smalls[8:12].reshape(hidden),
        total_down.T,
        smalls[7],
    )


def solution(mesh):
    devices = mesh.devices
    split = Mesh(
        devices.reshape(devices.shape[0] // 2, 2, devices.shape[1], devices.shape[2]), ("do", "c", "gx", "gy")
    )
    stream = P(None, ("do", "c", "gy"), "gx")
    flat = P()
    tall = P("gx", "gy")
    wide = P("gy", "gx")
    grads = (flat, flat, tall, flat, flat, wide, flat, flat, flat, tall, flat, wide, flat)
    return jax.shard_map(
        shards,
        mesh=split,
        in_specs=(stream, P(None, ("do", "c")), stream, *grads),
        out_specs=(stream, stream, *grads),
        check_vma=False,
    )
```

```python
import math

import jax
import jax.numpy as jnp
import numpy as np
from jax import lax
from jax.experimental import pallas as pl
from jax.experimental.pallas import tpu as pltpu
from jax.sharding import Mesh
from jax.sharding import PartitionSpec as P

HEAD_DIM = 64
PAIR = 2 * HEAD_DIM
EPSILON = 1e-05
BLOCKED = -1e30
BF = jnp.bfloat16
F32 = jnp.float32
PLANE = ("c", "gx")
EVERY = ("c", "gx", "gy")
ROOT = math.sqrt(2.0 / math.pi)
WINDOW = 128
TALL = WINDOW + 16
MIB = 1024 * 1024


def dot(left, right, dims):
    return lax.dot_general(left, right, (dims, ((), ())), preferred_element_type=F32)


def padded(shape, kind):
    size = jnp.dtype(kind).itemsize
    lines = 1 if len(shape) < 2 else -(-shape[-2] // 16) * 16
    return math.prod(shape[:-2]) * lines * (-(-shape[-1] // 128) * 128) * size


def kernel(body, outs, scratch, ids, *arrays, us=0.2, work=2, after=(), far=False):
    count, late = len(arrays), len(after)

    def run(*refs):
        body(*refs[: 1 + count], *refs[1 + count + late :])

    vmem = pl.BlockSpec(memory_space=pltpu.VMEM)
    total = sum(padded(a.shape, a.dtype) for a in arrays) + sum(padded(*o) for o in [*outs, *scratch])
    result = pl.pallas_call(
        run,
        name=body.__name__,
        out_shape=tuple(jax.ShapeDtypeStruct(shape, kind) for shape, kind in outs),
        in_specs=[pl.BlockSpec(memory_space=pltpu.SMEM)] + [vmem] * count + [pl.BlockSpec(memory_space=pl.ANY)] * late,
        out_specs=tuple(vmem for _ in outs),
        scratch_shapes=[pltpu.VMEM(shape, kind) for shape, kind in scratch],
        compiler_params=pltpu.CompilerParams(vmem_limit_bytes=60 * MIB if far else int(total * 1.02) + work * MIB),
        cost_estimate=pl.CostEstimate(flops=int(us * 5e9), bytes_accessed=int(us * 1e5), transcendentals=0),
    )(ids, *arrays, *after)
    return result if len(outs) > 1 else result[0]


def swap_core(value):
    return lax.ppermute(value, "c", [(0, 1), (1, 0)])


def from_peer(value, step):
    return lax.ppermute(value, "gx", [(i, i ^ step) for i in range(4)])


def from_below(value, step):
    return lax.ppermute(value, "gy", [(i, (i + step) % 4) for i in range(4)])


def gather_plane(own):
    near = [own] + [from_peer(own, k) for k in range(1, 4)]
    return near + [swap_core(piece) for piece in near]


def position(c, g, z):
    return (c * 4 + g) * 4 + z


def token_moves():
    moves = []
    for m in range(4):
        move = []
        for c in range(2):
            for g in range(4):
                for z in range(4):
                    t, mb = (m ^ g) >> 1, (m ^ g) & 1
                    move.append((position(c, g, z), position(z // 2, 2 * (z % 2) + t, 2 * mb + c)))
        moves.append(move)
    return moves


MOVES = token_moves()
BACK = [[(b, a) for a, b in move] for move in MOVES]


def run_table(width, cols):
    table = np.zeros((8, 4, 3), np.int32)
    for d in range(8):
        filled = 0
        for z in range(4):
            for t in range(3):
                low = max(width * t + PAIR * d, cols * z)
                high = min(width * t + PAIR * (d + 1), cols * (z + 1))
                if high > low:
                    table[d, z] = (low - cols * z, high - low, filled)
                    filled += high - low
            if table[d, z, 1] == 0:
                table[d, z, 2] = filled
    return table.reshape(-1)


def aligned(value, step):
    return pl.multiple_of(value, step)


def normed(rows):
    average = jnp.mean(rows, axis=1, keepdims=True)
    centered = rows - average
    inverse = lax.rsqrt(jnp.mean(centered * centered, axis=1, keepdims=True) + EPSILON)
    return centered * inverse, inverse


def norm_pull(upstream, centered, inverse, gain):
    scaled = upstream * gain
    return inverse * (
        scaled
        - jnp.mean(scaled, axis=1, keepdims=True)
        - centered * jnp.mean(scaled * centered, axis=1, keepdims=True)
    )


def column_sum(rows):
    return jnp.sum(rows, axis=0, keepdims=True)


def place(ids):
    return ids[0], ids[1], ids[2], ids[3]


def run_of(ids, d, z):
    at = 4 + d * 12 + z * 3
    return ids[at], ids[at + 1], ids[at + 2]


def lanes_of(half, rows):
    return pl.ds(aligned(half * rows, rows), rows)


def send_tokens(ids, x, g_in, *outs):
    g = ids[1]
    for m in range(4):
        v = m ^ g
        for t, src in enumerate((x, g_in)):
            outs[m][t] = src[v & 1, :, lanes_of(v >> 1, outs[m].shape[2])]


def own_rows(ids, blocks, held, which):
    e = 2 * (ids[1] & 1) + (ids[2] >> 1)
    for m in range(4):
        held[m ^ e] = blocks[m][which]
    return held[...].astype(F32).reshape(-1, held.shape[2]).T


def take_tokens(ids, b0, b1, b2, b3, out, held):
    out[...] = own_rows(ids, (b0, b1, b2, b3), held, 1).astype(BF)


def take_normed(ids, b0, b1, b2, b3, vectors, out, low, held):
    rows = own_rows(ids, (b0, b1, b2, b3), held, 0)
    out[...] = rows.astype(BF)
    low[...] = (normed(rows)[0] * vectors[0:1] + vectors[1:2]).astype(BF)


def land_tokens(ids, b0, b1, b2, b3, first, second):
    g = ids[1]
    for m, block in enumerate((b0, b1, b2, b3)):
        v = m ^ g
        for t, out in enumerate((first, second)):
            out[v & 1, :, lanes_of(v >> 1, block.shape[2])] = block[t]


def qkv_windows(ids, w, o0, o1, o2, o3, tall):
    c, g, z, d = place(ids)
    rows = w.shape[1]
    tall[:rows] = w[...].astype(F32).T
    tall[rows:] = jnp.zeros((tall.shape[0] - rows, tall.shape[1]), F32)
    for k, ref in enumerate((o0, o1, o2, o3)):
        start, _, _ = run_of(ids, c * 4 + (g ^ k), z)
        ref[...] = tall[pl.ds(aligned(start, 16), WINDOW)].astype(BF)


def join_lanes(ids, b0, b1, b2, b3, piece, out, held):
    g = ids[1]
    for k, block in enumerate((b0, b1, b2, b3)):
        held[g ^ k] = block[...]
    part = held.shape[2]
    lines = piece.shape[0] // 4
    for i in range(4):
        at = slice(i * part, (i + 1) * part)
        out[:WINDOW, at] = held[i]
        out[WINDOW:, at] = piece[i * lines : (i + 1) * lines]


def qkv_assemble(ids, b0, b1, b2, b3, out, row, held, tall):
    c, g, z, d = place(ids)
    for s, block in enumerate((b0, b1, b2, b3)):
        held[(z + 4 - s) & 3] = block[...]
    for i in range(4):
        _, _, filled = run_of(ids, d, i)
        tall[pl.ds(aligned(filled, 16), WINDOW)] = held[i, :WINDOW]
    out[...] = tall[: out.shape[0]]
    part = out.shape[1] // 4
    lines = held.shape[1] - WINDOW
    shared = []
    for i in range(4):
        for j in range(3):
            piece = held[i, WINDOW:, j * part : (j + 1) * part]
            row[j * lines : (j + 1) * lines, i * part : (i + 1) * part] = piece
        if i:
            piece = held[i, WINDOW:, 3 * part :].astype(F32)
            shared.append(jnp.concatenate([piece[8 * k : 8 * k + 8] for k in range(4)], 1))
    shared.append(jnp.zeros_like(shared[0]))
    row[TALL:] = jnp.concatenate(shared, 0).astype(BF)


def mlp_blocks(ids, up, down, bias, o0, o1, o2, o3, own_bias, held):
    c, g, z, d = place(ids)
    for t, w in enumerate((up, down)):
        held[t] = w[...].astype(F32).T.reshape(held.shape[1:])
    for k, ref in enumerate((o0, o1, o2, o3)):
        to = c * 4 + (g ^ k)
        ref[0] = held[0, to].astype(BF)
        ref[1] = held[1, to].astype(BF)
    own_bias[...] = jnp.concatenate([bias[i, pl.ds(d, 1)] for i in range(4)], 1)


def mlp_join(ids, b0, b1, b2, b3, out, held):
    g = ids[1]
    for k, block in enumerate((b0, b1, b2, b3)):
        held[g ^ k] = block[...]
    part = held.shape[3]
    for i in range(4):
        out[:, :, i * part : (i + 1) * part] = held[i]


def rows_of(both, which):
    return both[:, which].astype(F32).reshape(-1, both.shape[3]).astype(BF)


def out_half(ids, w, wq, out, tall):
    c, _, z, _ = place(ids)
    tall[: w.shape[1]] = w[...].astype(F32).T
    out[:TALL] = tall[pl.ds(aligned(c * WINDOW, 8), TALL)].astype(BF)
    tall[: wq.shape[1]] = wq[...].astype(F32).T
    at = jnp.maximum(272 * z - HEAD_DIM, 0) + c * (HEAD_DIM // 2)
    shared = tall[pl.ds(aligned(at, 8), HEAD_DIM // 2)]
    out[TALL:] = jnp.concatenate([shared, jnp.zeros((16, shared.shape[1]), F32)], 0).astype(BF)


def out_whole(ids, *refs):
    pieces, out, w16, held = refs[:8], refs[8], refs[9], refs[10]
    d = ids[3]
    part = held.shape[5]
    for r in range(8):
        owner = r ^ d
        core, quarter = owner >> 2, owner & 3
        out[pl.ds(aligned(272 * quarter + WINDOW * core, 16), TALL)] = pieces[r][:TALL]
        shared = pieces[r][TALL:].astype(F32)
        for t in range(3):
            for i in range(4):
                held[quarter, t, core, i] = shared[8 * t : 8 * t + 8, i * part : (i + 1) * part]
    for q in range(4):
        w16[:, q * part : (q + 1) * part] = held[q].reshape(3 * HEAD_DIM, part).astype(BF)


def lane_head(shape):
    return lax.broadcasted_iota(jnp.int32, shape, len(shape) - 1) < HEAD_DIM


def only_head(value, head):
    low = lane_head(value.shape)
    zero = jnp.zeros_like(value)
    return jnp.where(low, value, zero) if head == 0 else jnp.where(low, zero, value)


def softmax_down(scores, allowed):
    masked = jnp.where(allowed, scores, BLOCKED)
    weights = jnp.exp(masked - jnp.max(masked, axis=0, keepdims=True))
    return (weights * (1.0 / jnp.sum(weights, axis=0, keepdims=True))).astype(BF)


def causal_mask(shape, first):
    return lax.broadcasted_iota(jnp.int32, shape, 0) <= lax.broadcasted_iota(jnp.int32, shape, 1) + first


def segments_of(ids, mine, theirs):
    c, _, z, _ = place(ids)
    second = (z >> 1) == 1
    near = jnp.where(second, mine[1:2], mine[0:1])
    far = jnp.where(second, theirs[1:2], theirs[0:1])
    return jnp.where((z & 1) == c, near, far).astype(F32)


def upright(seg_row):
    return jnp.broadcast_to(seg_row, (8, seg_row.shape[1])).T[:, :1]


def attend(ids, *refs):
    n, refs = refs[:8], refs[8:]
    w, vectors, mine, theirs, n_abs, q_out, k_out, v_out, probs, att_abs = refs
    d = ids[3]
    rows = n_abs.shape[1]
    seq = 8 * rows
    for r in range(8):
        n_abs[r ^ d] = n[r][...]
    tokens = n_abs[...].reshape(seq, n_abs.shape[2])
    pair = aligned(d * PAIR, PAIR)
    projected = dot(tokens, w[...], ((1,), (1,)))
    q = (projected[:, :PAIR] + vectors[6:7, pl.ds(pair, PAIR)]).astype(BF) * BF(HEAD_DIM**-0.5)
    k = projected[:, PAIR : 2 * PAIR].astype(BF)
    v = (projected[:, 2 * PAIR :] + vectors[7:8, pl.ds(pair, PAIR)]).astype(BF)
    q_out[...] = q
    k_out[...] = k
    v_out[...] = v
    seg_row = segments_of(ids, mine, theirs)
    seg_col = upright(seg_row)
    v_t = v.astype(F32).T.astype(BF)
    keys = [only_head(k, h) for h in range(2)]
    step = 2 * rows
    for b in range(4):
        seen = (b + 1) * step
        at = slice(b * step, seen)
        allowed = (seg_col[:seen] == seg_row[:, at]) & causal_mask((seen, step), b * step)
        turned = []
        for h in range(2):
            p = softmax_down(dot(keys[h][:seen], q[at], ((1,), (1,))), allowed)
            probs[h, :seen, at] = p
            turned.append(dot(v_t[h * HEAD_DIM : (h + 1) * HEAD_DIM, :seen], p, ((1,), (0,))))
        attended = jnp.concatenate(turned, 0).T.astype(BF)
        att_abs[2 * b] = attended[:rows]
        att_abs[2 * b + 1] = attended[rows:]


def attend_shared(ids, n_abs, n_own, w16, vectors, mine, theirs, kv_out, qs_out, probs_s, att_s, seg_row):
    d = ids[3]
    rows, width = n_abs.shape[1], n_abs.shape[2]
    seq = 8 * rows
    w16_rows = w16[...]
    nothing = jnp.zeros((1, HEAD_DIM), F32)
    shared_v = jnp.concatenate([nothing, vectors[7:8, 8 * PAIR :]], 1)
    shared_q = vectors[6:7, 8 * PAIR :]
    kv = (dot(n_abs[...].reshape(seq, width), w16_rows[HEAD_DIM:], ((1,), (1,))) + shared_v).astype(BF)
    qs = (dot(n_own[...], w16_rows[:HEAD_DIM], ((1,), (1,))) + shared_q).astype(BF) * BF(HEAD_DIM**-0.5)
    qs = jnp.concatenate([qs, jnp.zeros_like(qs)], 1)
    kv_out[...] = kv
    qs_out[...] = qs
    first = aligned(d * rows, rows)
    seg_row[...] = segments_of(ids, mine, theirs)
    allowed = (upright(seg_row[...]) == seg_row[:, pl.ds(first, rows)]) & causal_mask((seq, rows), first)
    p = softmax_down(dot(only_head(kv, 0), qs, ((1,), (1,))), allowed)
    probs_s[...] = p
    kv_t = kv.astype(F32).T.astype(BF)
    att_s[...] = dot(kv_t[HEAD_DIM:], p, ((1,), (0,))).T.astype(BF)


def out_norm(ids, got, att_s, wo, x_own, vectors, middle, low):
    attended = jnp.concatenate([got[a] for a in range(8)] + [att_s[...]], 1)
    rows = x_own[...].astype(F32) + (dot(attended, wo[...], ((1,), (1,))) + vectors[4:5])
    middle[...] = rows
    low[...] = (normed(rows)[0] * vectors[2:3] + vectors[3:4]).astype(BF)


def weighted(sums, w):
    high = sums.astype(BF)
    low = (sums - high.astype(F32)).astype(BF)
    return dot(high, w, ((1,), (0,))) + dot(low, w, ((1,), (0,)))


def attend_back(ids, g_in, gs_in, q_in, k_in, v_in, kv_in, qs_in, probs, probs_s, w, w16, n_abs, *refs):
    grad_kv, grad_qs, sums, moments, near = refs[:5]
    far, windows, grads, grads_rel, tall = refs[5:9], *refs[9:]
    d = ids[3]
    rows = g_in.shape[1]
    seq = 8 * rows
    g_all = g_in[...].reshape(seq, PAIR)
    g_s = gs_in[...]
    q, k, v, kv, qs = q_in[...], k_in[...], v_in[...], kv_in[...], qs_in[...]
    scale = HEAD_DIM**-0.5
    k_t = k.astype(F32).T.astype(BF)
    values = [only_head(v, h) for h in range(2)]
    step = 2 * rows
    grad_q = []
    grad_k = [[jnp.zeros((step, PAIR), F32) for _ in range(4)] for _ in range(2)]
    grad_v = [[jnp.zeros((step, PAIR), F32) for _ in range(4)] for _ in range(2)]
    for b in range(4):
        seen = (b + 1) * step
        at = slice(b * step, seen)
        turned = []
        for h in range(2):
            p_low = probs[h, :seen, at]
            p = p_low.astype(F32)
            gp = dot(values[h][:seen], g_all[at], ((1,), (1,)))
            inner = jnp.sum(p * gp, axis=0, keepdims=True)
            gs = (p * (gp - inner)).astype(BF)
            turned.append(dot(k_t[h * HEAD_DIM : (h + 1) * HEAD_DIM, :seen], gs, ((1,), (0,))) * scale)
            dk = dot(gs, q[at], ((1,), (0,)))
            dv = dot(p_low, g_all[at], ((1,), (0,)))
            for i in range(b + 1):
                grad_k[h][i] = grad_k[h][i] + dk[i * step : (i + 1) * step]
                grad_v[h][i] = grad_v[h][i] + dv[i * step : (i + 1) * step]
        grad_q.append(jnp.concatenate(turned, 0).T)
    low = lane_head((step, PAIR))
    qsum = jnp.zeros((1, PAIR), F32)
    ksum = jnp.zeros((1, PAIR), F32)
    vsum = jnp.zeros((1, PAIR), F32)
    for i in range(4):
        dq = grad_q[i].astype(BF)
        dk = jnp.where(low, grad_k[0][i], grad_k[1][i]).astype(BF)
        dv = jnp.where(low, grad_v[0][i], grad_v[1][i]).astype(BF)
        qsum = qsum + column_sum(dq.astype(F32))
        ksum = ksum + column_sum(dk.astype(F32))
        vsum = vsum + column_sum(dv.astype(F32))
        for j in range(2):
            part = slice(j * rows, (j + 1) * rows)
            grads[2 * i + j, :, :PAIR] = dq[part]
            grads[2 * i + j, :, PAIR : 2 * PAIR] = dk[part]
            grads[2 * i + j, :, 2 * PAIR : 3 * PAIR] = dv[part]

    p_low = probs_s[...]
    p = p_low.astype(F32)
    v_s = jnp.concatenate([kv[:, HEAD_DIM:], jnp.zeros((seq, HEAD_DIM), BF)], 1)
    g_pad = jnp.concatenate([g_s, jnp.zeros((rows, HEAD_DIM), BF)], 1)
    gp = dot(v_s, g_pad, ((1,), (1,)))
    inner = jnp.sum(p * gp, axis=0, keepdims=True)
    gs = (p * (gp - inner)).astype(BF)
    kv_t = kv.astype(F32).T.astype(BF)
    dq = (dot(kv_t[:HEAD_DIM], gs, ((1,), (0,))) * scale).T.astype(BF)
    grad_qs[...] = dq
    dk = dot(gs, qs, ((1,), (0,)))[:, :HEAD_DIM]
    dv = dot(p_low, g_pad, ((1,), (0,)))[:, :HEAD_DIM]
    dkv = jnp.concatenate([dk, dv], 1).astype(BF)
    for r in range(8):
        grads[r, :, 3 * PAIR :] = dkv[r * rows : (r + 1) * rows]
    last = jnp.concatenate([column_sum(dq.astype(F32)), column_sum(dv.astype(BF).astype(F32))], 1)
    sums[...] = jnp.concatenate([qsum, vsum, last, jnp.zeros((5, PAIR), F32)], 0)

    grad_kv[...] = dkv
    joined = jnp.concatenate([w[...], w16[HEAD_DIM:]], 0)
    for r in range(8):
        grads_rel[r] = grads[r ^ d]
    out = dot(grads_rel[4:].reshape(4 * rows, 4 * PAIR), joined, ((1,), (0,)))
    for k, ref in enumerate(far):
        ref[...] = out[k * rows : (k + 1) * rows].astype(BF)

    width = n_abs.shape[2]
    tokens = n_abs[...].reshape(seq, width)
    pairs = dot(grads[:, :, : 3 * PAIR].reshape(seq, 3 * PAIR), tokens, ((0,), (0,)))
    tall[: 3 * PAIR] = pairs
    tall[3 * PAIR :] = jnp.zeros((WINDOW, width), F32)
    line = lax.broadcasted_iota(jnp.int32, (WINDOW, width), 0)
    for i in range(4):
        _, length, filled = run_of(ids, d, i)
        window = tall[pl.ds(aligned(filled, 16), WINDOW)]
        windows[i] = jnp.where(line < length, window, 0.0).astype(BF)
    pair_sums = jnp.concatenate([qsum, ksum, vsum], 1)
    moments[...] = jnp.concatenate(
        [column_sum(pairs * w[...].astype(F32)), weighted(jnp.broadcast_to(pair_sums, (8, 3 * PAIR)), w[...])[:1]], 0
    )

    out = dot(grads_rel[:4].reshape(4 * rows, 4 * PAIR), joined, ((1,), (0,)))
    near[...] = out.astype(BF)
    near[:rows] = (out[:rows] + dot(dq, w16[:HEAD_DIM], ((1,), (0,)))).astype(BF)


def out_grads(ids, *refs):
    gb, att_abs, att_s, grad_kv, grad_qs, n_abs, n_own, w16, out, moments, gb_abs = refs[:8], *refs[8:]
    d = ids[3]
    rows, width = gb_abs.shape[1], gb_abs.shape[2]
    seq = 8 * rows
    for r in range(8):
        gb_abs[r ^ d] = gb[r][...]
    pair = dot(att_abs[...].reshape(seq, PAIR), gb_abs[...].reshape(seq, width), ((0,), (0,)))
    shared = dot(att_s[...], gb[0][...], ((0,), (0,)))
    q_part = dot(grad_qs[...], n_own[...], ((0,), (0,)))
    kv_part = dot(grad_kv[...], n_abs[...].reshape(seq, width), ((0,), (0,)))
    projections = jnp.concatenate([q_part, kv_part], 0)
    sums = jnp.concatenate([column_sum(grad_qs[...].astype(F32)), column_sum(grad_kv[...].astype(F32))], 1)
    moments[...] = jnp.concatenate(
        [
            column_sum(projections * w16[...].astype(F32)),
            weighted(jnp.broadcast_to(sums, (8, 3 * HEAD_DIM)), w16[...])[:1],
        ],
        0,
    )
    tall = jnp.concatenate([pair, shared, projections], 0).T
    part = out.shape[1]
    for core in range(2):
        for quarter in range(4):
            at = slice((2 * quarter + core) * part, (2 * quarter + core + 1) * part)
            out[core * 4 + quarter] = tall[at].astype(BF)


def add_far(ids, near, f0, f1, f2, f3, s0, s1, s2, s3):
    rows = s0.shape[0]
    for k, (far, ref) in enumerate(((f0, s0), (f1, s1), (f2, s2), (f3, s3))):
        ref[...] = (near[k * rows : (k + 1) * rows].astype(F32) + far[...].astype(F32)).astype(ref.dtype)


def total_of(s0, r1, r2, r3):
    return s0[...] + r1[...].astype(F32) + r2[...].astype(F32) + r3[...].astype(F32)


def middle_back(ids, s0, r1, r2, r3, middle, g_own, wo, vectors, grad_middle, low, sums, back, back_s):
    upstream = total_of(s0, r1, r2, r3)
    centered, inverse = normed(middle[...])
    g = g_own[...].astype(F32)
    grad = g + norm_pull(upstream, centered, inverse, vectors[2:3])
    grad_middle[...] = grad
    rounded = grad.astype(BF)
    low[...] = rounded
    attended = dot(rounded, wo[...], ((1,), (0,))).astype(BF)
    for a in range(8):
        back[a] = attended[:, a * PAIR : (a + 1) * PAIR]
    back_s[...] = attended[:, 8 * PAIR :]
    sums[...] = jnp.concatenate(
        [
            column_sum(rounded.astype(F32)),
            column_sum(upstream * centered),
            column_sum(upstream),
            column_sum(g),
        ],
        0,
    )


def split_features(ids, rows, held, outs, which):
    e = 2 * (ids[1] & 1) + (ids[2] >> 1)
    held[...] = rows.T.reshape(held.shape).astype(BF)
    for m in range(4):
        outs[m][which] = held[m ^ e]


def finish(ids, s0, r1, r2, r3, t0, u1, u2, u3, middle, grad_middle, x_own, vectors, *refs):
    outs, held = refs[:4], refs[4]
    rows = middle[...] + (total_of(t0, u1, u2, u3) + vectors[5:6])
    split_features(ids, rows, held, outs, 0)
    upstream = total_of(s0, r1, r2, r3)
    centered, inverse = normed(x_own[...].astype(F32))
    rows = grad_middle[...] + norm_pull(upstream, centered, inverse, vectors[0:1])
    split_features(ids, rows, held, outs, 1)


def grad_activated(ids, *refs):
    g, both, out, held = refs[:8], *refs[8:]
    rows = held.shape[1]
    down = rows_of(both, 1)
    for r in range(8):
        held[r] = g[r][...]
    for b in range(4):
        block = held[2 * b : 2 * b + 2].reshape(2 * rows, held.shape[2])
        out[b * 2 * rows : (b + 1) * 2 * rows] = dot(block, down, ((1,), (1,)))


def feed_forward(ids, *refs):
    n, refs = refs[:8], refs[8:]
    both, grad_act, bias, n_rel, act, grad_pre, bias_sum = refs[:7]
    up = rows_of(both, 0)
    far, near = refs[7:11], refs[11]
    rows = n_rel.shape[1]
    for r in range(8):
        n_rel[r] = n[r][...]
    total = jnp.zeros(bias_sum.shape, F32)
    for b in (2, 3, 0, 1):
        at = slice(b * 2 * rows, (b + 1) * 2 * rows)
        block = n_rel[2 * b : 2 * b + 2].reshape(2 * rows, n_rel.shape[2])
        pre = dot(block, up, ((1,), (1,))) + bias[...]
        square = pre * pre
        bent = jnp.tanh(ROOT * pre * (1.0 + 0.044715 * square))
        half = 0.5 * (1.0 + bent)
        act[at] = (pre * half).astype(BF)
        slope = half + 0.5 * pre * (1.0 - bent * bent) * (ROOT + ROOT * 3.0 * 0.044715 * square)
        low = (grad_act[at] * slope).astype(BF)
        grad_pre[at] = low
        total = total + column_sum(low.astype(F32))
        out = dot(low, up, ((1,), (0,))).astype(BF)
        if b >= 2:
            far[2 * b - 4][...] = out[:rows]
            far[2 * b - 3][...] = out[rows:]
        else:
            near[2 * rows * b : 2 * rows * (b + 1)] = out
    bias_sum[...] = total


def feed_out(ids, act, both, *refs):
    far, near = refs[:4], refs[4]
    down = rows_of(both, 1)
    half = near.shape[0]
    out = dot(act[half:], down, ((1,), (0,))).astype(BF)
    rows = half // 4
    for k, ref in enumerate(far):
        ref[...] = out[k * rows : (k + 1) * rows]
    near[...] = dot(act[:half], down, ((1,), (0,))).astype(BF)


def mlp_grads(ids, act, grad_pre, n_rel, *refs):
    g, out, held = refs[:8], refs[8], refs[9]
    rows, width = n_rel.shape[1], n_rel.shape[2]
    part = out.shape[2]
    for r in range(8):
        held[r] = g[r][...]
    up = dot(grad_pre[...], n_rel[...].reshape(8 * rows, width), ((0,), (0,)))
    for i in range(4):
        out[i, 0] = up[i * part : (i + 1) * part].astype(BF)
    down = dot(act[...], held[...].reshape(8 * rows, width), ((0,), (0,)))
    for i in range(4):
        out[i, 1] = down[i * part : (i + 1) * part].astype(BF)


def mlp_lanes(ids, summed, o0, o1, o2, o3, held):
    g = ids[1]
    part = held.shape[3]
    for i in range(4):
        held[i] = summed[:, :, i * part : (i + 1) * part]
    for k, ref in enumerate((o0, o1, o2, o3)):
        ref[...] = held[g ^ k]


def mlp_land(ids, *refs):
    blocks, up, down, held = refs[:8], refs[8], refs[9], refs[10]
    d = ids[3]
    for r in range(8):
        held[r ^ d] = blocks[r][...].astype(F32)
    up[...] = held[:, 0].reshape(-1, held.shape[3]).T
    down[...] = held[:, 1].reshape(-1, held.shape[3]).T


def qkv_lanes(ids, window, o0, o1, o2, o3, held):
    g = ids[1]
    part = held.shape[2]
    for i in range(4):
        held[i] = window[:, i * part : (i + 1) * part]
    for k, ref in enumerate((o0, o1, o2, o3)):
        ref[...] = held[g ^ k]


def qkv_land(ids, *refs):
    blocks, mine, theirs, out, tall, held = refs[:8], *refs[8:]
    c, g, z, d = place(ids)
    tall[...] = jnp.zeros(tall.shape, F32)
    for r in range(8):
        start, _, _ = run_of(ids, r ^ d, z)
        at = pl.ds(aligned(start, 16), WINDOW)
        tall[at] = tall[at] + blocks[r][...].astype(F32)
    held[c] = mine[:, 272:].astype(F32)
    held[1 - c] = theirs[:, 272:].astype(F32)
    shared = held[...].reshape(-1, HEAD_DIM).T
    keep = jnp.where(z > 0, 1.0, 0.0)
    at = pl.ds(aligned(jnp.maximum(272 * z - HEAD_DIM, 0), 8), HEAD_DIM)
    tall[at] = tall[at] + shared * keep
    out[...] = tall[: out.shape[1]].T


def out_split(ids, got, o0, o1, o2, o3, wide, held):
    z = ids[2]
    part = wide.shape[1] // 4
    shared = jnp.zeros((got.shape[1], 4 * HEAD_DIM), F32)
    for a in range(8):
        wide[:, a * PAIR : (a + 1) * PAIR] = got[a, :, :PAIR].astype(F32)
        shared = shared + got[a, :, PAIR:].astype(F32)
    wide[:, 8 * PAIR :] = shared[:, :HEAD_DIM]
    for i in range(4):
        at = max(i, 1) * HEAD_DIM
        held[i] = jnp.concatenate(
            [wide[:, i * part : (i + 1) * part], shared[:, at : at + HEAD_DIM]], 1
        ).astype(BF)
    for s, ref in enumerate((o0, o1, o2, o3)):
        ref[...] = held[(z + s) & 3]


def sum_four(ids, b0, b1, b2, b3, out):
    out[...] = sum(ref[...].astype(F32) for ref in (b0, b1, b2, b3)).astype(BF)


def out_land(ids, mine, theirs, out, held):
    c = ids[0]
    held[c] = mine[:, :272].astype(F32)
    held[1 - c] = theirs[:, :272].astype(F32)
    out[...] = held[...].reshape(-1, held.shape[2]).T


def join_sums(ids, first, second, qkv, middle, up, out):
    d = ids[3]
    out[:2] = first[...] + second[...]
    out[2:4] = jnp.zeros((2, out.shape[1]), F32)
    at = pl.ds(aligned(d * PAIR, PAIR), PAIR)
    out[2:3, at] = qkv[0:1]
    out[3:4, at] = qkv[1:2]
    out[2:3, 8 * PAIR :] = qkv[2:3, :HEAD_DIM]
    out[3:4, 8 * PAIR :] = qkv[2:3, HEAD_DIM:]
    out[4:8] = middle[...]
    part = up.shape[1] // 4
    for i in range(4):
        piece = up[:, i * part : (i + 1) * part]
        out[8 + i : 9 + i] = jnp.concatenate([jnp.where(d == a, piece, 0.0) for a in range(8)], 1)


def keep(ids, *refs):
    count = len(refs) // 2
    for source, target in zip(refs[:count], refs[count:], strict=True):
        target[...] = source[...]


def add_two(ids, a, b, out):
    out[...] = a[...] + b[...]


def split_sums(ids, a, b, vectors, out):
    total = a[...] + b[...]
    out[...] = total
    out[0:1] = (total[0:1] - vectors[1:2] * total[1:2]) / vectors[0:1]


def shards(
    hidden_in,
    segment_ids,
    cotangent,
    norm1_gain,
    norm1_shift,
    w_qkv,
    q_bias,
    v_bias,
    w_out,
    out_bias,
    norm2_gain,
    norm2_shift,
    w_up,
    up_bias,
    w_down,
    down_bias,
):
    c = lax.axis_index("c")
    g = lax.axis_index("gx")
    z = lax.axis_index("gy")
    d = c * 4 + g
    width = norm1_gain.shape[0]
    hidden = up_bias.shape[0]
    quarter = hidden_in.shape[2]
    half = quarter // 2
    part = hidden // 32
    own_hidden = hidden // 8
    cols = w_qkv.shape[1]
    seq = segment_ids.shape[1]
    rows = seq // 8
    outer = lax.axis_size("do") > 1
    ids = jnp.concatenate(
        [jnp.stack([c, g, z, d]).astype(jnp.int32), jnp.asarray(run_table(width, cols))]
    )
    vectors = jnp.stack(
        [norm1_gain, norm1_shift, norm2_gain, norm2_shift, out_bias, down_bias, q_bias, v_bias]
    ).astype(F32)

    def row(vector):
        return vector.reshape(1, -1)

    def over_outer(value):
        return lax.psum(value, "do") if outer else value

    block = ((2, quarter, rows), BF)
    own_bf, own_f32 = ((rows, width), BF), ((rows, width), F32)
    held_tokens = ((4, quarter, rows), BF)

    def peers(blocks):
        return [blocks[0]] + [from_peer(blocks[k], k) for k in range(1, 4)]

    def gather_near(own):
        return [own] + [from_peer(own, k) for k in range(1, 4)]

    def gather_later(near, after):
        held = kernel(keep, [(a.shape, a.dtype) for a in near], [], ids, *near, us=0.8, after=after)
        return near + [swap_core(piece) for piece in held]

    def shifted(blocks):
        return [blocks[0]] + [from_below(blocks[s], s) for s in range(1, 4)]

    window = ((WINDOW, quarter), BF)
    window_wide = ((WINDOW, width), BF)
    windows = kernel(qkv_windows, [window] * 4, [((cols + WINDOW, quarter), F32)], ids, w_qkv, us=1.5)
    first = windows[0]
    windows = peers(windows)
    sent = kernel(
        send_tokens, [block] * 4, [], ids, hidden_in.transpose(0, 2, 1), cotangent.transpose(0, 2, 1), us=0.5, after=(first,)
    )
    blocks = [lax.ppermute(sent[m], EVERY, MOVES[m]) for m in range(4)]
    lines = TALL + 3 * 16
    out_piece = kernel(
        out_half, [((lines, quarter), BF)], [((cols, quarter), F32)], ids, w_out, w_qkv, us=0.2, after=(sent[0],)
    )
    piece = ((WINDOW + lines // 4, width), BF)
    joined = kernel(join_lanes, [piece], [((4, WINDOW, quarter), BF)], ids, *windows, out_piece, us=1)
    joined = shifted([joined] * 4)
    *mlp_sent, up_bias_own = kernel(
        mlp_blocks,
        [((2, part, quarter), BF)] * 4 + [((1, own_hidden), F32)],
        [((2, 8, part, quarter), F32)],
        ids,
        w_up,
        w_down.T,
        up_bias.astype(F32).reshape(4, 8, part),
        us=2,
        after=(joined[0],),
    )
    mlp_got = peers(mlp_sent)
    x_own, n1_own = kernel(
        take_normed, [own_bf, own_bf], [held_tokens], ids, *blocks, vectors, us=1.5, after=(joined[1], joined[3], *mlp_got[1:])
    )
    n1 = gather_plane(n1_own)
    g_own = kernel(
        take_tokens, [own_bf], [held_tokens], ids, *blocks, us=1, after=(n1_own,)
    )
    g_near = gather_near(g_own)
    w_own, out_row = kernel(
        qkv_assemble,
        [((3 * PAIR, width), BF), ((TALL + 32, width), BF)],
        [((4, *piece[0]), BF), ((3 * PAIR + WINDOW, width), BF)],
        ids,
        *joined,
        us=1,
        after=(g_own,),
    )
    mlp_part = kernel(
        mlp_join,
        [((2, part, width), BF)],
        [((4, 2, part, quarter), BF)],
        ids,
        *mlp_got,
        us=0.2,
        after=(w_own,),
    )
    mlp_own = lax.all_gather(mlp_part, "gy", axis=0, tiled=False)
    swapped_ids = swap_core(segment_ids)

    half_rows = ((4 * rows, width), BF)
    all_bf = ((8, rows, width), BF)
    heads_bf = ((8, rows, PAIR), BF)
    pair_seq = ((seq, PAIR), BF)
    n_abs, q, k, v, probs, att = kernel(
        attend,
        [all_bf, pair_seq, pair_seq, pair_seq, ((2, seq, seq), BF), heads_bf],
        [],
        ids,
        *n1,
        w_own,
        vectors,
        segment_ids,
        swapped_ids,
        us=3,
        far=True,
        after=(mlp_part,),
    )
    att_got = lax.all_to_all(att, PLANE, split_axis=0, concat_axis=0, tiled=True)
    out_rows = gather_later(gather_near(out_row), (att_got,))
    wo, w16 = kernel(
        out_whole,
        [((width, width), BF), ((3 * HEAD_DIM, width), BF)],
        [((4, 3, 2, 4, 8, quarter), F32)],
        ids,
        *out_rows,
        us=1,
    )
    kv, qs, probs_s, att_s = kernel(
        attend_shared,
        [pair_seq, ((rows, PAIR), BF), ((seq, rows), BF), ((rows, HEAD_DIM), BF)],
        [((1, seq), F32)],
        ids,
        n_abs,
        n1_own,
        w16,
        vectors,
        segment_ids,
        swapped_ids,
        us=0.5,
        work=6,
    )
    middle, n2_own = kernel(
        out_norm, [own_f32, own_bf], [], ids, att_got, att_s, wo, x_own, vectors, us=0.1, work=6
    )
    g_all = gather_later(g_near, (n2_own,))
    summed = [own_f32, own_bf, own_bf, own_bf]

    def scatter(near, far, after=()):
        return peers(
            kernel(add_far, summed, [], ids, near, *[swap_core(f) for f in far], us=1.2, after=after)
        )

    n2 = gather_plane(n2_own)

    grad_act = kernel(
        grad_activated,
        [((seq, own_hidden), F32)],
        [all_bf],
        ids,
        *g_all,
        mlp_own,
        us=12,
        far=True,
        after=(n2_own,),
    )
    n_rel, act, grad_pre, up_sum, *far, near = kernel(
        feed_forward,
        [
            all_bf,
            ((seq, own_hidden), BF),
            ((seq, own_hidden), BF),
            ((1, own_hidden), F32),
            *[own_bf] * 4,
            half_rows,
        ],
        [],
        ids,
        *n2,
        mlp_own,
        grad_act,
        up_bias_own,
        us=1.4,
        work=14,
    )
    parts = scatter(near, far)
    mlp_partial = kernel(
        mlp_grads,
        [((4, 2, part, width), BF)],
        [all_bf],
        ids,
        act,
        grad_pre,
        n_rel,
        *g_all,
        us=20,
        far=True,
        after=(parts[0],),
    )
    *feed_far, feed_near = kernel(
        feed_out, [own_bf] * 4 + [half_rows], [], ids, act, mlp_own, us=2.5, work=8, after=(mlp_partial,)
    )
    mlp_summed = over_outer(lax.psum_scatter(mlp_partial, "gy", scatter_dimension=0, tiled=False))
    grad_middle, gb_own, middle_sums, back, back_s = kernel(
        middle_back,
        [own_f32, own_bf, ((4, width), F32), heads_bf, ((rows, HEAD_DIM), BF)],
        [],
        ids,
        *parts,
        middle,
        g_own,
        wo,
        vectors,
        us=2.5,
        work=6,
        after=(mlp_partial,),
    )
    back = lax.all_to_all(back, PLANE, split_axis=0, concat_axis=0, tiled=True)
    gb = gather_plane(gb_own)

    feed_parts = scatter(feed_near, feed_far, (back,))

    grad_kv, grad_qs, qkv_sums, moments, near, *rest = kernel(
        attend_back,
        [pair_seq, ((rows, HEAD_DIM), BF), ((8, PAIR), F32), ((2, width), F32), half_rows]
        + [own_bf] * 4
        + [((4, WINDOW, width), BF)],
        [
            ((8, rows, 4 * PAIR), BF),
            ((8, rows, 4 * PAIR), BF),
            ((3 * PAIR + WINDOW, width), F32),
        ],
        ids,
        back,
        back_s,
        q,
        k,
        v,
        kv,
        qs,
        probs,
        probs_s,
        w_own,
        w16,
        n_abs,
        us=3,
        far=True,
        after=(feed_parts[0],),
    )
    far = rest[:4]
    window_sum = lax.psum_scatter(rest[4], "gy", scatter_dimension=0, tiled=False)
    parts = scatter(near, far)
    out_sent, moments_s = kernel(
        out_grads,
        [((8, half, PAIR + 4 * HEAD_DIM), BF), ((2, width), F32)],
        [all_bf],
        ids,
        *gb,
        att,
        att_s,
        grad_kv,
        grad_qs,
        n_abs,
        n1_own,
        w16,
        us=3.5,
        work=10,
        after=tuple(parts[1:]),
    )
    out_got = lax.all_to_all(out_sent, PLANE, split_axis=0, concat_axis=0, tiled=True)
    mlp_parts = kernel(
        mlp_lanes,
        [((2, part, quarter), BF)] * 4,
        [((4, 2, part, quarter), BF)],
        ids,
        mlp_summed,
        us=1,
    )
    split_piece = ((half, quarter + HEAD_DIM), BF)
    out_split_parts = shifted(
        kernel(
            out_split,
            [split_piece] * 4,
            [((half, width), F32), ((4, half, quarter + HEAD_DIM), BF)],
            ids,
            out_got,
            us=1,
        )
    )
    done = kernel(
        finish,
        [block] * 4,
        [held_tokens],
        ids,
        *parts,
        *feed_parts,
        middle,
        grad_middle,
        x_own,
        vectors,
        us=2.5,
    )
    landed = [lax.ppermute(done[m], EVERY, BACK[m]) for m in range(4)]
    hidden_out, grad_in = kernel(land_tokens, [((2, quarter, 2 * rows), BF)] * 2, [], ids, *landed, us=1)

    smalls = kernel(
        join_sums, [((12, width), F32)], [], ids, moments, moments_s, qkv_sums, middle_sums, up_sum, us=0.7
    )
    smalls = smalls + swap_core(smalls)
    smalls = smalls + from_peer(smalls, 1)
    others = from_peer(smalls, 2)
    blocks = peers(mlp_parts)
    lanes = kernel(
        qkv_lanes, [window] * 4, [((4, WINDOW, quarter), BF)], ids, window_sum, us=0.2, after=(*landed, *blocks[1:], out_split_parts[0], others)
    )
    near = peers(lanes)
    near = [*near, *[swap_core(piece) for piece in near]]
    total_up, total_down = kernel(
        mlp_land,
        [((quarter, hidden // 4), F32)] * 2,
        [((8, 2, part, quarter), F32)],
        ids,
        *blocks,
        *[swap_core(piece) for piece in blocks],
        us=2,
        after=(lanes[0],),
    )
    mine = kernel(sum_four, [split_piece], [], ids, *out_split_parts, us=0.6, after=(lanes[0],))
    theirs = swap_core(mine)
    total_out = kernel(
        out_land, [((quarter, quarter), F32)], [((2, half, quarter), F32)], ids, mine, theirs, us=0.7
    )
    total_out = over_outer(total_out)

    total_qkv = kernel(
        qkv_land,
        [((quarter, cols), F32)],
        [((cols + WINDOW, quarter), F32), ((2, half, HEAD_DIM), F32)],
        ids,
        *near,
        mine,
        theirs,
        us=2,
    )
    total_qkv = over_outer(total_qkv)
    smalls = kernel(add_two, [((12, width), F32)], [], ids, smalls, others, us=2.8, after=(lanes[0],))
    smalls = smalls + lax.ppermute(smalls, "gy", [(i, i ^ 1) for i in range(4)])
    others = lax.ppermute(smalls, "gy", [(i, i ^ 2) for i in range(4)])
    smalls, others = over_outer(smalls), over_outer(others)
    smalls = kernel(split_sums, [((12, width), F32)], [], ids, smalls, others, vectors, us=0.7)


    return (
        hidden_out.transpose(0, 2, 1),
        grad_in.transpose(0, 2, 1),
        smalls[0],
        smalls[1],
        total_qkv,
        smalls[2],
        smalls[3],
        total_out,
        smalls[4],
        smalls[5],
        smalls[6],
        total_up,
        smalls[8:12].reshape(hidden),
        total_down.T,
        smalls[7],
    )


def solution(mesh):
    devices = mesh.devices
    split = Mesh(
        devices.reshape(devices.shape[0] // 2, 2, devices.shape[1], devices.shape[2]), ("do", "c", "gx", "gy")
    )
    stream = P(None, ("do", "c", "gy"), "gx")
    flat = P()
    tall = P("gx", "gy")
    wide = P("gy", "gx")
    grads = (flat, flat, tall, flat, flat, wide, flat, flat, flat, tall, flat, wide, flat)
    return jax.shard_map(
        shards,
        mesh=split,
        in_specs=(stream, P(None, ("do", "c")), stream, *grads),
        out_specs=(stream, stream, *grads),
        check_vma=False,
    )
```

```python
import math

import jax
import jax.numpy as jnp
import numpy as np
from jax import lax
from jax.experimental import pallas as pl
from jax.experimental.pallas import tpu as pltpu
from jax.sharding import Mesh
from jax.sharding import PartitionSpec as P

HEAD_DIM = 64
PAIR = 2 * HEAD_DIM
EPSILON = 1e-05
BLOCKED = -1e30
BF = jnp.bfloat16
F32 = jnp.float32
PLANE = ("c", "gx")
EVERY = ("c", "gx", "gy")
ROOT = math.sqrt(2.0 / math.pi)
WINDOW = 128
TALL = WINDOW + 16
MIB = 1024 * 1024


def dot(left, right, dims):
    return lax.dot_general(left, right, (dims, ((), ())), preferred_element_type=F32)


def padded(shape, kind):
    size = jnp.dtype(kind).itemsize
    lines = 1 if len(shape) < 2 else -(-shape[-2] // 16) * 16
    return math.prod(shape[:-2]) * lines * (-(-shape[-1] // 128) * 128) * size


def kernel(body, outs, scratch, ids, *arrays, us=0.2, work=2, after=(), far=False):
    count, late = len(arrays), len(after)

    def run(*refs):
        body(*refs[: 1 + count], *refs[1 + count + late :])

    vmem = pl.BlockSpec(memory_space=pltpu.VMEM)
    total = sum(padded(a.shape, a.dtype) for a in arrays) + sum(padded(*o) for o in [*outs, *scratch])
    result = pl.pallas_call(
        run,
        name=body.__name__,
        out_shape=tuple(jax.ShapeDtypeStruct(shape, kind) for shape, kind in outs),
        in_specs=[pl.BlockSpec(memory_space=pltpu.SMEM)] + [vmem] * count + [pl.BlockSpec(memory_space=pl.ANY)] * late,
        out_specs=tuple(vmem for _ in outs),
        scratch_shapes=[pltpu.VMEM(shape, kind) for shape, kind in scratch],
        compiler_params=pltpu.CompilerParams(vmem_limit_bytes=60 * MIB if far else int(total * 1.02) + work * MIB),
        cost_estimate=pl.CostEstimate(flops=int(us * 5e9), bytes_accessed=int(us * 1e5), transcendentals=0),
    )(ids, *arrays, *after)
    return result if len(outs) > 1 else result[0]


def swap_core(value):
    return lax.ppermute(value, "c", [(0, 1), (1, 0)])


def from_peer(value, step):
    return lax.ppermute(value, "gx", [(i, i ^ step) for i in range(4)])


def from_below(value, step):
    return lax.ppermute(value, "gy", [(i, (i + step) % 4) for i in range(4)])


def gather_plane(own):
    near = [own] + [from_peer(own, k) for k in range(1, 4)]
    return near + [swap_core(piece) for piece in near]


def position(c, g, z):
    return (c * 4 + g) * 4 + z


def token_moves():
    moves = []
    for m in range(4):
        move = []
        for c in range(2):
            for g in range(4):
                for z in range(4):
                    t, mb = (m ^ g) >> 1, (m ^ g) & 1
                    move.append((position(c, g, z), position(z // 2, 2 * (z % 2) + t, 2 * mb + c)))
        moves.append(move)
    return moves


MOVES = token_moves()
BACK = [[(b, a) for a, b in move] for move in MOVES]


def run_table(width, cols):
    table = np.zeros((8, 4, 3), np.int32)
    for d in range(8):
        filled = 0
        for z in range(4):
            for t in range(3):
                low = max(width * t + PAIR * d, cols * z)
                high = min(width * t + PAIR * (d + 1), cols * (z + 1))
                if high > low:
                    table[d, z] = (low - cols * z, high - low, filled)
                    filled += high - low
            if table[d, z, 1] == 0:
                table[d, z, 2] = filled
    return table.reshape(-1)


def aligned(value, step):
    return pl.multiple_of(value, step)


def normed(rows):
    average = jnp.mean(rows, axis=1, keepdims=True)
    centered = rows - average
    inverse = lax.rsqrt(jnp.mean(centered * centered, axis=1, keepdims=True) + EPSILON)
    return centered * inverse, inverse


def norm_pull(upstream, centered, inverse, gain):
    scaled = upstream * gain
    return inverse * (
        scaled
        - jnp.mean(scaled, axis=1, keepdims=True)
        - centered * jnp.mean(scaled * centered, axis=1, keepdims=True)
    )


def column_sum(rows):
    return jnp.sum(rows, axis=0, keepdims=True)


def place(ids):
    return ids[0], ids[1], ids[2], ids[3]


def run_of(ids, d, z):
    at = 4 + d * 12 + z * 3
    return ids[at], ids[at + 1], ids[at + 2]


def lanes_of(half, rows):
    return pl.ds(aligned(half * rows, rows), rows)


def send_tokens(ids, x, g_in, *outs):
    g = ids[1]
    for m in range(4):
        v = m ^ g
        for t, src in enumerate((x, g_in)):
            outs[m][t] = src[v & 1, :, lanes_of(v >> 1, outs[m].shape[2])]


def own_rows(ids, blocks, held, which):
    e = 2 * (ids[1] & 1) + (ids[2] >> 1)
    for m in range(4):
        held[m ^ e] = blocks[m][which]
    return held[...].astype(F32).reshape(-1, held.shape[2]).T


def take_tokens(ids, b0, b1, b2, b3, out, held):
    out[...] = own_rows(ids, (b0, b1, b2, b3), held, 1).astype(BF)


def take_normed(ids, b0, b1, b2, b3, vectors, out, low, held):
    rows = own_rows(ids, (b0, b1, b2, b3), held, 0)
    out[...] = rows.astype(BF)
    low[...] = (normed(rows)[0] * vectors[0:1] + vectors[1:2]).astype(BF)


def land_tokens(ids, b0, b1, b2, b3, first, second):
    g = ids[1]
    for m, block in enumerate((b0, b1, b2, b3)):
        v = m ^ g
        for t, out in enumerate((first, second)):
            out[v & 1, :, lanes_of(v >> 1, block.shape[2])] = block[t]


def qkv_windows(ids, w, o0, o1, o2, o3, tall):
    c, g, z, d = place(ids)
    rows = w.shape[1]
    tall[:rows] = w[...].astype(F32).T
    tall[rows:] = jnp.zeros((tall.shape[0] - rows, tall.shape[1]), F32)
    for k, ref in enumerate((o0, o1, o2, o3)):
        start, _, _ = run_of(ids, c * 4 + (g ^ k), z)
        ref[...] = tall[pl.ds(aligned(start, 16), WINDOW)].astype(BF)


def join_lanes(ids, b0, b1, b2, b3, piece, out, held):
    g = ids[1]
    for k, block in enumerate((b0, b1, b2, b3)):
        held[g ^ k] = block[...]
    part = held.shape[2]
    lines = piece.shape[0] // 4
    for i in range(4):
        at = slice(i * part, (i + 1) * part)
        out[:WINDOW, at] = held[i]
        out[WINDOW:, at] = piece[i * lines : (i + 1) * lines]


def qkv_assemble(ids, b0, b1, b2, b3, out, row, held, tall):
    c, g, z, d = place(ids)
    for s, block in enumerate((b0, b1, b2, b3)):
        held[(z + 4 - s) & 3] = block[...]
    for i in range(4):
        _, _, filled = run_of(ids, d, i)
        tall[pl.ds(aligned(filled, 16), WINDOW)] = held[i, :WINDOW]
    out[...] = tall[: out.shape[0]]
    part = out.shape[1] // 4
    lines = held.shape[1] - WINDOW
    shared = []
    for i in range(4):
        for j in range(3):
            piece = held[i, WINDOW:, j * part : (j + 1) * part]
            row[j * lines : (j + 1) * lines, i * part : (i + 1) * part] = piece
        if i:
            piece = held[i, WINDOW:, 3 * part :].astype(F32)
            shared.append(jnp.concatenate([piece[8 * k : 8 * k + 8] for k in range(4)], 1))
    shared.append(jnp.zeros_like(shared[0]))
    row[TALL:] = jnp.concatenate(shared, 0).astype(BF)


def mlp_blocks(ids, up, down, bias, o0, o1, o2, o3, own_bias, held):
    c, g, z, d = place(ids)
    for t, w in enumerate((up, down)):
        held[t] = w[...].astype(F32).T.reshape(held.shape[1:])
    for k, ref in enumerate((o0, o1, o2, o3)):
        to = c * 4 + (g ^ k)
        ref[0] = held[0, to].astype(BF)
        ref[1] = held[1, to].astype(BF)
    own_bias[...] = jnp.concatenate([bias[i, pl.ds(d, 1)] for i in range(4)], 1)


def mlp_join(ids, b0, b1, b2, b3, out, held):
    g = ids[1]
    for k, block in enumerate((b0, b1, b2, b3)):
        held[g ^ k] = block[...]
    part = held.shape[3]
    for i in range(4):
        out[:, :, i * part : (i + 1) * part] = held[i]


def rows_of(both, which):
    return both[:, which].astype(F32).reshape(-1, both.shape[3]).astype(BF)


def out_half(ids, w, wq, out, tall):
    c, _, z, _ = place(ids)
    tall[: w.shape[1]] = w[...].astype(F32).T
    out[:TALL] = tall[pl.ds(aligned(c * WINDOW, 8), TALL)].astype(BF)
    tall[: wq.shape[1]] = wq[...].astype(F32).T
    at = jnp.maximum(272 * z - HEAD_DIM, 0) + c * (HEAD_DIM // 2)
    shared = tall[pl.ds(aligned(at, 8), HEAD_DIM // 2)]
    out[TALL:] = jnp.concatenate([shared, jnp.zeros((16, shared.shape[1]), F32)], 0).astype(BF)


def out_whole(ids, *refs):
    pieces, out, w16, held = refs[:8], refs[8], refs[9], refs[10]
    d = ids[3]
    part = held.shape[5]
    for r in range(8):
        owner = r ^ d
        core, quarter = owner >> 2, owner & 3
        out[pl.ds(aligned(272 * quarter + WINDOW * core, 16), TALL)] = pieces[r][:TALL]
        shared = pieces[r][TALL:].astype(F32)
        for t in range(3):
            for i in range(4):
                held[quarter, t, core, i] = shared[8 * t : 8 * t + 8, i * part : (i + 1) * part]
    for q in range(4):
        w16[:, q * part : (q + 1) * part] = held[q].reshape(3 * HEAD_DIM, part).astype(BF)


def lane_head(shape):
    return lax.broadcasted_iota(jnp.int32, shape, len(shape) - 1) < HEAD_DIM


def only_head(value, head):
    low = lane_head(value.shape)
    zero = jnp.zeros_like(value)
    return jnp.where(low, value, zero) if head == 0 else jnp.where(low, zero, value)


def softmax_down(scores, allowed):
    masked = jnp.where(allowed, scores, BLOCKED)
    weights = jnp.exp(masked - jnp.max(masked, axis=0, keepdims=True))
    return (weights * (1.0 / jnp.sum(weights, axis=0, keepdims=True))).astype(BF)


def causal_mask(shape, first):
    return lax.broadcasted_iota(jnp.int32, shape, 0) <= lax.broadcasted_iota(jnp.int32, shape, 1) + first


def segments_of(ids, mine, theirs):
    c, _, z, _ = place(ids)
    second = (z >> 1) == 1
    near = jnp.where(second, mine[1:2], mine[0:1])
    far = jnp.where(second, theirs[1:2], theirs[0:1])
    return jnp.where((z & 1) == c, near, far).astype(F32)


def upright(seg_row):
    return jnp.broadcast_to(seg_row, (8, seg_row.shape[1])).T[:, :1]


def attend(ids, *refs):
    n, refs = refs[:8], refs[8:]
    w, vectors, mine, theirs, n_abs, q_out, k_out, v_out, probs, att_abs = refs
    d = ids[3]
    rows = n_abs.shape[1]
    seq = 8 * rows
    for r in range(8):
        n_abs[r ^ d] = n[r][...]
    tokens = n_abs[...].reshape(seq, n_abs.shape[2])
    pair = aligned(d * PAIR, PAIR)
    projected = dot(tokens, w[...], ((1,), (1,)))
    q = (projected[:, :PAIR] + vectors[6:7, pl.ds(pair, PAIR)]).astype(BF) * BF(HEAD_DIM**-0.5)
    k = projected[:, PAIR : 2 * PAIR].astype(BF)
    v = (projected[:, 2 * PAIR :] + vectors[7:8, pl.ds(pair, PAIR)]).astype(BF)
    q_out[...] = q
    k_out[...] = k
    v_out[...] = v
    seg_row = segments_of(ids, mine, theirs)
    seg_col = upright(seg_row)
    v_t = v.astype(F32).T.astype(BF)
    keys = [only_head(k, h) for h in range(2)]
    step = 2 * rows
    for b in range(4):
        seen = (b + 1) * step
        at = slice(b * step, seen)
        allowed = (seg_col[:seen] == seg_row[:, at]) & causal_mask((seen, step), b * step)
        turned = []
        for h in range(2):
            p = softmax_down(dot(keys[h][:seen], q[at], ((1,), (1,))), allowed)
            probs[h, :seen, at] = p
            turned.append(dot(v_t[h * HEAD_DIM : (h + 1) * HEAD_DIM, :seen], p, ((1,), (0,))))
        attended = jnp.concatenate(turned, 0).T.astype(BF)
        att_abs[2 * b] = attended[:rows]
        att_abs[2 * b + 1] = attended[rows:]


def attend_shared(ids, n_abs, n_own, w16, vectors, mine, theirs, kv_out, qs_out, probs_s, att_s, seg_row):
    d = ids[3]
    rows, width = n_abs.shape[1], n_abs.shape[2]
    seq = 8 * rows
    w16_rows = w16[...]
    nothing = jnp.zeros((1, HEAD_DIM), F32)
    shared_v = jnp.concatenate([nothing, vectors[7:8, 8 * PAIR :]], 1)
    shared_q = vectors[6:7, 8 * PAIR :]
    kv = (dot(n_abs[...].reshape(seq, width), w16_rows[HEAD_DIM:], ((1,), (1,))) + shared_v).astype(BF)
    qs = (dot(n_own[...], w16_rows[:HEAD_DIM], ((1,), (1,))) + shared_q).astype(BF) * BF(HEAD_DIM**-0.5)
    qs = jnp.concatenate([qs, jnp.zeros_like(qs)], 1)
    kv_out[...] = kv
    qs_out[...] = qs
    first = aligned(d * rows, rows)
    seg_row[...] = segments_of(ids, mine, theirs)
    allowed = (upright(seg_row[...]) == seg_row[:, pl.ds(first, rows)]) & causal_mask((seq, rows), first)
    p = softmax_down(dot(only_head(kv, 0), qs, ((1,), (1,))), allowed)
    probs_s[...] = p
    kv_t = kv.astype(F32).T.astype(BF)
    att_s[...] = dot(kv_t[HEAD_DIM:], p, ((1,), (0,))).T.astype(BF)


def out_norm(ids, got, att_s, wo, x_own, vectors, middle, low):
    attended = jnp.concatenate([got[a] for a in range(8)] + [att_s[...]], 1)
    rows = x_own[...].astype(F32) + (dot(attended, wo[...], ((1,), (1,))) + vectors[4:5])
    middle[...] = rows
    low[...] = (normed(rows)[0] * vectors[2:3] + vectors[3:4]).astype(BF)


def weighted(sums, w):
    high = sums.astype(BF)
    low = (sums - high.astype(F32)).astype(BF)
    return dot(high, w, ((1,), (0,))) + dot(low, w, ((1,), (0,)))


def attend_back(ids, g_in, gs_in, q_in, k_in, v_in, kv_in, qs_in, probs, probs_s, w, w16, n_abs, *refs):
    grad_kv, grad_qs, sums, moments, near = refs[:5]
    far, windows, grads, grads_rel, tall = refs[5:9], *refs[9:]
    d = ids[3]
    rows = g_in.shape[1]
    seq = 8 * rows
    g_all = g_in[...].reshape(seq, PAIR)
    g_s = gs_in[...]
    q, k, v, kv, qs = q_in[...], k_in[...], v_in[...], kv_in[...], qs_in[...]
    scale = HEAD_DIM**-0.5
    k_t = k.astype(F32).T.astype(BF)
    values = [only_head(v, h) for h in range(2)]
    step = 2 * rows
    grad_q = []
    grad_k = [[jnp.zeros((step, PAIR), F32) for _ in range(4)] for _ in range(2)]
    grad_v = [[jnp.zeros((step, PAIR), F32) for _ in range(4)] for _ in range(2)]
    for b in range(4):
        seen = (b + 1) * step
        at = slice(b * step, seen)
        turned = []
        for h in range(2):
            p_low = probs[h, :seen, at]
            p = p_low.astype(F32)
            gp = dot(values[h][:seen], g_all[at], ((1,), (1,)))
            inner = jnp.sum(p * gp, axis=0, keepdims=True)
            gs = (p * (gp - inner)).astype(BF)
            turned.append(dot(k_t[h * HEAD_DIM : (h + 1) * HEAD_DIM, :seen], gs, ((1,), (0,))) * scale)
            dk = dot(gs, q[at], ((1,), (0,)))
            dv = dot(p_low, g_all[at], ((1,), (0,)))
            for i in range(b + 1):
                grad_k[h][i] = grad_k[h][i] + dk[i * step : (i + 1) * step]
                grad_v[h][i] = grad_v[h][i] + dv[i * step : (i + 1) * step]
        grad_q.append(jnp.concatenate(turned, 0).T)
    low = lane_head((step, PAIR))
    qsum = jnp.zeros((1, PAIR), F32)
    ksum = jnp.zeros((1, PAIR), F32)
    vsum = jnp.zeros((1, PAIR), F32)
    for i in range(4):
        dq = grad_q[i].astype(BF)
        dk = jnp.where(low, grad_k[0][i], grad_k[1][i]).astype(BF)
        dv = jnp.where(low, grad_v[0][i], grad_v[1][i]).astype(BF)
        qsum = qsum + column_sum(dq.astype(F32))
        ksum = ksum + column_sum(dk.astype(F32))
        vsum = vsum + column_sum(dv.astype(F32))
        for j in range(2):
            part = slice(j * rows, (j + 1) * rows)
            grads[2 * i + j, :, :PAIR] = dq[part]
            grads[2 * i + j, :, PAIR : 2 * PAIR] = dk[part]
            grads[2 * i + j, :, 2 * PAIR : 3 * PAIR] = dv[part]

    p_low = probs_s[...]
    p = p_low.astype(F32)
    v_s = jnp.concatenate([kv[:, HEAD_DIM:], jnp.zeros((seq, HEAD_DIM), BF)], 1)
    g_pad = jnp.concatenate([g_s, jnp.zeros((rows, HEAD_DIM), BF)], 1)
    gp = dot(v_s, g_pad, ((1,), (1,)))
    inner = jnp.sum(p * gp, axis=0, keepdims=True)
    gs = (p * (gp - inner)).astype(BF)
    kv_t = kv.astype(F32).T.astype(BF)
    dq = (dot(kv_t[:HEAD_DIM], gs, ((1,), (0,))) * scale).T.astype(BF)
    grad_qs[...] = dq
    dk = dot(gs, qs, ((1,), (0,)))[:, :HEAD_DIM]
    dv = dot(p_low, g_pad, ((1,), (0,)))[:, :HEAD_DIM]
    dkv = jnp.concatenate([dk, dv], 1).astype(BF)
    for r in range(8):
        grads[r, :, 3 * PAIR :] = dkv[r * rows : (r + 1) * rows]
    last = jnp.concatenate([column_sum(dq.astype(F32)), column_sum(dv.astype(BF).astype(F32))], 1)
    sums[...] = jnp.concatenate([qsum, vsum, last, jnp.zeros((5, PAIR), F32)], 0)

    grad_kv[...] = dkv
    joined = jnp.concatenate([w[...], w16[HEAD_DIM:]], 0)
    for r in range(8):
        grads_rel[r] = grads[r ^ d]
    out = dot(grads_rel[4:].reshape(4 * rows, 4 * PAIR), joined, ((1,), (0,)))
    for k, ref in enumerate(far):
        ref[...] = out[k * rows : (k + 1) * rows].astype(BF)

    width = n_abs.shape[2]
    tokens = n_abs[...].reshape(seq, width)
    pairs = dot(grads[:, :, : 3 * PAIR].reshape(seq, 3 * PAIR), tokens, ((0,), (0,)))
    tall[: 3 * PAIR] = pairs
    tall[3 * PAIR :] = jnp.zeros((WINDOW, width), F32)
    line = lax.broadcasted_iota(jnp.int32, (WINDOW, width), 0)
    for i in range(4):
        _, length, filled = run_of(ids, d, i)
        window = tall[pl.ds(aligned(filled, 16), WINDOW)]
        windows[i] = jnp.where(line < length, window, 0.0).astype(BF)
    pair_sums = jnp.concatenate([qsum, ksum, vsum], 1)
    moments[...] = jnp.concatenate(
        [column_sum(pairs * w[...].astype(F32)), weighted(jnp.broadcast_to(pair_sums, (8, 3 * PAIR)), w[...])[:1]], 0
    )

    out = dot(grads_rel[:4].reshape(4 * rows, 4 * PAIR), joined, ((1,), (0,)))
    near[...] = out.astype(BF)
    near[:rows] = (out[:rows] + dot(dq, w16[:HEAD_DIM], ((1,), (0,)))).astype(BF)


def out_grads(ids, *refs):
    gb, att_abs, att_s, grad_kv, grad_qs, n_abs, n_own, w16, out, moments, gb_abs = refs[:8], *refs[8:]
    d = ids[3]
    rows, width = gb_abs.shape[1], gb_abs.shape[2]
    seq = 8 * rows
    for r in range(8):
        gb_abs[r ^ d] = gb[r][...]
    pair = dot(att_abs[...].reshape(seq, PAIR), gb_abs[...].reshape(seq, width), ((0,), (0,)))
    shared = dot(att_s[...], gb[0][...], ((0,), (0,)))
    q_part = dot(grad_qs[...], n_own[...], ((0,), (0,)))
    kv_part = dot(grad_kv[...], n_abs[...].reshape(seq, width), ((0,), (0,)))
    projections = jnp.concatenate([q_part, kv_part], 0)
    sums = jnp.concatenate([column_sum(grad_qs[...].astype(F32)), column_sum(grad_kv[...].astype(F32))], 1)
    moments[...] = jnp.concatenate(
        [
            column_sum(projections * w16[...].astype(F32)),
            weighted(jnp.broadcast_to(sums, (8, 3 * HEAD_DIM)), w16[...])[:1],
        ],
        0,
    )
    tall = jnp.concatenate([pair, shared, projections], 0).T
    part = out.shape[1]
    for core in range(2):
        for quarter in range(4):
            at = slice((2 * quarter + core) * part, (2 * quarter + core + 1) * part)
            out[core * 4 + quarter] = tall[at].astype(BF)


def add_far(ids, near, f0, f1, f2, f3, s0, s1, s2, s3):
    rows = s0.shape[0]
    for k, (far, ref) in enumerate(((f0, s0), (f1, s1), (f2, s2), (f3, s3))):
        ref[...] = (near[k * rows : (k + 1) * rows].astype(F32) + far[...].astype(F32)).astype(ref.dtype)


def total_of(s0, r1, r2, r3):
    return s0[...] + r1[...].astype(F32) + r2[...].astype(F32) + r3[...].astype(F32)


def middle_back(ids, s0, r1, r2, r3, middle, g_own, wo, vectors, grad_middle, low, sums, back, back_s):
    upstream = total_of(s0, r1, r2, r3)
    centered, inverse = normed(middle[...])
    g = g_own[...].astype(F32)
    grad = g + norm_pull(upstream, centered, inverse, vectors[2:3])
    grad_middle[...] = grad
    rounded = grad.astype(BF)
    low[...] = rounded
    attended = dot(rounded, wo[...], ((1,), (0,))).astype(BF)
    for a in range(8):
        back[a] = attended[:, a * PAIR : (a + 1) * PAIR]
    back_s[...] = attended[:, 8 * PAIR :]
    sums[...] = jnp.concatenate(
        [
            column_sum(rounded.astype(F32)),
            column_sum(upstream * centered),
            column_sum(upstream),
            column_sum(g),
        ],
        0,
    )


def split_features(ids, rows, held, outs, which):
    e = 2 * (ids[1] & 1) + (ids[2] >> 1)
    held[...] = rows.T.reshape(held.shape).astype(BF)
    for m in range(4):
        outs[m][which] = held[m ^ e]


def finish(ids, s0, r1, r2, r3, t0, u1, u2, u3, middle, grad_middle, x_own, vectors, *refs):
    outs, held = refs[:4], refs[4]
    rows = middle[...] + (total_of(t0, u1, u2, u3) + vectors[5:6])
    split_features(ids, rows, held, outs, 0)
    upstream = total_of(s0, r1, r2, r3)
    centered, inverse = normed(x_own[...].astype(F32))
    rows = grad_middle[...] + norm_pull(upstream, centered, inverse, vectors[0:1])
    split_features(ids, rows, held, outs, 1)


def grad_activated(ids, *refs):
    g, both, out, held = refs[:8], *refs[8:]
    rows = held.shape[1]
    down = rows_of(both, 1)
    for r in range(8):
        held[r] = g[r][...]
    for b in range(4):
        block = held[2 * b : 2 * b + 2].reshape(2 * rows, held.shape[2])
        out[b * 2 * rows : (b + 1) * 2 * rows] = dot(block, down, ((1,), (1,)))


def feed_forward(ids, *refs):
    n, refs = refs[:8], refs[8:]
    both, grad_act, bias, n_rel, act, grad_pre, bias_sum = refs[:7]
    up = rows_of(both, 0)
    far, near = refs[7:11], refs[11]
    rows = n_rel.shape[1]
    for r in range(8):
        n_rel[r] = n[r][...]
    total = jnp.zeros(bias_sum.shape, F32)
    for b in (2, 3, 0, 1):
        at = slice(b * 2 * rows, (b + 1) * 2 * rows)
        block = n_rel[2 * b : 2 * b + 2].reshape(2 * rows, n_rel.shape[2])
        pre = dot(block, up, ((1,), (1,))) + bias[...]
        square = pre * pre
        bent = jnp.tanh(ROOT * pre * (1.0 + 0.044715 * square))
        half = 0.5 * (1.0 + bent)
        act[at] = (pre * half).astype(BF)
        slope = half + 0.5 * pre * (1.0 - bent * bent) * (ROOT + ROOT * 3.0 * 0.044715 * square)
        low = (grad_act[at] * slope).astype(BF)
        grad_pre[at] = low
        total = total + column_sum(low.astype(F32))
        out = dot(low, up, ((1,), (0,))).astype(BF)
        if b >= 2:
            far[2 * b - 4][...] = out[:rows]
            far[2 * b - 3][...] = out[rows:]
        else:
            near[2 * rows * b : 2 * rows * (b + 1)] = out
    bias_sum[...] = total


def feed_out(ids, act, both, *refs):
    far, near = refs[:4], refs[4]
    down = rows_of(both, 1)
    half = near.shape[0]
    out = dot(act[half:], down, ((1,), (0,))).astype(BF)
    rows = half // 4
    for k, ref in enumerate(far):
        ref[...] = out[k * rows : (k + 1) * rows]
    near[...] = dot(act[:half], down, ((1,), (0,))).astype(BF)


def mlp_grads(ids, act, grad_pre, n_rel, *refs):
    g, out, held = refs[:8], refs[8], refs[9]
    rows, width = n_rel.shape[1], n_rel.shape[2]
    part = out.shape[2]
    for r in range(8):
        held[r] = g[r][...]
    up = dot(grad_pre[...], n_rel[...].reshape(8 * rows, width), ((0,), (0,)))
    for i in range(4):
        out[i, 0] = up[i * part : (i + 1) * part].astype(BF)
    down = dot(act[...], held[...].reshape(8 * rows, width), ((0,), (0,)))
    for i in range(4):
        out[i, 1] = down[i * part : (i + 1) * part].astype(BF)


def mlp_lanes(ids, summed, o0, o1, o2, o3, held):
    g = ids[1]
    part = held.shape[3]
    for i in range(4):
        held[i] = summed[:, :, i * part : (i + 1) * part]
    for k, ref in enumerate((o0, o1, o2, o3)):
        ref[...] = held[g ^ k]


def mlp_land(ids, *refs):
    blocks, up, down, held = refs[:8], refs[8], refs[9], refs[10]
    d = ids[3]
    for r in range(8):
        held[r ^ d] = blocks[r][...].astype(F32)
    up[...] = held[:, 0].reshape(-1, held.shape[3]).T
    down[...] = held[:, 1].reshape(-1, held.shape[3]).T


def qkv_lanes(ids, window, o0, o1, o2, o3, held):
    g = ids[1]
    part = held.shape[2]
    for i in range(4):
        held[i] = window[:, i * part : (i + 1) * part]
    for k, ref in enumerate((o0, o1, o2, o3)):
        ref[...] = held[g ^ k]


def qkv_land(ids, *refs):
    blocks, mine, theirs, out, tall, held = refs[:8], *refs[8:]
    c, g, z, d = place(ids)
    tall[...] = jnp.zeros(tall.shape, F32)
    for r in range(8):
        start, _, _ = run_of(ids, r ^ d, z)
        at = pl.ds(aligned(start, 16), WINDOW)
        tall[at] = tall[at] + blocks[r][...].astype(F32)
    held[c] = mine[:, 272:].astype(F32)
    held[1 - c] = theirs[:, 272:].astype(F32)
    shared = held[...].reshape(-1, HEAD_DIM).T
    keep = jnp.where(z > 0, 1.0, 0.0)
    at = pl.ds(aligned(jnp.maximum(272 * z - HEAD_DIM, 0), 8), HEAD_DIM)
    tall[at] = tall[at] + shared * keep
    out[...] = tall[: out.shape[1]].T


def out_split(ids, got, o0, o1, o2, o3, wide, held):
    z = ids[2]
    part = wide.shape[1] // 4
    shared = jnp.zeros((got.shape[1], 4 * HEAD_DIM), F32)
    for a in range(8):
        wide[:, a * PAIR : (a + 1) * PAIR] = got[a, :, :PAIR].astype(F32)
        shared = shared + got[a, :, PAIR:].astype(F32)
    wide[:, 8 * PAIR :] = shared[:, :HEAD_DIM]
    for i in range(4):
        at = max(i, 1) * HEAD_DIM
        held[i] = jnp.concatenate(
            [wide[:, i * part : (i + 1) * part], shared[:, at : at + HEAD_DIM]], 1
        ).astype(BF)
    for s, ref in enumerate((o0, o1, o2, o3)):
        ref[...] = held[(z + s) & 3]


def sum_four(ids, b0, b1, b2, b3, out):
    out[...] = sum(ref[...].astype(F32) for ref in (b0, b1, b2, b3)).astype(BF)


def out_land(ids, mine, theirs, out, held):
    c = ids[0]
    held[c] = mine[:, :272].astype(F32)
    held[1 - c] = theirs[:, :272].astype(F32)
    out[...] = held[...].reshape(-1, held.shape[2]).T


def join_sums(ids, first, second, qkv, middle, up, out):
    d = ids[3]
    out[:2] = first[...] + second[...]
    out[2:4] = jnp.zeros((2, out.shape[1]), F32)
    at = pl.ds(aligned(d * PAIR, PAIR), PAIR)
    out[2:3, at] = qkv[0:1]
    out[3:4, at] = qkv[1:2]
    out[2:3, 8 * PAIR :] = qkv[2:3, :HEAD_DIM]
    out[3:4, 8 * PAIR :] = qkv[2:3, HEAD_DIM:]
    out[4:8] = middle[...]
    part = up.shape[1] // 4
    for i in range(4):
        piece = up[:, i * part : (i + 1) * part]
        out[8 + i : 9 + i] = jnp.concatenate([jnp.where(d == a, piece, 0.0) for a in range(8)], 1)


def keep(ids, *refs):
    count = len(refs) // 2
    for source, target in zip(refs[:count], refs[count:], strict=True):
        target[...] = source[...]


def add_two(ids, a, b, out):
    out[...] = a[...] + b[...]


def split_sums(ids, a, b, vectors, out):
    total = a[...] + b[...]
    out[...] = total
    out[0:1] = (total[0:1] - vectors[1:2] * total[1:2]) / vectors[0:1]


def shards(
    hidden_in,
    segment_ids,
    cotangent,
    norm1_gain,
    norm1_shift,
    w_qkv,
    q_bias,
    v_bias,
    w_out,
    out_bias,
    norm2_gain,
    norm2_shift,
    w_up,
    up_bias,
    w_down,
    down_bias,
):
    c = lax.axis_index("c")
    g = lax.axis_index("gx")
    z = lax.axis_index("gy")
    d = c * 4 + g
    width = norm1_gain.shape[0]
    hidden = up_bias.shape[0]
    quarter = hidden_in.shape[2]
    half = quarter // 2
    part = hidden // 32
    own_hidden = hidden // 8
    cols = w_qkv.shape[1]
    seq = segment_ids.shape[1]
    rows = seq // 8
    outer = lax.axis_size("do") > 1
    ids = jnp.concatenate(
        [jnp.stack([c, g, z, d]).astype(jnp.int32), jnp.asarray(run_table(width, cols))]
    )
    vectors = jnp.stack(
        [norm1_gain, norm1_shift, norm2_gain, norm2_shift, out_bias, down_bias, q_bias, v_bias]
    ).astype(F32)

    def row(vector):
        return vector.reshape(1, -1)

    def over_outer(value):
        return lax.psum(value, "do") if outer else value

    block = ((2, quarter, rows), BF)
    own_bf, own_f32 = ((rows, width), BF), ((rows, width), F32)
    held_tokens = ((4, quarter, rows), BF)

    def peers(blocks):
        return [blocks[0]] + [from_peer(blocks[k], k) for k in range(1, 4)]

    def gather_near(own):
        return [own] + [from_peer(own, k) for k in range(1, 4)]

    def gather_later(near, after):
        held = kernel(keep, [(a.shape, a.dtype) for a in near], [], ids, *near, us=0.8, after=after)
        return near + [swap_core(piece) for piece in held]

    def shifted(blocks):
        return [blocks[0]] + [from_below(blocks[s], s) for s in range(1, 4)]

    window = ((WINDOW, quarter), BF)
    window_wide = ((WINDOW, width), BF)
    windows = kernel(qkv_windows, [window] * 4, [((cols + WINDOW, quarter), F32)], ids, w_qkv, us=1.5)
    first = windows[0]
    windows = peers(windows)
    sent = kernel(
        send_tokens, [block] * 4, [], ids, hidden_in.transpose(0, 2, 1), cotangent.transpose(0, 2, 1), us=0.5, after=(first,)
    )
    blocks = [lax.ppermute(sent[m], EVERY, MOVES[m]) for m in range(4)]
    lines = TALL + 3 * 16
    out_piece = kernel(
        out_half, [((lines, quarter), BF)], [((cols, quarter), F32)], ids, w_out, w_qkv, us=0.2, after=(sent[0],)
    )
    piece = ((WINDOW + lines // 4, width), BF)
    joined = kernel(join_lanes, [piece], [((4, WINDOW, quarter), BF)], ids, *windows, out_piece, us=1)
    joined = shifted([joined] * 4)
    *mlp_sent, up_bias_own = kernel(
        mlp_blocks,
        [((2, part, quarter), BF)] * 4 + [((1, own_hidden), F32)],
        [((2, 8, part, quarter), F32)],
        ids,
        w_up,
        w_down.T,
        up_bias.astype(F32).reshape(4, 8, part),
        us=2,
        after=(joined[0],),
    )
    mlp_got = peers(mlp_sent)
    x_own, n1_own = kernel(
        take_normed, [own_bf, own_bf], [held_tokens], ids, *blocks, vectors, us=1.5, after=(joined[1], joined[3], *mlp_got[1:])
    )
    n1 = gather_plane(n1_own)
    g_own = kernel(
        take_tokens, [own_bf], [held_tokens], ids, *blocks, us=1, after=(n1_own,)
    )
    g_near = gather_near(g_own)
    w_own, out_row = kernel(
        qkv_assemble,
        [((3 * PAIR, width), BF), ((TALL + 32, width), BF)],
        [((4, *piece[0]), BF), ((3 * PAIR + WINDOW, width), BF)],
        ids,
        *joined,
        us=1,
        after=(g_own,),
    )
    mlp_part = kernel(
        mlp_join,
        [((2, part, width), BF)],
        [((4, 2, part, quarter), BF)],
        ids,
        *mlp_got,
        us=0.2,
        after=(w_own,),
    )
    mlp_own = lax.all_gather(mlp_part, "gy", axis=0, tiled=False)
    swapped_ids = swap_core(segment_ids)

    half_rows = ((4 * rows, width), BF)
    all_bf = ((8, rows, width), BF)
    heads_bf = ((8, rows, PAIR), BF)
    pair_seq = ((seq, PAIR), BF)
    n_abs, q, k, v, probs, att = kernel(
        attend,
        [all_bf, pair_seq, pair_seq, pair_seq, ((2, seq, seq), BF), heads_bf],
        [],
        ids,
        *n1,
        w_own,
        vectors,
        segment_ids,
        swapped_ids,
        us=3,
        far=True,
        after=(mlp_part,),
    )
    att_got = lax.all_to_all(att, PLANE, split_axis=0, concat_axis=0, tiled=True)
    out_rows = gather_later(gather_near(out_row), (att_got,))
    wo, w16 = kernel(
        out_whole,
        [((width, width), BF), ((3 * HEAD_DIM, width), BF)],
        [((4, 3, 2, 4, 8, quarter), F32)],
        ids,
        *out_rows,
        us=1,
    )
    kv, qs, probs_s, att_s = kernel(
        attend_shared,
        [pair_seq, ((rows, PAIR), BF), ((seq, rows), BF), ((rows, HEAD_DIM), BF)],
        [((1, seq), F32)],
        ids,
        n_abs,
        n1_own,
        w16,
        vectors,
        segment_ids,
        swapped_ids,
        us=0.5,
        work=6,
    )
    middle, n2_own = kernel(
        out_norm, [own_f32, own_bf], [], ids, att_got, att_s, wo, x_own, vectors, us=0.1, work=6
    )
    g_all = gather_later(g_near, (n2_own,))
    summed = [own_f32, own_bf, own_bf, own_bf]

    def scatter(near, far, after=()):
        return peers(
            kernel(add_far, summed, [], ids, near, *[swap_core(f) for f in far], us=1.2, after=after)
        )

    n2 = gather_plane(n2_own)

    grad_act = kernel(
        grad_activated,
        [((seq, own_hidden), F32)],
        [all_bf],
        ids,
        *g_all,
        mlp_own,
        us=12,
        far=True,
        after=(n2_own,),
    )
    n_rel, act, grad_pre, up_sum, *far, near = kernel(
        feed_forward,
        [
            all_bf,
            ((seq, own_hidden), BF),
            ((seq, own_hidden), BF),
            ((1, own_hidden), F32),
            *[own_bf] * 4,
            half_rows,
        ],
        [],
        ids,
        *n2,
        mlp_own,
        grad_act,
        up_bias_own,
        us=1.4,
        work=14,
    )
    parts = scatter(near, far)
    mlp_partial = kernel(
        mlp_grads,
        [((4, 2, part, width), BF)],
        [all_bf],
        ids,
        act,
        grad_pre,
        n_rel,
        *g_all,
        us=20,
        far=True,
        after=(parts[0],),
    )
    *feed_far, feed_near = kernel(
        feed_out, [own_bf] * 4 + [half_rows], [], ids, act, mlp_own, us=2.5, work=8, after=(mlp_partial,)
    )
    mlp_summed = over_outer(lax.psum_scatter(mlp_partial, "gy", scatter_dimension=0, tiled=False))
    grad_middle, gb_own, middle_sums, back, back_s = kernel(
        middle_back,
        [own_f32, own_bf, ((4, width), F32), heads_bf, ((rows, HEAD_DIM), BF)],
        [],
        ids,
        *parts,
        middle,
        g_own,
        wo,
        vectors,
        us=2.5,
        work=6,
        after=(mlp_partial,),
    )
    back = lax.all_to_all(back, PLANE, split_axis=0, concat_axis=0, tiled=True)
    gb = gather_plane(gb_own)

    feed_parts = scatter(feed_near, feed_far, (back,))

    grad_kv, grad_qs, qkv_sums, moments, near, *rest = kernel(
        attend_back,
        [pair_seq, ((rows, HEAD_DIM), BF), ((8, PAIR), F32), ((2, width), F32), half_rows]
        + [own_bf] * 4
        + [((4, WINDOW, width), BF)],
        [
            ((8, rows, 4 * PAIR), BF),
            ((8, rows, 4 * PAIR), BF),
            ((3 * PAIR + WINDOW, width), F32),
        ],
        ids,
        back,
        back_s,
        q,
        k,
        v,
        kv,
        qs,
        probs,
        probs_s,
        w_own,
        w16,
        n_abs,
        us=3,
        far=True,
        after=(feed_parts[0],),
    )
    far = rest[:4]
    window_sum = lax.psum_scatter(rest[4], "gy", scatter_dimension=0, tiled=False)
    parts = scatter(near, far)
    out_sent, moments_s = kernel(
        out_grads,
        [((8, half, PAIR + 4 * HEAD_DIM), BF), ((2, width), F32)],
        [all_bf],
        ids,
        *gb,
        att,
        att_s,
        grad_kv,
        grad_qs,
        n_abs,
        n1_own,
        w16,
        us=3.5,
        far=True,
        work=10,
        after=tuple(parts[1:]),
    )
    out_got = lax.all_to_all(out_sent, PLANE, split_axis=0, concat_axis=0, tiled=True)
    mlp_parts = kernel(
        mlp_lanes,
        [((2, part, quarter), BF)] * 4,
        [((4, 2, part, quarter), BF)],
        ids,
        mlp_summed,
        us=1,
    )
    split_piece = ((half, quarter + HEAD_DIM), BF)
    out_split_parts = shifted(
        kernel(
            out_split,
            [split_piece] * 4,
            [((half, width), F32), ((4, half, quarter + HEAD_DIM), BF)],
            ids,
            out_got,
            us=1,
        )
    )
    done = kernel(
        finish,
        [block] * 4,
        [held_tokens],
        ids,
        *parts,
        *feed_parts,
        middle,
        grad_middle,
        x_own,
        vectors,
        us=2.5,
        far=True,
    )
    landed = [lax.ppermute(done[m], EVERY, BACK[m]) for m in range(4)]
    hidden_out, grad_in = kernel(land_tokens, [((2, quarter, 2 * rows), BF)] * 2, [], ids, *landed, us=1)

    smalls = kernel(
        join_sums, [((12, width), F32)], [], ids, moments, moments_s, qkv_sums, middle_sums, up_sum, us=0.7
    )
    smalls = smalls + swap_core(smalls)
    smalls = smalls + from_peer(smalls, 1)
    others = from_peer(smalls, 2)
    blocks = peers(mlp_parts)
    lanes = kernel(
        qkv_lanes, [window] * 4, [((4, WINDOW, quarter), BF)], ids, window_sum, us=0.2, after=(*landed, *blocks[1:], out_split_parts[0], others)
    )
    near = peers(lanes)
    near = [*near, *[swap_core(piece) for piece in near]]
    total_up, total_down = kernel(
        mlp_land,
        [((quarter, hidden // 4), F32)] * 2,
        [((8, 2, part, quarter), F32)],
        ids,
        *blocks,
        *[swap_core(piece) for piece in blocks],
        us=2,
        after=(lanes[0],),
    )
    mine = kernel(sum_four, [split_piece], [], ids, *out_split_parts, us=0.6, after=(lanes[0],))
    theirs = swap_core(mine)
    total_out = kernel(
        out_land, [((quarter, quarter), F32)], [((2, half, quarter), F32)], ids, mine, theirs, us=0.7
    )
    total_out = over_outer(total_out)

    total_qkv = kernel(
        qkv_land,
        [((quarter, cols), F32)],
        [((cols + WINDOW, quarter), F32), ((2, half, HEAD_DIM), F32)],
        ids,
        *near,
        mine,
        theirs,
        us=2,
    )
    total_qkv = over_outer(total_qkv)
    smalls = kernel(add_two, [((12, width), F32)], [], ids, smalls, others, us=2.8, after=(lanes[0],))
    smalls = smalls + lax.ppermute(smalls, "gy", [(i, i ^ 1) for i in range(4)])
    others = lax.ppermute(smalls, "gy", [(i, i ^ 2) for i in range(4)])
    smalls, others = over_outer(smalls), over_outer(others)
    smalls = kernel(split_sums, [((12, width), F32)], [], ids, smalls, others, vectors, us=0.7)


    return (
        hidden_out.transpose(0, 2, 1),
        grad_in.transpose(0, 2, 1),
        smalls[0],
        smalls[1],
        total_qkv,
        smalls[2],
        smalls[3],
        total_out,
        smalls[4],
        smalls[5],
        smalls[6],
        total_up,
        smalls[8:12].reshape(hidden),
        total_down.T,
        smalls[7],
    )


def solution(mesh):
    devices = mesh.devices
    split = Mesh(
        devices.reshape(devices.shape[0] // 2, 2, devices.shape[1], devices.shape[2]), ("do", "c", "gx", "gy")
    )
    stream = P(None, ("do", "c", "gy"), "gx")
    flat = P()
    tall = P("gx", "gy")
    wide = P("gy", "gx")
    grads = (flat, flat, tall, flat, flat, wide, flat, flat, flat, tall, flat, wide, flat)
    return jax.shard_map(
        shards,
        mesh=split,
        in_specs=(stream, P(None, ("do", "c")), stream, *grads),
        out_specs=(stream, stream, *grads),
        check_vma=False,
    )
```
